512 devices in a mesh: shot: 8 (over x, core), gx: 8 (over z_lo), gy: 8 (over y, z_hi).
Axes of the slice: x: 4, y: 4, z: 16 (z_hi: 2, z_lo: 8; z = z_hi * 8 + z_lo), core: 2. Of those that a mesh axis runs over, the one named last changes fastest.
Arguments:
- features: bfloat16 [32, 256, 128, 128], P('shot', 'gx', 'gy'), may hold values from -6 to 6
- conv_weight: float32 [32, 27], P('shot'), may hold values from -0.21875 to 0.21875
- fwd_prev: float32 [8, 256, 128, 128], P('shot', 'gx', 'gy'), may hold values from -6 to 6
- fwd_now: float32 [8, 256, 128, 128], P('shot', 'gx', 'gy'), may hold values from -6 to 6
- back_prev: float32 [8, 256, 128, 128], P('shot', 'gx', 'gy'), may hold values from -96 to 96
- back_now: float32 [8, 256, 128, 128], P('shot', 'gx', 'gy'), may hold values from -96 to 96
- sources: int32 [8], P('shot'), may hold values from 0 to 4194303
- wavelet: float32 [8, 2], P('shot'), may hold values from -24 to 24
- receivers: int32 [8, 512], P('shot'), may hold values from 0 to 32767
- residual: float32 [8, 2, 512], P('shot'), may hold values from -96 to 96
- damping: float32 [1], replicated, may hold values from 100 to 1000
Outputs:
- fwd_last: float32 [8, 256, 128, 128], P('shot', 'gx', 'gy')
- back_last: float32 [8, 256, 128, 128], P('shot', 'gx', 'gy')
- traces: float32 [8, 2, 512], P('shot')
- update: float32 [256, 128, 128], P('gx', 'gy')
- weight_grad: float32 [32, 27], P('shot')
The draws below stay inside these ranges and needn't reach their ends.
All inputs are finite; a program needn't handle non-finite values.
Results may differ from the reference program's by a relative error of at most 0.0003.
Values may be sent and summed in bfloat16 or wider, within the bound.
No kernel may reach another device: no remote copies, remote signals or barrier semaphores. Data moves between devices by JAX's collectives and lax.ppermute only.
A program may use at most 64 MiB of HBM per device.

```python
import math
import jax
import jax.numpy as jnp
from jax import lax

CH = 32
NZ = 128
REC = 512
RDEPTH = 3
SHOTS = 8
NX = 256
NY = 128


def plant(array, own_key, least, top_value):
    extent = array.shape
    spot = [jax.random.randint(jax.random.fold_in(own_key, axis), (), 0, extent[axis]) for axis in range(len(extent))]
    array = array.at[tuple(spot)].set(least)
    longest = extent.index(max(extent))
    spot[longest] = (spot[longest] + 1) % extent[longest]
    return array.at[tuple(spot)].set(top_value)


def levels(rng, dims, cuts, smallest, largest):
    level = 1.0
    for dim, shards_of in cuts:
        steps = jax.random.uniform(jax.random.fold_in(jax.random.fold_in(rng, 6), dim), (shards_of,), jnp.float32, smallest / len(cuts), largest / len(cuts))
        level = level * jnp.repeat(jnp.exp(steps), dims[dim] // shards_of).reshape((-1,) + (1,) * (len(dims) - 1 - dim))
    return level


def centred(rng, dims, scale, most, cuts=(), held_as=jnp.bfloat16):
    gain = levels(rng, dims, cuts, -0.22, 0.18) if cuts else 1.0
    values = jax.random.normal(rng, dims, jnp.float32) * scale * gain
    return jnp.minimum(jnp.maximum(values, -most), most).astype(held_as)


def setup_inputs(seed: int = 0) -> dict:
    key_of = jax.random.split(jax.random.key(seed), 12)
    return {
        "features": centred(key_of[0], (CH, NX, NY, NZ), 1.0, 6.0, ((0, 8), (1, 8), (2, 8))),
        "conv_weight": centred(key_of[1], (CH, 27), (27 * CH) ** -0.5, 0.21875, ((0, 8),), jnp.float32),
        "fwd_prev": centred(key_of[2], (SHOTS, NX, NY, NZ), 1.0, 6.0, ((0, 8), (1, 8), (2, 8)), jnp.float32),
        "fwd_now": centred(key_of[3], (SHOTS, NX, NY, NZ), 1.0, 6.0, ((0, 8), (1, 8), (2, 8)), jnp.float32),
        "back_prev": centred(key_of[4], (SHOTS, NX, NY, NZ), 16.0, 96.0, ((0, 8), (1, 8), (2, 8)), jnp.float32),
        "back_now": centred(key_of[5], (SHOTS, NX, NY, NZ), 16.0, 96.0, ((0, 8), (1, 8), (2, 8)), jnp.float32),
        "sources": plant(jax.random.randint(key_of[6], (SHOTS,), 0, NX * NY * NZ), jax.random.fold_in(key_of[6], 1), 0, (NX * NY * NZ) - 1).astype(jnp.int32),
        "wavelet": centred(key_of[7], (SHOTS, 2), 4.0, 24.0, ((0, 8),), jnp.float32),
        "receivers": plant(jax.random.randint(key_of[8], (SHOTS, REC), 0, NX * NY), jax.random.fold_in(key_of[8], 1), 0, (NX * NY) - 1).astype(jnp.int32),
        "residual": centred(key_of[9], (SHOTS, 2, REC), 16.0, 96.0, ((0, 8),), jnp.float32),
        "damping": jnp.clip(jnp.exp(jax.random.uniform(key_of[10], (1,), jnp.float32, math.log(100.0), math.log(1000.0))), 100.0, 1000.0),
    }


COEFFICIENTS = (-205.0 / 72.0, 8.0 / 5.0, -1.0 / 5.0, 8.0 / 315.0, -1.0 / 560.0)


def laplace(field):
    size_x, size_y, depth = field.shape
    padded = jnp.pad(field, 4)
    total = 3.0 * COEFFICIENTS[0] * field
    for reach in range(1, 5):
        along_x = padded[4 + reach:4 + reach + size_x, 4:4 + size_y, 4:4 + depth] + padded[4 - reach:4 - reach + size_x, 4:4 + size_y, 4:4 + depth]
        along_y = padded[4:4 + size_x, 4 + reach:4 + reach + size_y, 4:4 + depth] + padded[4:4 + size_x, 4 - reach:4 - reach + size_y, 4:4 + depth]
        along_z = padded[4:4 + size_x, 4:4 + size_y, 4 + reach:4 + reach + depth] + padded[4:4 + size_x, 4:4 + size_y, 4 - reach:4 - reach + depth]
        total = total + COEFFICIENTS[reach] * (along_x + along_y + along_z)
    return total


def prior(features, conv_weight):
    size_x, size_y, depth = features.shape[1:]

    def one_channel(total, item):
        channel, tap_weights = item
        padded = jnp.pad(channel.astype(jnp.float32), 1)
        for offset_x in range(3):
            for offset_y in range(3):
                for offset_z in range(3):
                    window = padded[offset_x:offset_x + size_x, offset_y:offset_y + size_y, offset_z:offset_z + depth]
                    total = total + tap_weights[9 * offset_x + 3 * offset_y + offset_z] * window
        return total, None

    start = jnp.zeros((size_x, size_y, depth), jnp.float32)
    total, _ = lax.scan(one_channel, start, (features, conv_weight))
    return total


def pull_back(features, pulled):
    size_x, size_y, depth = features.shape[1:]

    def one_channel(carry, channel):
        padded = jnp.pad(channel.astype(jnp.float32), 1)
        columns = []
        for offset_x in range(3):
            for offset_y in range(3):
                for offset_z in range(3):
                    window = padded[offset_x:offset_x + size_x, offset_y:offset_y + size_y, offset_z:offset_z + depth]
                    columns.append(jnp.sum(pulled * window))
        return carry, jnp.stack(columns)

    _, grads = lax.scan(one_channel, jnp.zeros((), jnp.float32), features)
    return grads


def reference(features, conv_weight, fwd_prev, fwd_now, back_prev, back_now, sources, wavelet, receivers, residual, damping):
    raw_field = prior(features, conv_weight)
    squashed = jax.nn.sigmoid(raw_field)
    courant = 0.02 + 0.16 * squashed
    derivative = 0.16 * squashed * (1.0 - squashed)

    def one_shot(carry, item):
        image_total, light_total = carry
        older_fwd, current_fwd, older_back, current_back, spot, amplitude, placed, injected = item
        spot_x = spot // (NY * NZ)
        spot_y = (spot // NZ) % NY
        spot_z = spot % NZ
        place_x = placed // NY
        place_y = placed % NY
        records = []
        for moment in range(2):
            lap_fwd = laplace(current_fwd)
            lap_back = laplace(current_back)
            new_fwd = 2.0 * current_fwd - older_fwd + courant * lap_fwd
            new_fwd = new_fwd.at[spot_x, spot_y, spot_z].add(courant[spot_x, spot_y, spot_z] * amplitude[moment])
            new_back = 2.0 * current_back - older_back + courant * lap_back
            plane = jnp.zeros((NX, NY), jnp.float32).at[place_x, place_y].add(injected[moment])
            new_back = new_back.at[:, :, RDEPTH].add(courant[:, :, RDEPTH] * plane)
            image_total = image_total + lap_fwd * new_back
            light_total = light_total + lap_fwd * lap_fwd
            records.append(new_fwd[place_x, place_y, RDEPTH])
            older_fwd, current_fwd = current_fwd, new_fwd
            older_back, current_back = current_back, new_back
        return (image_total, light_total), (current_fwd, current_back, jnp.stack(records))

    empty = jnp.zeros((NX, NY, NZ), jnp.float32)
    items = (fwd_prev, fwd_now, back_prev, back_now, sources, wavelet, receivers, residual)
    (image_total, light_total), (fwd_last, back_last, traces) = lax.scan(one_shot, (empty, empty), items)
    update = image_total / (light_total + damping[0])
    weight_grad = pull_back(features, update * derivative)
    return fwd_last, back_last, traces, update, weight_grad
```

```python
import functools

import jax
import jax.numpy as jnp
from jax import lax
from jax.experimental import pallas as pl
from jax.experimental.pallas import tpu as pltpu
from jax.sharding import PartitionSpec as P

RDEPTH = 3
COEFFICIENTS = (-205.0 / 72.0, 8.0 / 5.0, -1.0 / 5.0, 8.0 / 315.0, -1.0 / 560.0)
F32 = jnp.float32
BF16 = jnp.bfloat16
VMEM_LIMIT = 48 * 1024 * 1024

VM = pl.BlockSpec(memory_space=pltpu.VMEM)
SM = pl.BlockSpec(memory_space=pltpu.SMEM)


def call(body, outs, ins, specs, scratch=(), flops=1_000_000, name=None):
    moved = sum(a.size * a.dtype.itemsize for a in ins) + sum(
        o.size * jnp.dtype(o.dtype).itemsize for o in outs
    )
    single = len(outs) == 1
    return pl.pallas_call(
        body,
        out_shape=outs[0] if single else tuple(outs),
        in_specs=specs,
        out_specs=VM if single else tuple(VM for _ in outs),
        scratch_shapes=list(scratch),
        compiler_params=pltpu.CompilerParams(vmem_limit_bytes=VMEM_LIMIT),
        cost_estimate=pl.CostEstimate(flops=flops, bytes_accessed=moved, transcendentals=0),
        name=name,
    )(*ins)


def shape(*dims, dtype=F32):
    return jax.ShapeDtypeStruct(dims, dtype)


def split3(value):
    top = value.astype(BF16)
    rest = value - top.astype(F32)
    middle = rest.astype(BF16)
    low = (rest - middle.astype(F32)).astype(BF16)
    return (top, middle, low)


def shifted_lanes(value, by):
    depth = value.shape[1]
    lane = lax.broadcasted_iota(jnp.int32, value.shape, 1)
    if by > 0:
        return jnp.where(lane < depth - by, pltpu.roll(value, depth - by, 1), 0.0)
    return jnp.where(lane >= -by, pltpu.roll(value, -by, 1), 0.0)


def shifted_rows(value, by):
    count = value.shape[0]
    row = lax.broadcasted_iota(jnp.int32, value.shape, 0)
    if by > 0:
        return jnp.where(row < count - by, pltpu.roll(value, count - by, 0), 0.0)
    return jnp.where(row >= -by, pltpu.roll(value, -by, 0), 0.0)


def pack_x_body(feat_ref, fwd_ref, back_ref, up_ref, down_ref):
    channels, size_x = feat_ref.shape[:2]
    up_ref[0:4] = fwd_ref[size_x - 4 : size_x]
    up_ref[4:8] = back_ref[size_x - 4 : size_x]
    down_ref[0:4] = fwd_ref[0:4]
    down_ref[4:8] = back_ref[0:4]
    for c in range(channels):
        up_ref[8 + c] = feat_ref[c, size_x - 1].astype(F32)
        down_ref[8 + c] = feat_ref[c, 0].astype(F32)


def pack_y_body(feat_ref, fwd_ref, back_ref, low_ref, high_ref, up_ref, down_ref, plane_ref):
    channels, size_x, size_y, depth = feat_ref.shape
    groups = size_x // 8 + 1
    up_ref[0:size_x, 0:4] = fwd_ref[:, size_y - 4 : size_y]
    up_ref[0:size_x, 4:8] = back_ref[:, size_y - 4 : size_y]
    down_ref[0:size_x, 0:4] = fwd_ref[:, 0:4]
    down_ref[0:size_x, 4:8] = back_ref[:, 0:4]
    row = lax.broadcasted_iota(jnp.int32, (8, depth), 0)
    for c in range(channels):
        plane_ref[...] = feat_ref[c].astype(F32)
        for out_ref, y in ((up_ref, size_y - 1), (down_ref, 0)):
            own = plane_ref[:, y, :]
            first = size_x + c * groups
            out_ref[first : first + groups - 1] = own.reshape(groups - 1, 8, depth)
            low = low_ref[8 + c, y : y + 1, :]
            high = high_ref[8 + c, y : y + 1, :]
            tail = jnp.where(row == 0, low, jnp.where(row == 1, high, 0.0))
            out_ref[first + groups - 1] = tail


def fill_features(ext_ref, feat_ref, low_ref, high_ref):
    channels, size_x = feat_ref.shape[:2]
    for c in range(channels):
        ext_ref[c, 0] = low_ref[8 + c]
        ext_ref[c, 1 : 1 + size_x] = feat_ref[c].astype(F32)
        ext_ref[c, 1 + size_x] = high_ref[8 + c]


def conv_body(feat_ref, low_ref, high_ref, weight_ref, out_ref, ext_ref):
    channels, size_x = feat_ref.shape[:2]
    fill_features(ext_ref, feat_ref, low_ref, high_ref)

    def one_row(i, carry):
        terms = [[None] * 3 for _ in range(3)]
        for c in range(channels):
            for dx in range(3):
                row = ext_ref[c, i + dx]
                for dy in range(3):
                    for dz in range(3):
                        part = weight_ref[c, 9 * dx + 3 * dy + dz] * row
                        old = terms[dy][dz]
                        terms[dy][dz] = part if old is None else old + part
        total = None
        for dy in range(3):
            part = (
                terms[dy][1]
                + shifted_lanes(terms[dy][0], -1)
                + shifted_lanes(terms[dy][2], 1)
            )
            if dy != 1:
                part = shifted_rows(part, dy - 1)
            total = part if total is None else total + part
        out_ref[i] = total
        return carry

    lax.fori_loop(0, size_x, one_row, 0)


def load_plane(plane_ref, buffer_ref, c, size_x):
    groups = size_x // 8 + 1
    depth = plane_ref.shape[1]
    first = size_x + c * groups
    plane_ref[8 : 8 + size_x] = buffer_ref[first : first + groups - 1].reshape(size_x, depth)
    plane_ref[7:8] = buffer_ref[first + groups - 1, 0:1, :]
    plane_ref[8 + size_x : 9 + size_x] = buffer_ref[first + groups - 1, 1:2, :]


def conv_edge_body(main_ref, low_ref, high_ref, weight_ref, out_ref, plane_ref):
    size_x, size_y, depth = main_ref.shape
    channels = weight_ref.shape[0]
    out_ref[...] = main_ref[...]
    for buffer_ref, dy, y in ((low_ref, 0, 0), (high_ref, 2, size_y - 1)):
        terms = [None] * 3
        for c in range(channels):
            load_plane(plane_ref, buffer_ref, c, size_x)
            for dx in range(3):
                rows = plane_ref[7 + dx : 7 + dx + size_x]
                for dz in range(3):
                    part = weight_ref[c, 9 * dx + 3 * dy + dz] * rows
                    terms[dz] = part if terms[dz] is None else terms[dz] + part
        total = terms[1] + shifted_lanes(terms[0], -1) + shifted_lanes(terms[2], 1)
        out_ref[:, y : y + 1, :] += total.reshape(size_x, 1, depth)


def squash_body(parts_ref, out_ref):
    count = parts_ref.shape[0]
    total = parts_ref[0]
    for n in range(1, count):
        total = total + parts_ref[n]
    squashed = jax.nn.sigmoid(total)
    for n in range(count):
        out_ref[n] = squashed


def update_body(parts_ref, damping_ref, out_ref):
    count, rows = parts_ref.shape[:2]
    half = rows // 2
    total = parts_ref[0]
    for n in range(1, count):
        total = total + parts_ref[n]
    update = total[:half] / (total[half:] + damping_ref[0])
    for n in range(count):
        out_ref[n] = update


def step_body(moment, plane_y, rows, refs):
    (
        fwd_ref,
        back_ref,
        fwd_old_ref,
        back_old_ref,
        squashed_ref,
        x_low_ref,
        x_high_ref,
        y_low_ref,
        y_high_ref,
        place_ref,
        wavelet_ref,
        receivers_ref,
        residual_ref,
        *rest,
    ) = refs
    if moment == 0:
        (fwd_new_ref, back_new_ref, lap_ref, trace_ref) = rest[:4]
        (x_up_ref, x_down_ref, y_up_ref, y_down_ref) = rest[4:8]
        scratch = rest[8:]
    else:
        lap_old_ref = rest[0]
        (fwd_new_ref, back_new_ref, sums_ref, trace_ref) = rest[1:5]
        scratch = rest[5:]
    fwd_x_ref, back_x_ref, fwd_y_ref, back_y_ref, inject_ref = scratch
    size_x, size_y, depth = fwd_ref.shape
    cells = size_x * size_y
    count = receivers_ref.shape[1]
    for first, ref, x_ref, y_ref in (
        (0, fwd_ref, fwd_x_ref, fwd_y_ref),
        (4, back_ref, back_x_ref, back_y_ref),
    ):
        x_ref[0:4] = x_low_ref[first : first + 4]
        x_ref[4 : 4 + size_x] = ref[...]
        x_ref[4 + size_x : 8 + size_x] = x_high_ref[first : first + 4]
        y_ref[:, 4:8] = y_low_ref[0:size_x, first : first + 4]
        y_ref[:, 8 : 8 + size_y] = ref[...]
        y_ref[:, 8 + size_y : 12 + size_y] = y_high_ref[0:size_x, first : first + 4]

    anchor_x, anchor_y, source = place_ref[0], place_ref[1], place_ref[2]
    shift_y = plane_y.bit_length() - 1
    shift_z = depth.bit_length() - 1
    column = lax.shift_right_logical(source, shift_z)
    source_x = lax.shift_right_logical(column, shift_y) - anchor_x
    source_y = (column & (plane_y - 1)) - anchor_y
    source_z = source & (depth - 1)
    here = (source_x >= 0) & (source_x < size_x) & (source_y >= 0) & (source_y < size_y)
    spot = jnp.where(here, (source_x * size_y + source_y) * depth + source_z, -1)
    amplitude = wavelet_ref[0, moment]

    receivers = receivers_ref[...]
    place_x = lax.shift_right_logical(receivers, shift_y) - anchor_x
    place_y = (receivers & (plane_y - 1)) - anchor_y
    inside = (place_x >= 0) & (place_x < size_x) & (place_y >= 0) & (place_y < size_y)
    cell = jnp.where(inside, place_x * size_y + place_y, -1)
    hit = (
        (lax.broadcasted_iota(jnp.int32, (cells, count), 0) == cell).astype(F32).astype(BF16)
    )
    injected = jnp.where(
        lax.broadcasted_iota(jnp.int32, (depth, count), 0) == RDEPTH,
        residual_ref[0, moment : moment + 1, :],
        0.0,
    )
    total = None
    for part in split3(injected):
        product = lax.dot_general(
            hit, part, (((1,), (1,)), ((), ())), preferred_element_type=F32
        )
        total = product if total is None else total + product
    inject_ref[...] = total.reshape(size_x, size_y, depth)

    def laplacian(x_ref, y_ref, start):
        centre = x_ref[pl.ds(start + 4, rows)]
        flat = centre.reshape(rows * size_y, depth)
        result = (3.0 * COEFFICIENTS[0]) * centre
        for k in range(1, 5):
            along_x = x_ref[pl.ds(start + 4 + k, rows)] + x_ref[pl.ds(start + 4 - k, rows)]
            along_y = (
                y_ref[pl.ds(start, rows), 8 + k : 8 + k + size_y, :]
                + y_ref[pl.ds(start, rows), 8 - k : 8 - k + size_y, :]
            )
            along_z = (shifted_lanes(flat, k) + shifted_lanes(flat, -k)).reshape(centre.shape)
            result = result + COEFFICIENTS[k] * (along_x + along_y + along_z)
        return centre, result

    def one_block(i, carry):
        start = i * rows
        here = pl.ds(start, rows)
        courant = 0.02 + 0.16 * squashed_ref[here]
        fwd, lap_fwd = laplacian(fwd_x_ref, fwd_y_ref, start)
        back, lap_back = laplacian(back_x_ref, back_y_ref, start)
        index = (
            lax.broadcasted_iota(jnp.int32, fwd.shape, 0) * (size_y * depth)
            + lax.broadcasted_iota(jnp.int32, fwd.shape, 1) * depth
            + lax.broadcasted_iota(jnp.int32, fwd.shape, 2)
        )
        added = jnp.where(index == spot - start * (size_y * depth), amplitude, 0.0)
        fwd_new = 2.0 * fwd - fwd_old_ref[here] + courant * lap_fwd + courant * added
        back_new = (
            2.0 * back - back_old_ref[here] + courant * lap_back + courant * inject_ref[here]
        )
        fwd_new_ref[here] = fwd_new
        back_new_ref[here] = back_new
        if moment == 0:
            lap_ref[here] = lap_fwd
        else:
            lap_old = lap_old_ref[here]
            sums_ref[i, 0:rows] = lap_old * back + lap_fwd * back_new
            sums_ref[i, rows : 2 * rows] = lap_old * lap_old + lap_fwd * lap_fwd
        return carry

    lax.fori_loop(0, size_x // rows, one_block, 0)

    total = None
    for part in split3(fwd_new_ref[...].reshape(cells, depth)):
        product = lax.dot_general(
            part, hit, (((0,), (0,)), ((), ())), preferred_element_type=F32
        )
        total = product if total is None else total + product
    trace_ref[...] = total[RDEPTH : RDEPTH + 1, :]

    if moment == 0:
        x_up_ref[0:4] = fwd_new_ref[size_x - 4 : size_x]
        x_up_ref[4:8] = back_new_ref[size_x - 4 : size_x]
        x_down_ref[0:4] = fwd_new_ref[0:4]
        x_down_ref[4:8] = back_new_ref[0:4]
        y_up_ref[:, 0:4] = fwd_new_ref[:, size_y - 4 : size_y]
        y_up_ref[:, 4:8] = back_new_ref[:, size_y - 4 : size_y]
        y_down_ref[:, 0:4] = fwd_new_ref[:, 0:4]
        y_down_ref[:, 4:8] = back_new_ref[:, 0:4]


def gradient_body(
    update_ref,
    squashed_ref,
    feat_ref,
    x_low_ref,
    x_high_ref,
    y_low_ref,
    y_high_ref,
    first_ref,
    second_ref,
    out_ref,
    ext_ref,
    moved_ref,
    plane_ref,
    rows_ref,
):
    size_x, size_y, depth = update_ref.shape
    channels = feat_ref.shape[0]
    copies = out_ref.shape[0]
    fill_features(ext_ref, feat_ref, x_low_ref, x_high_ref)

    def one_row(i, carry):
        squashed = squashed_ref[i]
        pulled = update_ref[i] * (0.16 * squashed * (1.0 - squashed))
        for dz in range(3):
            along = pulled if dz == 1 else shifted_lanes(pulled, 1 - dz)
            for dy in range(3):
                moved_ref[3 * dy + dz, i] = along if dy == 1 else shifted_rows(along, 1 - dy)
        edge = pulled[0:1, :], pulled[size_y - 1 : size_y, :]
        plane_ref[1, pl.ds(i, 1)] = edge[0]
        plane_ref[2, pl.ds(i, 1)] = edge[1]
        return carry

    lax.fori_loop(0, size_x, one_row, 0)
    rows_ref[...] = jnp.zeros_like(rows_ref)

    for c in range(channels):

        def add_row(i, totals):
            features = [ext_ref[c, i + dx] for dx in range(3)]
            new = []
            for dx in range(3):
                for dy in range(3):
                    for dz in range(3):
                        product = features[dx] * moved_ref[3 * dy + dz, i]
                        folded = product[0:8]
                        for y in range(8, size_y, 8):
                            folded = folded + product[y : y + 8]
                        new.append(totals[9 * dx + 3 * dy + dz] + folded)
            return tuple(new)

        zero = jnp.zeros((8, depth), F32)
        totals = lax.fori_loop(0, size_x, add_row, (zero,) * 27)
        for o in range(27):
            at = c * 27 + o
            rows_ref[at : at + 1] = jnp.sum(totals[o], axis=0, keepdims=True)

    for buffer_ref, dy, which in ((y_low_ref, 0, 1), (y_high_ref, 2, 2)):
        pulled = plane_ref[which, 0:size_x]
        along = [pulled if dz == 1 else shifted_lanes(pulled, 1 - dz) for dz in range(3)]
        for c in range(channels):
            load_plane(plane_ref.at[0], buffer_ref, c, size_x)
            for dx in range(3):
                features = plane_ref[0, 7 + dx : 7 + dx + size_x]
                for dz in range(3):
                    at = c * 27 + 9 * dx + 3 * dy + dz
                    rows_ref[at : at + 1] += jnp.sum(
                        features * along[dz], axis=0, keepdims=True
                    )

    ones = jnp.ones((8, depth), BF16)
    sums = None
    for part in split3(rows_ref[...]):
        product = lax.dot_general(
            ones, part, (((1,), (1,)), ((), ())), preferred_element_type=F32
        )
        sums = product if sums is None else sums + product
    row = lax.broadcasted_iota(jnp.int32, (8, depth), 0)
    lines = jnp.zeros((8, depth), F32)
    for moment, ref in enumerate((first_ref, second_ref)):
        pieces = ref.shape[1] // depth
        for q in range(pieces):
            piece = ref[0:1, q * depth : (q + 1) * depth]
            lines = jnp.where(row == moment * pieces + q, piece, lines)
    for n in range(copies):
        out_ref[n, 0:8] = lines
        out_ref[n, 8:16] = sums


def neighbours(up, down, axis):
    count = lax.axis_size(axis)
    low = lax.ppermute(up, axis, [(i, i + 1) for i in range(count - 1)])
    high = lax.ppermute(down, axis, [(i + 1, i) for i in range(count - 1)])
    return low, high


def per_device(
    features,
    conv_weight,
    fwd_prev,
    fwd_now,
    back_prev,
    back_now,
    sources,
    wavelet,
    receivers,
    residual,
    damping,
):
    channels, size_x, size_y, depth = features.shape
    shots = lax.axis_size("shot")
    rows = size_x // shots
    count = receivers.shape[1]
    plane_y = size_y * lax.axis_size("gy")
    blocks = lax.axis_size("gx") * lax.axis_size("gy")
    groups = size_x // 8 + 1
    grid = (size_x, size_y, depth)
    fwd_prev, fwd_now, back_prev, back_now = (
        a.reshape(grid) for a in (fwd_prev, fwd_now, back_prev, back_now)
    )
    place = jnp.stack(
        [lax.axis_index("gx") * size_x, lax.axis_index("gy") * size_y, sources[0]]
    ).astype(jnp.int32)

    x_shape = shape(8 + channels, size_y, depth)
    with jax.named_scope("pack_x"):
        x_up, x_down = call(
            pack_x_body, [x_shape, x_shape], (features, fwd_now, back_now), [VM] * 3, name="pack_x"
        )
    with jax.named_scope("halo_x"):
        x_low, x_high = neighbours(x_up, x_down, "gx")
    y_shape = shape(size_x + channels * groups, 8, depth)
    with jax.named_scope("pack_y"):
        y_up, y_down = call(
            pack_y_body,
            [y_shape, y_shape],
            (features, fwd_now, back_now, x_low, x_high),
            [VM] * 5,
            scratch=[pltpu.VMEM(grid, F32)],
            name="pack_y",
        )
    with jax.named_scope("halo_y"):
        y_low, y_high = neighbours(y_up, y_down, "gy")
    ext = pltpu.VMEM((channels, size_x + 2, size_y, depth), F32)
    with jax.named_scope("conv"):
        main = call(
            conv_body,
            [shape(*grid)],
            (features, x_low, x_high, conv_weight),
            [VM, VM, VM, SM],
            scratch=[ext],
            flops=54 * channels * size_x * size_y * depth,
            name="conv",
        )
        part = call(
            conv_edge_body,
            [shape(*grid)],
            (main, y_low, y_high, conv_weight),
            [VM, VM, VM, SM],
            scratch=[pltpu.VMEM((size_x + 16, depth), F32)],
            name="conv_edge",
        )
    with jax.named_scope("squash"):
        parts = lax.all_to_all(part, "shot", 0, 0, tiled=True)
        squashed = call(
            squash_body,
            [shape(shots, rows, size_y, depth)],
            (parts.reshape(shots, rows, size_y, depth),),
            [VM],
            name="squash",
        )
        squashed = lax.all_to_all(squashed.reshape(grid), "shot", 0, 0, tiled=True)

    scratch = [
        pltpu.VMEM((size_x + 8, size_y, depth), F32),
        pltpu.VMEM((size_x + 8, size_y, depth), F32),
        pltpu.VMEM((size_x, size_y + 16, depth), F32),
        pltpu.VMEM((size_x, size_y + 16, depth), F32),
        pltpu.VMEM(grid, F32),
    ]
    full = shape(*grid)
    specs = [VM] * 9 + [SM, SM, VM, VM]

    def step_1(*refs):
        step_body(0, plane_y, rows, refs)

    def step_2(*refs):
        step_body(1, plane_y, rows, refs)

    with jax.named_scope("step_1"):
        fwd_1, back_1, lap_1, trace_1, x_up, x_down, y_up, y_down = call(
            step_1,
            [full, full, full, shape(1, count)]
            + [shape(8, size_y, depth)] * 2
            + [shape(size_x, 8, depth)] * 2,
            (
                fwd_now,
                back_now,
                fwd_prev,
                back_prev,
                squashed,
                x_low,
                x_high,
                y_low,
                y_high,
                place,
                wavelet,
                receivers,
                residual,
            ),
            specs,
            scratch=scratch,
            name="step_1",
        )
    with jax.named_scope("halo_2"):
        y_low_2, y_high_2 = neighbours(y_up, y_down, "gy")
        x_low_2, x_high_2 = neighbours(x_up, x_down, "gx")
    with jax.named_scope("step_2"):
        fwd_2, back_2, sums, trace_2 = call(
            step_2,
            [full, full, shape(shots, 2 * rows, size_y, depth), shape(1, count)],
            (
                fwd_1,
                back_1,
                fwd_now,
                back_now,
                squashed,
                x_low_2,
                x_high_2,
                y_low_2,
                y_high_2,
                place,
                wavelet,
                receivers,
                residual,
                lap_1,
            ),
            specs + [VM],
            scratch=scratch,
            name="step_2",
        )
    with jax.named_scope("update"):
        sums = lax.all_to_all(
            sums.reshape(shots * 2 * rows, size_y, depth), "shot", 0, 0, tiled=True
        )
        update = call(
            update_body,
            [shape(shots, rows, size_y, depth)],
            (sums.reshape(shots, 2 * rows, size_y, depth), damping),
            [VM, SM],
            name="update",
        )
        update = lax.all_to_all(update.reshape(grid), "shot", 0, 0, tiled=True)
    with jax.named_scope("gradient"):
        share = call(
            gradient_body,
            [shape(blocks, 16, depth)],
            (update, squashed, features, x_low, x_high, y_low, y_high, trace_1, trace_2),
            [VM] * 9,
            scratch=[
                ext,
                pltpu.VMEM((9,) + grid, F32),
                pltpu.VMEM((3, size_x + 16, depth), F32),
                pltpu.VMEM((128, depth), F32),
            ],
            flops=54 * channels * size_x * size_y * depth,
            name="gradient",
        )
        shares = lax.all_to_all(
            share.reshape(blocks * 16, depth), ("gx", "gy"), 0, 0, tiled=True
        )
        total = jnp.sum(shares.reshape(blocks, 16, depth), axis=0)
    traces = total[:8].reshape(-1)[: 2 * count].reshape(1, 2, count)
    weight_grad = total[8, : 27 * channels].reshape(channels, 27)
    return (fwd_2[None], back_2[None], traces, update, weight_grad)


def solution(mesh):
    in_specs = (
        P("shot", "gx", "gy", None),
        P("shot", None),
        P("shot", "gx", "gy", None),
        P("shot", "gx", "gy", None),
        P("shot", "gx", "gy", None),
        P("shot", "gx", "gy", None),
        P("shot"),
        P("shot", None),
        P("shot", None),
        P("shot", None, None),
        P(),
    )
    out_specs = (
        P("shot", "gx", "gy", None),
        P("shot", "gx", "gy", None),
        P("shot", None, None),
        P("gx", "gy", None),
        P("shot", None),
    )
    return jax.shard_map(
        per_device, mesh=mesh, in_specs=in_specs, out_specs=out_specs, check_vma=False
    )
```

```python
import functools

import jax
import jax.numpy as jnp
from jax import lax
from jax.experimental import pallas as pl
from jax.experimental.pallas import tpu as pltpu
from jax.sharding import PartitionSpec as P

RDEPTH = 3
COEFFICIENTS = (-205.0 / 72.0, 8.0 / 5.0, -1.0 / 5.0, 8.0 / 315.0, -1.0 / 560.0)
F32 = jnp.float32
BF16 = jnp.bfloat16
VMEM_LIMIT = 48 * 1024 * 1024

VM = pl.BlockSpec(memory_space=pltpu.VMEM)
SM = pl.BlockSpec(memory_space=pltpu.SMEM)


def call(body, outs, ins, specs, scratch=(), flops=1_000_000, name=None, grid=()):
    moved = sum(a.size * a.dtype.itemsize for a in ins) + sum(
        o.size * jnp.dtype(o.dtype).itemsize for o in outs
    )
    single = len(outs) == 1
    return pl.pallas_call(
        body,
        grid=grid,
        out_shape=outs[0] if single else tuple(outs),
        in_specs=specs,
        out_specs=VM if single else tuple(VM for _ in outs),
        scratch_shapes=list(scratch),
        compiler_params=pltpu.CompilerParams(vmem_limit_bytes=VMEM_LIMIT),
        cost_estimate=pl.CostEstimate(flops=flops, bytes_accessed=moved, transcendentals=0),
        name=name,
    )(*ins)


def shape(*dims, dtype=F32):
    return jax.ShapeDtypeStruct(dims, dtype)


def split3(value):
    top = value.astype(BF16)
    rest = value - top.astype(F32)
    middle = rest.astype(BF16)
    low = (rest - middle.astype(F32)).astype(BF16)
    return (top, middle, low)


def shifted_lanes(value, by):
    depth = value.shape[1]
    lane = lax.broadcasted_iota(jnp.int32, value.shape, 1)
    if by > 0:
        return jnp.where(lane < depth - by, pltpu.roll(value, depth - by, 1), 0.0)
    return jnp.where(lane >= -by, pltpu.roll(value, -by, 1), 0.0)


def shifted_rows(value, by):
    count = value.shape[0]
    row = lax.broadcasted_iota(jnp.int32, value.shape, 0)
    if by > 0:
        return jnp.where(row < count - by, pltpu.roll(value, count - by, 0), 0.0)
    return jnp.where(row >= -by, pltpu.roll(value, -by, 0), 0.0)


def pack_x_body(
    feat_first_ref,
    feat_last_ref,
    fwd_first_ref,
    fwd_last_ref,
    back_first_ref,
    back_last_ref,
    up_ref,
    down_ref,
):
    channels = feat_first_ref.shape[0]
    up_ref[0:4] = fwd_last_ref[...]
    up_ref[4:8] = back_last_ref[...]
    down_ref[0:4] = fwd_first_ref[...]
    down_ref[4:8] = back_first_ref[...]
    for c in range(channels):
        up_ref[8 + c] = feat_last_ref[c, 0].astype(F32)
        down_ref[8 + c] = feat_first_ref[c, 0].astype(F32)


def pack_y_body(feat_ref, low_ref, high_ref, up_ref, down_ref, plane_ref):
    channels, size_x, size_y, depth = feat_ref.shape
    row = lax.broadcasted_iota(jnp.int32, (16, depth), 0)
    tails = [jnp.zeros((16, depth), F32), jnp.zeros((16, depth), F32)]
    for c in range(channels):
        plane_ref[...] = feat_ref[c].astype(F32)
        for n, (out_ref, y) in enumerate(((up_ref, size_y - 1), (down_ref, 0))):
            out_ref[c * size_x : (c + 1) * size_x] = plane_ref[:, y, :].astype(BF16)
            tails[n] = jnp.where(row == 2 * c, low_ref[8 + c, y : y + 1, :], tails[n])
            tails[n] = jnp.where(row == 2 * c + 1, high_ref[8 + c, y : y + 1, :], tails[n])
    for tail, out_ref in zip(tails, (up_ref, down_ref)):
        out_ref[channels * size_x : channels * size_x + 16] = tail.astype(BF16)


def pack_waves_body(fwd_ref, back_ref, up_ref, down_ref):
    size_y = fwd_ref.shape[1]
    up_ref[:, 0:4] = fwd_ref[:, size_y - 4 : size_y]
    up_ref[:, 4:8] = back_ref[:, size_y - 4 : size_y]
    down_ref[:, 0:4] = fwd_ref[:, 0:4]
    down_ref[:, 4:8] = back_ref[:, 0:4]


def fill_features(ext_ref, feat_ref, low_ref, high_ref):
    channels, size_x = feat_ref.shape[:2]
    for c in range(channels):
        ext_ref[c, 0] = low_ref[8 + c]
        ext_ref[c, 1 : 1 + size_x] = feat_ref[c].astype(F32)
        ext_ref[c, 1 + size_x] = high_ref[8 + c]


def conv_body(feat_ref, low_ref, high_ref, weight_ref, out_ref, ext_ref):
    channels, size_x = feat_ref.shape[:2]
    fill_features(ext_ref, feat_ref, low_ref, high_ref)

    def one_row(i, carry):
        terms = [[None] * 3 for _ in range(3)]
        for c in range(channels):
            for dx in range(3):
                row = ext_ref[c, i + dx]
                for dy in range(3):
                    for dz in range(3):
                        part = weight_ref[c, 9 * dx + 3 * dy + dz] * row
                        old = terms[dy][dz]
                        terms[dy][dz] = part if old is None else old + part
        total = None
        for dy in range(3):
            part = (
                terms[dy][1]
                + shifted_lanes(terms[dy][0], -1)
                + shifted_lanes(terms[dy][2], 1)
            )
            if dy != 1:
                part = shifted_rows(part, dy - 1)
            total = part if total is None else total + part
        out_ref[i] = total
        return carry

    lax.fori_loop(0, size_x, one_row, 0)


def load_plane(plane_ref, buffer_ref, c, size_x, channels):
    plane_ref[8 : 8 + size_x] = buffer_ref[c * size_x : (c + 1) * size_x].astype(F32)
    tail = buffer_ref[channels * size_x : channels * size_x + 16].astype(F32)
    plane_ref[7:8] = tail[2 * c : 2 * c + 1]
    plane_ref[8 + size_x : 9 + size_x] = tail[2 * c + 1 : 2 * c + 2]


def conv_edge_body(main_ref, low_ref, high_ref, weight_ref, out_ref, plane_ref):
    size_x, size_y, depth = main_ref.shape
    channels = weight_ref.shape[0]
    out_ref[...] = main_ref[...]
    for buffer_ref, dy, y in ((low_ref, 0, 0), (high_ref, 2, size_y - 1)):
        terms = [None] * 3
        for c in range(channels):
            load_plane(plane_ref, buffer_ref, c, size_x, channels)
            for dx in range(3):
                rows = plane_ref[7 + dx : 7 + dx + size_x]
                for dz in range(3):
                    part = weight_ref[c, 9 * dx + 3 * dy + dz] * rows
                    terms[dz] = part if terms[dz] is None else terms[dz] + part
        total = terms[1] + shifted_lanes(terms[0], -1) + shifted_lanes(terms[2], 1)
        out_ref[:, y : y + 1, :] += total.reshape(size_x, 1, depth)


def squash_body(parts_ref, out_ref):
    count = parts_ref.shape[0]
    total = parts_ref[0]
    for n in range(1, count):
        total = total + parts_ref[n]
    squashed = jax.nn.sigmoid(total)
    for n in range(count):
        out_ref[n] = squashed


def update_body(parts_ref, damping_ref, out_ref):
    count, rows = parts_ref.shape[:2]
    half = rows // 2
    total = parts_ref[0]
    for n in range(1, count):
        total = total + parts_ref[n]
    update = total[:half] / (total[half:] + damping_ref[0])
    for n in range(count):
        out_ref[n] = update


def step_body(moment, plane_y, rows, refs):
    (
        fwd_ref,
        back_ref,
        fwd_old_ref,
        back_old_ref,
        squashed_ref,
        x_low_ref,
        x_high_ref,
        y_low_ref,
        y_high_ref,
        place_ref,
        wavelet_ref,
        receivers_ref,
        residual_ref,
        *rest,
    ) = refs
    if moment == 0:
        (fwd_new_ref, back_new_ref, lap_ref, trace_ref) = rest[:4]
        (x_up_ref, x_down_ref, y_up_ref, y_down_ref) = rest[4:8]
        scratch = rest[8:]
    else:
        lap_old_ref = rest[0]
        (fwd_new_ref, back_new_ref, sums_ref, trace_ref) = rest[1:5]
        scratch = rest[5:]
    fwd_x_ref, back_x_ref, fwd_y_ref, back_y_ref, inject_ref = scratch
    size_x, size_y, depth = fwd_ref.shape
    cells = size_x * size_y
    count = receivers_ref.shape[1]
    for first, ref, x_ref, y_ref in (
        (0, fwd_ref, fwd_x_ref, fwd_y_ref),
        (4, back_ref, back_x_ref, back_y_ref),
    ):
        x_ref[0:4] = x_low_ref[first : first + 4]
        x_ref[4 : 4 + size_x] = ref[...]
        x_ref[4 + size_x : 8 + size_x] = x_high_ref[first : first + 4]
        y_ref[:, 4:8] = y_low_ref[0:size_x, first : first + 4]
        y_ref[:, 8 : 8 + size_y] = ref[...]
        y_ref[:, 8 + size_y : 12 + size_y] = y_high_ref[0:size_x, first : first + 4]

    anchor_x, anchor_y, source = place_ref[0], place_ref[1], place_ref[2]
    shift_y = plane_y.bit_length() - 1
    shift_z = depth.bit_length() - 1
    column = lax.shift_right_logical(source, shift_z)
    source_x = lax.shift_right_logical(column, shift_y) - anchor_x
    source_y = (column & (plane_y - 1)) - anchor_y
    source_z = source & (depth - 1)
    here = (source_x >= 0) & (source_x < size_x) & (source_y >= 0) & (source_y < size_y)
    spot = jnp.where(here, (source_x * size_y + source_y) * depth + source_z, -1)
    amplitude = wavelet_ref[0, moment]

    receivers = receivers_ref[...]
    place_x = lax.shift_right_logical(receivers, shift_y) - anchor_x
    place_y = (receivers & (plane_y - 1)) - anchor_y
    inside = (place_x >= 0) & (place_x < size_x) & (place_y >= 0) & (place_y < size_y)
    cell = jnp.where(inside, place_x * size_y + place_y, -1)
    hit = (
        (lax.broadcasted_iota(jnp.int32, (cells, count), 0) == cell).astype(F32).astype(BF16)
    )
    injected = jnp.where(
        lax.broadcasted_iota(jnp.int32, (depth, count), 0) == RDEPTH,
        residual_ref[0, moment : moment + 1, :],
        0.0,
    )
    total = None
    for part in split3(injected):
        product = lax.dot_general(
            hit, part, (((1,), (1,)), ((), ())), preferred_element_type=F32
        )
        total = product if total is None else total + product
    inject_ref[...] = total.reshape(size_x, size_y, depth)

    def laplacian(x_ref, y_ref, start):
        centre = x_ref[pl.ds(start + 4, rows)]
        flat = centre.reshape(rows * size_y, depth)
        result = (3.0 * COEFFICIENTS[0]) * centre
        for k in range(1, 5):
            along_x = x_ref[pl.ds(start + 4 + k, rows)] + x_ref[pl.ds(start + 4 - k, rows)]
            along_y = (
                y_ref[pl.ds(start, rows), 8 + k : 8 + k + size_y, :]
                + y_ref[pl.ds(start, rows), 8 - k : 8 - k + size_y, :]
            )
            along_z = (shifted_lanes(flat, k) + shifted_lanes(flat, -k)).reshape(centre.shape)
            result = result + COEFFICIENTS[k] * (along_x + along_y + along_z)
        return centre, result

    def one_block(i, carry):
        start = i * rows
        here = pl.ds(start, rows)
        courant = 0.02 + 0.16 * squashed_ref[here]
        fwd, lap_fwd = laplacian(fwd_x_ref, fwd_y_ref, start)
        back, lap_back = laplacian(back_x_ref, back_y_ref, start)
        index = (
            lax.broadcasted_iota(jnp.int32, fwd.shape, 0) * (size_y * depth)
            + lax.broadcasted_iota(jnp.int32, fwd.shape, 1) * depth
            + lax.broadcasted_iota(jnp.int32, fwd.shape, 2)
        )
        added = jnp.where(index == spot - start * (size_y * depth), amplitude, 0.0)
        fwd_new = 2.0 * fwd - fwd_old_ref[here] + courant * lap_fwd + courant * added
        back_new = (
            2.0 * back - back_old_ref[here] + courant * lap_back + courant * inject_ref[here]
        )
        fwd_new_ref[here] = fwd_new
        back_new_ref[here] = back_new
        if moment == 0:
            lap_ref[here] = lap_fwd
        else:
            lap_old = lap_old_ref[here]
            sums_ref[i, 0:rows] = lap_old * back + lap_fwd * back_new
            sums_ref[i, rows : 2 * rows] = lap_old * lap_old + lap_fwd * lap_fwd
        return carry

    lax.fori_loop(0, size_x // rows, one_block, 0)

    total = None
    for part in split3(fwd_new_ref[...].reshape(cells, depth)):
        product = lax.dot_general(
            part, hit, (((0,), (0,)), ((), ())), preferred_element_type=F32
        )
        total = product if total is None else total + product
    trace_ref[...] = total[RDEPTH : RDEPTH + 1, :]

    if moment == 0:
        x_up_ref[0:4] = fwd_new_ref[size_x - 4 : size_x]
        x_up_ref[4:8] = back_new_ref[size_x - 4 : size_x]
        x_down_ref[0:4] = fwd_new_ref[0:4]
        x_down_ref[4:8] = back_new_ref[0:4]
        y_up_ref[:, 0:4] = fwd_new_ref[:, size_y - 4 : size_y]
        y_up_ref[:, 4:8] = back_new_ref[:, size_y - 4 : size_y]
        y_down_ref[:, 0:4] = fwd_new_ref[:, 0:4]
        y_down_ref[:, 4:8] = back_new_ref[:, 0:4]


def gradient_body(
    update_ref,
    squashed_ref,
    feat_ref,
    x_low_ref,
    x_high_ref,
    y_low_ref,
    y_high_ref,
    first_ref,
    second_ref,
    out_ref,
    ext_ref,
    moved_ref,
    plane_ref,
    rows_ref,
):
    size_x, size_y, depth = update_ref.shape
    channels = feat_ref.shape[0]
    copies = out_ref.shape[0]
    fill_features(ext_ref, feat_ref, x_low_ref, x_high_ref)

    def one_row(i, carry):
        squashed = squashed_ref[i]
        pulled = update_ref[i] * (0.16 * squashed * (1.0 - squashed))
        for dz in range(3):
            along = pulled if dz == 1 else shifted_lanes(pulled, 1 - dz)
            for dy in range(3):
                moved_ref[3 * dy + dz, i] = along if dy == 1 else shifted_rows(along, 1 - dy)
        edge = pulled[0:1, :], pulled[size_y - 1 : size_y, :]
        plane_ref[1, pl.ds(i, 1)] = edge[0]
        plane_ref[2, pl.ds(i, 1)] = edge[1]
        return carry

    lax.fori_loop(0, size_x, one_row, 0)
    rows_ref[...] = jnp.zeros_like(rows_ref)

    for c in range(channels):

        def add_row(i, totals):
            features = [ext_ref[c, i + dx] for dx in range(3)]
            new = []
            for dx in range(3):
                for dy in range(3):
                    for dz in range(3):
                        product = features[dx] * moved_ref[3 * dy + dz, i]
                        folded = product[0:8]
                        for y in range(8, size_y, 8):
                            folded = folded + product[y : y + 8]
                        new.append(totals[9 * dx + 3 * dy + dz] + folded)
            return tuple(new)

        zero = jnp.zeros((8, depth), F32)
        totals = lax.fori_loop(0, size_x, add_row, (zero,) * 27)
        for o in range(27):
            at = c * 27 + o
            rows_ref[at : at + 1] = jnp.sum(totals[o], axis=0, keepdims=True)

    for buffer_ref, dy, which in ((y_low_ref, 0, 1), (y_high_ref, 2, 2)):
        pulled = plane_ref[which, 0:size_x]
        along = [pulled if dz == 1 else shifted_lanes(pulled, 1 - dz) for dz in range(3)]
        for c in range(channels):
            load_plane(plane_ref.at[0], buffer_ref, c, size_x, channels)
            for dx in range(3):
                features = plane_ref[0, 7 + dx : 7 + dx + size_x]
                for dz in range(3):
                    at = c * 27 + 9 * dx + 3 * dy + dz
                    rows_ref[at : at + 1] += jnp.sum(
                        features * along[dz], axis=0, keepdims=True
                    )

    ones = jnp.ones((8, depth), BF16)
    sums = None
    for part in split3(rows_ref[...]):
        product = lax.dot_general(
            ones, part, (((1,), (1,)), ((), ())), preferred_element_type=F32
        )
        sums = product if sums is None else sums + product
    count = first_ref.shape[1]
    for n in range(copies):
        out_ref[n, :, 0:count] = first_ref[...]
        out_ref[n, :, count : 2 * count] = second_ref[...]
        out_ref[n, :, 2 * count : 2 * count + depth] = sums[0:1]


def total_body(shares_ref, trace_ref, grad_ref):
    copies = shares_ref.shape[0]
    count = trace_ref.shape[2]
    channels, offsets = grad_ref.shape
    total = shares_ref[0]
    for n in range(1, copies):
        total = total + shares_ref[n]
    trace_ref[0, 0:1, :] = total[:, 0:count]
    trace_ref[0, 1:2, :] = total[:, count : 2 * count]
    last = total[:, 2 * count :]
    lanes = last.shape[1]
    last = jnp.broadcast_to(last, (8, lanes))
    for c in range(channels):
        turned = last if c == 0 else pltpu.roll(last, lanes - c * offsets, 1)
        grad_ref[c : c + 1, :] = turned[0:1, 0:offsets]


def neighbours(up, down, axis):
    count = lax.axis_size(axis)
    low = lax.ppermute(up, axis, [(i, i + 1) for i in range(count - 1)])
    high = lax.ppermute(down, axis, [(i + 1, i) for i in range(count - 1)])
    return low, high


def per_device(
    features,
    conv_weight,
    fwd_prev,
    fwd_now,
    back_prev,
    back_now,
    sources,
    wavelet,
    receivers,
    residual,
    damping,
):
    channels, size_x, size_y, depth = features.shape
    shots = lax.axis_size("shot")
    rows = size_x // shots
    count = receivers.shape[1]
    plane_y = size_y * lax.axis_size("gy")
    blocks = lax.axis_size("gx") * lax.axis_size("gy")
    grid = (size_x, size_y, depth)
    fwd_prev, fwd_now, back_prev, back_now = (
        a.reshape(grid) for a in (fwd_prev, fwd_now, back_prev, back_now)
    )
    place = jnp.stack(
        [lax.axis_index("gx") * size_x, lax.axis_index("gy") * size_y, sources[0]]
    ).astype(jnp.int32)

    def edge(last):
        return pl.BlockSpec((4, size_y, depth), lambda i: ((size_x // 4 - 1) * last, 0, 0))

    def feature_edge(last):
        return pl.BlockSpec(
            (channels, 1, size_y, depth), lambda i: (0, (size_x - 1) * last, 0, 0)
        )

    x_shape = shape(8 + channels, size_y, depth)
    with jax.named_scope("pack_x"):
        x_up, x_down = call(
            pack_x_body,
            [x_shape, x_shape],
            (features, features, fwd_now, fwd_now, back_now, back_now),
            [feature_edge(0), feature_edge(1), edge(0), edge(1), edge(0), edge(1)],
            name="pack_x",
            grid=(1,),
        )
    with jax.named_scope("halo_x"):
        x_low, x_high = neighbours(x_up, x_down, "gx")
    y_shape = shape(channels * size_x + 16, depth, dtype=BF16)
    with jax.named_scope("pack_y"):
        y_up, y_down = call(
            pack_y_body,
            [y_shape, y_shape],
            (features, x_low, x_high),
            [VM] * 3,
            scratch=[pltpu.VMEM(grid, F32)],
            name="pack_y",
        )
    with jax.named_scope("halo_y"):
        y_low, y_high = neighbours(y_up, y_down, "gy")
    ext = pltpu.VMEM((channels, size_x + 2, size_y, depth), F32)
    with jax.named_scope("conv"):
        main = call(
            conv_body,
            [shape(*grid)],
            (features, x_low, x_high, conv_weight),
            [VM, VM, VM, SM],
            scratch=[ext],
            flops=54 * channels * size_x * size_y * depth,
            name="conv",
        )
        part = call(
            conv_edge_body,
            [shape(*grid)],
            (main, y_low, y_high, conv_weight),
            [VM, VM, VM, SM],
            scratch=[pltpu.VMEM((size_x + 16, depth), F32)],
            name="conv_edge",
        )
    wave_shape = shape(size_x, 8, depth)
    with jax.named_scope("pack_waves"):
        wave_up, wave_down = call(
            pack_waves_body,
            [wave_shape, wave_shape],
            (fwd_now, back_now),
            [VM] * 2,
            name="pack_waves",
        )
        part, wave_up, wave_down = lax.optimization_barrier((part, wave_up, wave_down))
    with jax.named_scope("squash"):
        parts = lax.all_to_all(part, "shot", 0, 0, tiled=True)
        wave_low, wave_high = neighbours(wave_up, wave_down, "gy")
        squashed = call(
            squash_body,
            [shape(shots, rows, size_y, depth)],
            (parts.reshape(shots, rows, size_y, depth),),
            [VM],
            name="squash",
        )
        squashed = lax.all_to_all(squashed.reshape(grid), "shot", 0, 0, tiled=True)

    scratch = [
        pltpu.VMEM((size_x + 8, size_y, depth), F32),
        pltpu.VMEM((size_x + 8, size_y, depth), F32),
        pltpu.VMEM((size_x, size_y + 16, depth), F32),
        pltpu.VMEM((size_x, size_y + 16, depth), F32),
        pltpu.VMEM(grid, F32),
    ]
    full = shape(*grid)
    specs = [VM] * 9 + [SM, SM, VM, VM]

    def step_1(*refs):
        step_body(0, plane_y, rows, refs)

    def step_2(*refs):
        step_body(1, plane_y, rows, refs)

    with jax.named_scope("step_1"):
        fwd_1, back_1, lap_1, trace_1, x_up, x_down, y_up, y_down = call(
            step_1,
            [full, full, full, shape(1, count)]
            + [shape(8, size_y, depth)] * 2
            + [shape(size_x, 8, depth)] * 2,
            (
                fwd_now,
                back_now,
                fwd_prev,
                back_prev,
                squashed,
                x_low,
                x_high,
                wave_low,
                wave_high,
                place,
                wavelet,
                receivers,
                residual,
            ),
            specs,
            scratch=scratch,
            name="step_1",
        )
    with jax.named_scope("halo_2"):
        x_low_2, x_high_2 = neighbours(x_up, x_down, "gx")
        y_low_2, y_high_2 = neighbours(y_up, y_down, "gy")
    with jax.named_scope("step_2"):
        fwd_2, back_2, sums, trace_2 = call(
            step_2,
            [full, full, shape(shots, 2 * rows, size_y, depth), shape(1, count)],
            (
                fwd_1,
                back_1,
                fwd_now,
                back_now,
                squashed,
                x_low_2,
                x_high_2,
                y_low_2,
                y_high_2,
                place,
                wavelet,
                receivers,
                residual,
                lap_1,
            ),
            specs + [VM],
            scratch=scratch,
            name="step_2",
        )
    with jax.named_scope("update"):
        sums = lax.all_to_all(
            sums.reshape(shots * 2 * rows, size_y, depth), "shot", 0, 0, tiled=True
        )
        update = call(
            update_body,
            [shape(shots, rows, size_y, depth)],
            (sums.reshape(shots, 2 * rows, size_y, depth), damping),
            [VM, SM],
            name="update",
        )
        update = lax.all_to_all(update.reshape(grid), "shot", 0, 0, tiled=True)
    with jax.named_scope("gradient"):
        share = call(
            gradient_body,
            [shape(blocks, 1, 2 * count + depth)],
            (update, squashed, features, x_low, x_high, y_low, y_high, trace_1, trace_2),
            [VM] * 9,
            scratch=[
                ext,
                pltpu.VMEM((9,) + grid, F32),
                pltpu.VMEM((3, size_x + 16, depth), F32),
                pltpu.VMEM((128, depth), F32),
            ],
            flops=54 * channels * size_x * size_y * depth,
            name="gradient",
        )
        shares = lax.all_to_all(share, ("gx", "gy"), 0, 0, tiled=True)
        shares = shares.reshape(blocks, 1, 2 * count + depth)
        traces, weight_grad = call(
            total_body,
            [shape(1, 2, count), shape(channels, 27)],
            (shares,),
            [VM],
            name="total",
        )
    return (fwd_2[None], back_2[None], traces, update, weight_grad)


def solution(mesh):
    in_specs = (
        P("shot", "gx", "gy", None),
        P("shot", None),
        P("shot", "gx", "gy", None),
        P("shot", "gx", "gy", None),
        P("shot", "gx", "gy", None),
        P("shot", "gx", "gy", None),
        P("shot"),
        P("shot", None),
        P("shot", None),
        P("shot", None, None),
        P(),
    )
    out_specs = (
        P("shot", "gx", "gy", None),
        P("shot", "gx", "gy", None),
        P("shot", None, None),
        P("gx", "gy", None),
        P("shot", None),
    )
    return jax.shard_map(
        per_device, mesh=mesh, in_specs=in_specs, out_specs=out_specs, check_vma=False
    )
```

```python
import functools

import jax
import jax.numpy as jnp
from jax import lax
from jax.experimental import pallas as pl
from jax.experimental.pallas import tpu as pltpu
from jax.sharding import PartitionSpec as P

RDEPTH = 3
COEFFICIENTS = (-205.0 / 72.0, 8.0 / 5.0, -1.0 / 5.0, 8.0 / 315.0, -1.0 / 560.0)
F32 = jnp.float32
BF16 = jnp.bfloat16
VMEM_LIMIT = 48 * 1024 * 1024

VM = pl.BlockSpec(memory_space=pltpu.VMEM)
SM = pl.BlockSpec(memory_space=pltpu.SMEM)


def call(body, outs, ins, specs, scratch=(), flops=1_000_000, name=None, grid=()):
    moved = sum(a.size * a.dtype.itemsize for a in ins) + sum(
        o.size * jnp.dtype(o.dtype).itemsize for o in outs
    )
    single = len(outs) == 1
    return pl.pallas_call(
        body,
        grid=grid,
        out_shape=outs[0] if single else tuple(outs),
        in_specs=specs,
        out_specs=VM if single else tuple(VM for _ in outs),
        scratch_shapes=list(scratch),
        compiler_params=pltpu.CompilerParams(vmem_limit_bytes=VMEM_LIMIT),
        cost_estimate=pl.CostEstimate(flops=flops, bytes_accessed=moved, transcendentals=0),
        name=name,
    )(*ins)


def shape(*dims, dtype=F32):
    return jax.ShapeDtypeStruct(dims, dtype)


def split3(value):
    top = value.astype(BF16)
    rest = value - top.astype(F32)
    middle = rest.astype(BF16)
    low = (rest - middle.astype(F32)).astype(BF16)
    return (top, middle, low)


def shifted_lanes(value, by):
    depth = value.shape[1]
    lane = lax.broadcasted_iota(jnp.int32, value.shape, 1)
    if by > 0:
        return jnp.where(lane < depth - by, pltpu.roll(value, depth - by, 1), 0.0)
    return jnp.where(lane >= -by, pltpu.roll(value, -by, 1), 0.0)


def shifted_rows(value, by):
    count = value.shape[0]
    row = lax.broadcasted_iota(jnp.int32, value.shape, 0)
    if by > 0:
        return jnp.where(row < count - by, pltpu.roll(value, count - by, 0), 0.0)
    return jnp.where(row >= -by, pltpu.roll(value, -by, 0), 0.0)


def pack_x_body(feat_ref, fwd_ref, back_ref, up_ref, down_ref, edge_ref, sems):
    channels, size_x = feat_ref.shape[:2]
    copies = []
    for n, (out_ref, start, row) in enumerate(
        ((up_ref, size_x - 4, size_x - 1), (down_ref, 0, 0))
    ):
        pairs = [
            (fwd_ref.at[pl.ds(start, 4)], out_ref.at[pl.ds(0, 4)]),
            (back_ref.at[pl.ds(start, 4)], out_ref.at[pl.ds(4, 4)]),
        ]
        for c in range(channels):
            pairs.append((feat_ref.at[c, row], edge_ref.at[n * channels + c]))
        for m, (source, target) in enumerate(pairs):
            copies.append(
                pltpu.make_async_copy(source, target, sems.at[n * (2 + channels) + m])
            )
    for copy in copies:
        copy.start()
    for copy in copies:
        copy.wait()
    for c in range(channels):
        up_ref[8 + c] = edge_ref[c].astype(F32)
        down_ref[8 + c] = edge_ref[channels + c].astype(F32)


def wave_rows(size_x):
    return size_x * 12


def pack_waves(fwd_ref, back_ref, upward, out_ref, first, edge_ref, low_ref):
    size_x, size_y, depth = fwd_ref.shape
    start, near = (size_y - 4, 2) if upward else (0, 0)
    edge_ref[:, 0:4] = fwd_ref[:, start : start + 4]
    edge_ref[:, 4:8] = back_ref[:, start : start + 4]
    value = edge_ref[...].reshape(size_x * 8, depth)
    high = value.astype(BF16)
    out_ref[first : first + size_x * 8] = high
    edge_ref[...] = (value - high.astype(F32)).reshape(size_x, 8, depth)
    quarter = size_x // 4
    for q in range(4):
        part = slice(q * quarter, (q + 1) * quarter)
        low_ref[:, 4 * q : 4 * q + 2] = edge_ref[part, near : near + 2]
        low_ref[:, 4 * q + 2 : 4 * q + 4] = edge_ref[part, 4 + near : 6 + near]
    out_ref[first + size_x * 8 : first + size_x * 12] = (
        low_ref[...].reshape(size_x * 4, depth).astype(BF16)
    )


def unpack_waves(buffer_ref, upward, first, size_x, edge_ref, low_ref):
    depth = buffer_ref.shape[1]
    near = 2 if upward else 0
    quarter = size_x // 4
    edge_ref[...] = (
        buffer_ref[first : first + size_x * 8].astype(F32).reshape(size_x, 8, depth)
    )
    low_ref[...] = (
        buffer_ref[first + size_x * 8 : first + size_x * 12]
        .astype(F32)
        .reshape(quarter, 16, depth)
    )
    for q in range(4):
        part = slice(q * quarter, (q + 1) * quarter)
        edge_ref[part, near : near + 2] += low_ref[:, 4 * q : 4 * q + 2]
        edge_ref[part, 4 + near : 6 + near] += low_ref[:, 4 * q + 2 : 4 * q + 4]


def pack_y_body(
    feat_ref, fwd_ref, back_ref, low_ref, high_ref, up_ref, down_ref, plane_ref, edge_ref, rest_ref
):
    channels, size_x, size_y, depth = feat_ref.shape
    row = lax.broadcasted_iota(jnp.int32, (16, depth), 0)
    tails = [jnp.zeros((16, depth), F32), jnp.zeros((16, depth), F32)]
    for c in range(channels):
        plane_ref[...] = feat_ref[c].astype(F32)
        for n, (out_ref, y) in enumerate(((up_ref, size_y - 1), (down_ref, 0))):
            out_ref[c * size_x : (c + 1) * size_x] = plane_ref[:, y, :].astype(BF16)
            tails[n] = jnp.where(row == 2 * c, low_ref[8 + c, y : y + 1, :], tails[n])
            tails[n] = jnp.where(row == 2 * c + 1, high_ref[8 + c, y : y + 1, :], tails[n])
    first = channels * size_x
    for tail, out_ref in zip(tails, (up_ref, down_ref)):
        out_ref[first : first + 16] = tail.astype(BF16)
    pack_waves(fwd_ref, back_ref, True, up_ref, first + 16, edge_ref, rest_ref)
    pack_waves(fwd_ref, back_ref, False, down_ref, first + 16, edge_ref, rest_ref)


def fill_features(ext_ref, feat_ref, low_ref, high_ref):
    channels, size_x = feat_ref.shape[:2]
    for c in range(channels):
        ext_ref[c, 0] = low_ref[8 + c]
        ext_ref[c, 1 : 1 + size_x] = feat_ref[c].astype(F32)
        ext_ref[c, 1 + size_x] = high_ref[8 + c]


def conv_body(feat_ref, low_ref, high_ref, weight_ref, out_ref, ext_ref):
    channels, size_x = feat_ref.shape[:2]
    fill_features(ext_ref, feat_ref, low_ref, high_ref)

    def one_row(i, carry):
        terms = [[None] * 3 for _ in range(3)]
        for c in range(channels):
            for dx in range(3):
                row = ext_ref[c, i + dx]
                for dy in range(3):
                    for dz in range(3):
                        part = weight_ref[c, 9 * dx + 3 * dy + dz] * row
                        old = terms[dy][dz]
                        terms[dy][dz] = part if old is None else old + part
        total = None
        for dy in range(3):
            part = (
                terms[dy][1]
                + shifted_lanes(terms[dy][0], -1)
                + shifted_lanes(terms[dy][2], 1)
            )
            if dy != 1:
                part = shifted_rows(part, dy - 1)
            total = part if total is None else total + part
        out_ref[i] = total
        return carry

    lax.fori_loop(0, size_x, one_row, 0)


def load_plane(plane_ref, buffer_ref, c, size_x, channels):
    plane_ref[8 : 8 + size_x] = buffer_ref[c * size_x : (c + 1) * size_x].astype(F32)
    tail = buffer_ref[channels * size_x : channels * size_x + 16].astype(F32)
    plane_ref[7:8] = tail[2 * c : 2 * c + 1]
    plane_ref[8 + size_x : 9 + size_x] = tail[2 * c + 1 : 2 * c + 2]


def conv_edge_body(main_ref, low_ref, high_ref, weight_ref, out_ref, plane_ref):
    size_x, size_y, depth = main_ref.shape
    channels = weight_ref.shape[0]
    out_ref[...] = main_ref[...]
    for buffer_ref, dy, y in ((low_ref, 0, 0), (high_ref, 2, size_y - 1)):
        terms = [None] * 3
        for c in range(channels):
            load_plane(plane_ref, buffer_ref, c, size_x, channels)
            for dx in range(3):
                rows = plane_ref[7 + dx : 7 + dx + size_x]
                for dz in range(3):
                    part = weight_ref[c, 9 * dx + 3 * dy + dz] * rows
                    terms[dz] = part if terms[dz] is None else terms[dz] + part
        total = terms[1] + shifted_lanes(terms[0], -1) + shifted_lanes(terms[2], 1)
        out_ref[:, y : y + 1, :] += total.reshape(size_x, 1, depth)


def squash_body(parts_ref, out_ref):
    count = parts_ref.shape[0]
    total = parts_ref[0]
    for n in range(1, count):
        total = total + parts_ref[n]
    squashed = jax.nn.sigmoid(total)
    for n in range(count):
        out_ref[n] = squashed


def update_body(parts_ref, damping_ref, out_ref):
    count, rows = parts_ref.shape[:2]
    half = rows // 2
    total = parts_ref[0]
    for n in range(1, count):
        total = total + parts_ref[n]
    update = total[:half] / (total[half:] + damping_ref[0])
    for n in range(count):
        out_ref[n] = update


def receiver_hits(receivers_ref, place_ref, plane_y, size_x, size_y):
    shift_y = plane_y.bit_length() - 1
    receivers = receivers_ref[...]
    place_x = lax.shift_right_logical(receivers, shift_y) - place_ref[0]
    place_y = (receivers & (plane_y - 1)) - place_ref[1]
    inside = (place_x >= 0) & (place_x < size_x) & (place_y >= 0) & (place_y < size_y)
    cell = jnp.where(inside, place_x * size_y + place_y, -1)
    cells = lax.broadcasted_iota(jnp.int32, (size_x * size_y, receivers.shape[1]), 0)
    return (cells == cell).astype(F32).astype(BF16)


def exact_product(parts, other, contract, parts_first):
    total = None
    for part in parts:
        pair = (part, other) if parts_first else (other, part)
        product = lax.dot_general(
            *pair, (contract, ((), ())), preferred_element_type=F32
        )
        total = product if total is None else total + product
    return total


def sample(fwd_ref, hit, trace_ref):
    size_x, size_y, depth = fwd_ref.shape
    field = fwd_ref[...].reshape(size_x * size_y, depth)
    total = exact_product(split3(field), hit, ((0,), (0,)), True)
    trace_ref[...] = total[RDEPTH : RDEPTH + 1, :]


def trace_body(plane_y, fwd_ref, place_ref, receivers_ref, trace_ref):
    size_x, size_y, _ = fwd_ref.shape
    sample(fwd_ref, receiver_hits(receivers_ref, place_ref, plane_y, size_x, size_y), trace_ref)


def inner_body(moment, plane_y, *refs):
    fwd_ref, back_ref, fwd_old_ref, back_old_ref = refs[:4]
    place_ref, receivers_ref, residual_ref = refs[4:7]
    refs = refs[7:]
    if moment == 0:
        x_low_ref, x_high_ref = refs[:2]
        refs = refs[2:]
    fwd_ahead_ref, back_ahead_ref, lap_fwd_ref, lap_back_ref = refs[:4]
    refs = refs[4:]
    if moment == 1:
        trace_ref = refs[0]
        refs = refs[1:]
    x_ref, y_ref, inject_ref = refs
    size_x, size_y, depth = fwd_ref.shape
    rows = 4
    hit = receiver_hits(receivers_ref, place_ref, plane_y, size_x, size_y)
    injected = jnp.where(
        lax.broadcasted_iota(jnp.int32, (depth, hit.shape[1]), 0) == RDEPTH,
        residual_ref[0, moment : moment + 1, :],
        0.0,
    )
    inject_ref[...] = exact_product(split3(injected), hit, ((1,), (1,)), False).reshape(
        size_x, size_y, depth
    )
    if moment == 1:
        sample(fwd_ref, hit, trace_ref)
    zero_x = jnp.zeros((4, size_y, depth), F32)
    y_ref[:, 0:8] = jnp.zeros((size_x, 8, depth), F32)
    y_ref[:, 8 + size_y : 16 + size_y] = jnp.zeros((size_x, 8, depth), F32)
    for first, ref, old_ref, ahead_ref, lap_ref in (
        (0, fwd_ref, fwd_old_ref, fwd_ahead_ref, lap_fwd_ref),
        (4, back_ref, back_old_ref, back_ahead_ref, lap_back_ref),
    ):
        x_ref[0:4] = zero_x if moment else x_low_ref[first : first + 4]
        x_ref[4 : 4 + size_x] = ref[...]
        x_ref[4 + size_x : 8 + size_x] = zero_x if moment else x_high_ref[first : first + 4]
        y_ref[:, 8 : 8 + size_y] = ref[...]

        def one_block(i, carry):
            start = i * rows
            here = pl.ds(start, rows)
            centre = ref[here]
            flat = centre.reshape(rows * size_y, depth)
            result = (3.0 * COEFFICIENTS[0]) * centre
            for k in range(1, 5):
                along_x = x_ref[pl.ds(start + 4 + k, rows)] + x_ref[pl.ds(start + 4 - k, rows)]
                along_y = (
                    y_ref[here, 8 + k : 8 + k + size_y, :] + y_ref[here, 8 - k : 8 - k + size_y, :]
                )
                along_z = shifted_lanes(flat, k) + shifted_lanes(flat, -k)
                result = result + COEFFICIENTS[k] * (
                    along_x + along_y + along_z.reshape(centre.shape)
                )
            if first:
                result = result + inject_ref[here]
            lap_ref[here] = result
            ahead_ref[here] = 2.0 * centre - old_ref[here]
            return carry

        lax.fori_loop(0, size_x // rows, one_block, 0)


def step_body(moment, plane_y, *refs):
    fwd_ahead_ref, back_ahead_ref, lap_fwd_ref, lap_back_ref, squashed_ref = refs[:5]
    y_low_ref, y_high_ref, place_ref, wavelet_ref = refs[5:9]
    refs = refs[9:]
    if moment == 0:
        (fwd_new_ref, back_new_ref, lap_ref) = refs[:3]
        (x_up_ref, x_down_ref, y_up_ref, y_down_ref) = refs[3:7]
        refs = refs[7:]
    else:
        x_low_ref, x_high_ref, lap_old_ref, back_ref = refs[:4]
        (fwd_new_ref, back_new_ref, sums_ref) = refs[4:7]
        refs = refs[7:]
    edge_ref, rest_ref, *sides = refs
    size_x, size_y, depth = fwd_ahead_ref.shape
    start_row = y_low_ref.shape[0] - wave_rows(size_x)
    for n, (buffer_ref, upward) in enumerate(((y_low_ref, True), (y_high_ref, False))):
        unpack_waves(buffer_ref, upward, start_row, size_x, edge_ref, rest_ref)
        for m in range(2):
            side_ref = sides[2 * m + n]
            at, empty = (4, 8) if upward else (8, 0)
            side_ref[:, empty : empty + 8] = jnp.zeros((size_x, 8, depth), F32)
            side_ref[:, at : at + 4] = edge_ref[:, 4 * m : 4 * m + 4]

    anchor_x, anchor_y, source = place_ref[0], place_ref[1], place_ref[2]
    shift_y = plane_y.bit_length() - 1
    shift_z = depth.bit_length() - 1
    column = lax.shift_right_logical(source, shift_z)
    source_x = lax.shift_right_logical(column, shift_y) - anchor_x
    source_y = (column & (plane_y - 1)) - anchor_y
    source_z = source & (depth - 1)
    here = (source_x >= 0) & (source_x < size_x) & (source_y >= 0) & (source_y < size_y)
    spot = jnp.where(here, (source_x * size_y + source_y) * depth + source_z, -1)
    amplitude = wavelet_ref[0, moment]

    def edges(lap, m, start):
        block = slice(start, start + 4)
        low = high = None
        for k in range(1, 5):
            a = COEFFICIENTS[k] * sides[2 * m][block, 8 - k : 16 - k, :]
            b = COEFFICIENTS[k] * sides[2 * m + 1][block, k : 8 + k, :]
            low, high = (a, b) if low is None else (low + a, high + b)
        parts = [low, high]
        if size_y > 16:
            parts.insert(1, jnp.zeros((4, size_y - 16, depth), F32))
        lap = lap + jnp.concatenate(parts, axis=1)
        if moment == 0 or start not in (0, size_x - 4):
            return lap
        parts = []
        for j in range(4):
            total = None
            if start == 0:
                picks = [(k, x_low_ref, 4 * m + 4 + j - k) for k in range(j + 1, 5)]
            else:
                picks = [(k, x_high_ref, 4 * m + j + k - 4) for k in range(4 - j, 5)]
            for k, ref, row in picks:
                part = COEFFICIENTS[k] * ref[row]
                total = part if total is None else total + part
            parts.append(total)
        return lap + jnp.stack(parts)

    for start in range(0, size_x, 4):
        here = slice(start, start + 4)
        courant = 0.02 + 0.16 * squashed_ref[here]
        lap_fwd = edges(lap_fwd_ref[here], 0, start)
        lap_back = edges(lap_back_ref[here], 1, start)
        dims = lap_fwd.shape
        index = (
            lax.broadcasted_iota(jnp.int32, dims, 0) * (size_y * depth)
            + lax.broadcasted_iota(jnp.int32, dims, 1) * depth
            + lax.broadcasted_iota(jnp.int32, dims, 2)
        )
        added = jnp.where(index == spot - start * (size_y * depth), amplitude, 0.0)
        fwd_new_ref[here] = fwd_ahead_ref[here] + courant * (lap_fwd + added)
        back_new = back_ahead_ref[here] + courant * lap_back
        back_new_ref[here] = back_new
        if moment == 0:
            lap_ref[here] = lap_fwd
        else:
            rows = sums_ref.shape[1] // 2
            n, at = start // rows, start % rows
            lap_old = lap_old_ref[here]
            sums_ref[n, at : at + 4] = lap_old * back_ref[here] + lap_fwd * back_new
            sums_ref[n, rows + at : rows + at + 4] = lap_old * lap_old + lap_fwd * lap_fwd

    if moment == 0:
        x_up_ref[0:4] = fwd_new_ref[size_x - 4 : size_x]
        x_up_ref[4:8] = back_new_ref[size_x - 4 : size_x]
        x_down_ref[0:4] = fwd_new_ref[0:4]
        x_down_ref[4:8] = back_new_ref[0:4]
        pack_waves(fwd_new_ref, back_new_ref, True, y_up_ref, 0, edge_ref, rest_ref)
        pack_waves(fwd_new_ref, back_new_ref, False, y_down_ref, 0, edge_ref, rest_ref)


def gradient_body(
    update_ref,
    squashed_ref,
    feat_ref,
    x_low_ref,
    x_high_ref,
    y_low_ref,
    y_high_ref,
    first_ref,
    second_ref,
    out_ref,
    ext_ref,
    moved_ref,
    plane_ref,
    rows_ref,
):
    size_x, size_y, depth = update_ref.shape
    channels = feat_ref.shape[0]
    copies = out_ref.shape[0]
    fill_features(ext_ref, feat_ref, x_low_ref, x_high_ref)

    def one_row(i, carry):
        squashed = squashed_ref[i]
        pulled = update_ref[i] * (0.16 * squashed * (1.0 - squashed))
        for dz in range(3):
            along = pulled if dz == 1 else shifted_lanes(pulled, 1 - dz)
            for dy in range(3):
                moved_ref[3 * dy + dz, i] = along if dy == 1 else shifted_rows(along, 1 - dy)
        edge = pulled[0:1, :], pulled[size_y - 1 : size_y, :]
        plane_ref[1, pl.ds(i, 1)] = edge[0]
        plane_ref[2, pl.ds(i, 1)] = edge[1]
        return carry

    lax.fori_loop(0, size_x, one_row, 0)
    rows_ref[...] = jnp.zeros_like(rows_ref)

    for c in range(channels):

        def add_row(i, totals):
            features = [ext_ref[c, i + dx] for dx in range(3)]
            new = []
            for dx in range(3):
                for dy in range(3):
                    for dz in range(3):
                        product = features[dx] * moved_ref[3 * dy + dz, i]
                        folded = product[0:8]
                        for y in range(8, size_y, 8):
                            folded = folded + product[y : y + 8]
                        new.append(totals[9 * dx + 3 * dy + dz] + folded)
            return tuple(new)

        zero = jnp.zeros((8, depth), F32)
        totals = lax.fori_loop(0, size_x, add_row, (zero,) * 27)
        for o in range(27):
            at = c * 27 + o
            rows_ref[at : at + 1] = jnp.sum(totals[o], axis=0, keepdims=True)

    for buffer_ref, dy, which in ((y_low_ref, 0, 1), (y_high_ref, 2, 2)):
        pulled = plane_ref[which, 0:size_x]
        along = [pulled if dz == 1 else shifted_lanes(pulled, 1 - dz) for dz in range(3)]
        for c in range(channels):
            load_plane(plane_ref.at[0], buffer_ref, c, size_x, channels)
            for dx in range(3):
                features = plane_ref[0, 7 + dx : 7 + dx + size_x]
                for dz in range(3):
                    at = c * 27 + 9 * dx + 3 * dy + dz
                    rows_ref[at : at + 1] += jnp.sum(
                        features * along[dz], axis=0, keepdims=True
                    )

    ones = jnp.ones((8, depth), BF16)
    sums = None
    for part in split3(rows_ref[...]):
        product = lax.dot_general(
            ones, part, (((1,), (1,)), ((), ())), preferred_element_type=F32
        )
        sums = product if sums is None else sums + product
    count = first_ref.shape[1]
    for n in range(copies):
        out_ref[n, :, 0:count] = first_ref[...]
        out_ref[n, :, count : 2 * count] = second_ref[...]
        out_ref[n, :, 2 * count : 2 * count + depth] = sums[0:1]


def total_body(shares_ref, trace_ref, grad_ref):
    copies = shares_ref.shape[0]
    count = trace_ref.shape[2]
    channels, offsets = grad_ref.shape
    total = shares_ref[0]
    for n in range(1, copies):
        total = total + shares_ref[n]
    trace_ref[0, 0:1, :] = total[:, 0:count]
    trace_ref[0, 1:2, :] = total[:, count : 2 * count]
    last = total[:, 2 * count :]
    lanes = last.shape[1]
    last = jnp.broadcast_to(last, (8, lanes))
    for c in range(channels):
        turned = last if c == 0 else pltpu.roll(last, lanes - c * offsets, 1)
        grad_ref[c : c + 1, :] = turned[0:1, 0:offsets]


def neighbours(up, down, axis):
    count = lax.axis_size(axis)
    low = lax.ppermute(up, axis, [(i, i + 1) for i in range(count - 1)])
    high = lax.ppermute(down, axis, [(i + 1, i) for i in range(count - 1)])
    return low, high


def per_device(
    features,
    conv_weight,
    fwd_prev,
    fwd_now,
    back_prev,
    back_now,
    sources,
    wavelet,
    receivers,
    residual,
    damping,
):
    channels, size_x, size_y, depth = features.shape
    shots = lax.axis_size("shot")
    rows = size_x // shots
    count = receivers.shape[1]
    plane_y = size_y * lax.axis_size("gy")
    blocks = lax.axis_size("gx") * lax.axis_size("gy")
    grid = (size_x, size_y, depth)
    fwd_prev, fwd_now, back_prev, back_now = (
        a.reshape(grid) for a in (fwd_prev, fwd_now, back_prev, back_now)
    )
    place = jnp.stack(
        [lax.axis_index("gx") * size_x, lax.axis_index("gy") * size_y, sources[0]]
    ).astype(jnp.int32)

    x_shape = shape(8 + channels, size_y, depth)
    with jax.named_scope("pack_x"):
        x_up, x_down = call(
            pack_x_body,
            [x_shape, x_shape],
            (features, fwd_now, back_now),
            [pl.BlockSpec(memory_space=pltpu.HBM)] * 3,
            scratch=[
                pltpu.VMEM((2 * channels, size_y, depth), BF16),
                pltpu.SemaphoreType.DMA((2 * (2 + channels),)),
            ],
            name="pack_x",
        )
    with jax.named_scope("halo_x"):
        x_low, x_high = neighbours(x_up, x_down, "gx")
    packing = [
        pltpu.VMEM((size_x, 8, depth), F32),
        pltpu.VMEM((size_x // 4, 16, depth), F32),
    ]
    y_shape = shape(channels * size_x + 16 + wave_rows(size_x), depth, dtype=BF16)
    with jax.named_scope("pack_y"):
        y_up, y_down = call(
            pack_y_body,
            [y_shape, y_shape],
            (features, fwd_now, back_now, x_low, x_high),
            [VM] * 5,
            scratch=[pltpu.VMEM(grid, F32)] + packing,
            name="pack_y",
        )
    with jax.named_scope("halo_y"):
        y_low, y_high = neighbours(y_up, y_down, "gy")
    ext = pltpu.VMEM((channels, size_x + 2, size_y, depth), F32)
    with jax.named_scope("conv"):
        main = call(
            conv_body,
            [shape(*grid)],
            (features, x_low, x_high, conv_weight),
            [VM, VM, VM, SM],
            scratch=[ext],
            flops=54 * channels * size_x * size_y * depth,
            name="conv",
        )
        part = call(
            conv_edge_body,
            [shape(*grid)],
            (main, y_low, y_high, conv_weight),
            [VM, VM, VM, SM],
            scratch=[pltpu.VMEM((size_x + 16, depth), F32)],
            name="conv_edge",
        )
    with jax.named_scope("squash"):
        parts = lax.all_to_all(part, "shot", 0, 0, tiled=True)
        squashed = call(
            squash_body,
            [shape(shots, rows, size_y, depth)],
            (parts.reshape(shots, rows, size_y, depth),),
            [VM],
            name="squash",
        )
        squashed = lax.all_to_all(squashed.reshape(grid), "shot", 0, 0, tiled=True)

    full = shape(*grid)
    inner_scratch = [
        pltpu.VMEM((size_x + 8, size_y, depth), F32),
        pltpu.VMEM((size_x, size_y + 16, depth), F32),
        pltpu.VMEM(grid, F32),
    ]
    step_scratch = packing + [pltpu.VMEM((size_x, 16, depth), F32)] * 4
    work = 60 * size_x * size_y * depth
    with jax.named_scope("inner_1"):
        fwd_ahead, back_ahead, lap_fwd, lap_back = call(
            functools.partial(inner_body, 0, plane_y),
            [full] * 4,
            (fwd_now, back_now, fwd_prev, back_prev, place, receivers, residual, x_low, x_high),
            [VM] * 4 + [SM] + [VM] * 4,
            scratch=inner_scratch,
            flops=work,
            name="inner_1",
        )
    with jax.named_scope("step_1"):
        fwd_1, back_1, lap_1, x_up, x_down, y_up, y_down = call(
            functools.partial(step_body, 0, plane_y),
            [full] * 3
            + [shape(8, size_y, depth)] * 2
            + [shape(wave_rows(size_x), depth, dtype=BF16)] * 2,
            (
                fwd_ahead,
                back_ahead,
                lap_fwd,
                lap_back,
                squashed,
                y_low,
                y_high,
                place,
                wavelet,
            ),
            [VM] * 7 + [SM] * 2,
            scratch=step_scratch,
            name="step_1",
        )
    with jax.named_scope("halo_2"):
        x_low_2, x_high_2 = neighbours(x_up, x_down, "gx")
        y_low_2, y_high_2 = neighbours(y_up, y_down, "gy")
    with jax.named_scope("inner_2"):
        fwd_ahead, back_ahead, lap_fwd, lap_back, trace_1 = call(
            functools.partial(inner_body, 1, plane_y),
            [full] * 4 + [shape(1, count)],
            (fwd_1, back_1, fwd_now, back_now, place, receivers, residual),
            [VM] * 4 + [SM] + [VM] * 2,
            scratch=inner_scratch,
            flops=work,
            name="inner_2",
        )
    with jax.named_scope("step_2"):
        fwd_2, back_2, sums = call(
            functools.partial(step_body, 1, plane_y),
            [full, full, shape(shots, 2 * rows, size_y, depth)],
            (
                fwd_ahead,
                back_ahead,
                lap_fwd,
                lap_back,
                squashed,
                y_low_2,
                y_high_2,
                place,
                wavelet,
                x_low_2,
                x_high_2,
                lap_1,
                back_1,
            ),
            [VM] * 7 + [SM] * 2 + [VM] * 4,
            scratch=step_scratch,
            name="step_2",
        )
    with jax.named_scope("traces"):
        trace_2 = call(
            functools.partial(trace_body, plane_y),
            [shape(1, count)],
            (fwd_2, place, receivers),
            [VM, SM, VM],
            name="trace_2",
        )
    with jax.named_scope("update"):
        sums = lax.all_to_all(
            sums.reshape(shots * 2 * rows, size_y, depth), "shot", 0, 0, tiled=True
        )
        update = call(
            update_body,
            [shape(shots, rows, size_y, depth)],
            (sums.reshape(shots, 2 * rows, size_y, depth), damping),
            [VM, SM],
            name="update",
        )
        update = lax.all_to_all(update.reshape(grid), "shot", 0, 0, tiled=True)
    with jax.named_scope("gradient"):
        share = call(
            gradient_body,
            [shape(blocks, 1, 2 * count + depth)],
            (update, squashed, features, x_low, x_high, y_low, y_high, trace_1, trace_2),
            [VM] * 9,
            scratch=[
                ext,
                pltpu.VMEM((9,) + grid, F32),
                pltpu.VMEM((3, size_x + 16, depth), F32),
                pltpu.VMEM((128, depth), F32),
            ],
            flops=54 * channels * size_x * size_y * depth,
            name="gradient",
        )
        shares = lax.all_to_all(share, ("gx", "gy"), 0, 0, tiled=True)
        shares = shares.reshape(blocks, 1, 2 * count + depth)
        traces, weight_grad = call(
            total_body,
            [shape(1, 2, count), shape(channels, 27)],
            (shares,),
            [VM],
            name="total",
        )
    return (fwd_2[None], back_2[None], traces, update, weight_grad)


def solution(mesh):
    in_specs = (
        P("shot", "gx", "gy", None),
        P("shot", None),
        P("shot", "gx", "gy", None),
        P("shot", "gx", "gy", None),
        P("shot", "gx", "gy", None),
        P("shot", "gx", "gy", None),
        P("shot"),
        P("shot", None),
        P("shot", None),
        P("shot", None, None),
        P(),
    )
    out_specs = (
        P("shot", "gx", "gy", None),
        P("shot", "gx", "gy", None),
        P("shot", None, None),
        P("gx", "gy", None),
        P("shot", None),
    )
    return jax.shard_map(
        per_device, mesh=mesh, in_specs=in_specs, out_specs=out_specs, check_vma=False
    )
```

```python
import functools

import jax
import jax.numpy as jnp
from jax import lax
from jax.experimental import pallas as pl
from jax.experimental.pallas import tpu as pltpu
from jax.sharding import PartitionSpec as P

RDEPTH = 3
COEFFICIENTS = (-205.0 / 72.0, 8.0 / 5.0, -1.0 / 5.0, 8.0 / 315.0, -1.0 / 560.0)
F32 = jnp.float32
BF16 = jnp.bfloat16
VMEM_LIMIT = 48 * 1024 * 1024
VMEM_WHOLE = 63 * 1024 * 1024

VM = pl.BlockSpec(memory_space=pltpu.VMEM)
SM = pl.BlockSpec(memory_space=pltpu.SMEM)


def call(body, outs, ins, specs, scratch=(), flops=1_000_000, name=None, limit=VMEM_LIMIT):
    moved = sum(a.size * a.dtype.itemsize for a in ins) + sum(
        o.size * jnp.dtype(o.dtype).itemsize for o in outs
    )
    single = len(outs) == 1
    return pl.pallas_call(
        body,
        out_shape=outs[0] if single else tuple(outs),
        in_specs=specs,
        out_specs=VM if single else tuple(VM for _ in outs),
        scratch_shapes=list(scratch),
        compiler_params=pltpu.CompilerParams(vmem_limit_bytes=limit),
        cost_estimate=pl.CostEstimate(flops=flops, bytes_accessed=moved, transcendentals=0),
        name=name,
    )(*ins)


def shape(*dims, dtype=F32):
    return jax.ShapeDtypeStruct(dims, dtype)


def split3(value):
    top = value.astype(BF16)
    rest = value - top.astype(F32)
    middle = rest.astype(BF16)
    low = (rest - middle.astype(F32)).astype(BF16)
    return (top, middle, low)


def shifted_lanes(value, by):
    depth = value.shape[1]
    lane = lax.broadcasted_iota(jnp.int32, value.shape, 1)
    if by > 0:
        return jnp.where(lane < depth - by, pltpu.roll(value, depth - by, 1), 0.0)
    return jnp.where(lane >= -by, pltpu.roll(value, -by, 1), 0.0)


def shifted_rows(value, by):
    count = value.shape[0]
    row = lax.broadcasted_iota(jnp.int32, value.shape, 0)
    if by > 0:
        return jnp.where(row < count - by, pltpu.roll(value, count - by, 0), 0.0)
    return jnp.where(row >= -by, pltpu.roll(value, -by, 0), 0.0)


def pack_x_body(feat_ref, fwd_ref, back_ref, up_ref, down_ref, edge_ref, sems):
    channels, size_x = feat_ref.shape[:2]
    copies = []
    for n, (out_ref, start, row) in enumerate(
        ((up_ref, size_x - 4, size_x - 1), (down_ref, 0, 0))
    ):
        pairs = [
            (fwd_ref.at[pl.ds(start, 4)], out_ref.at[pl.ds(0, 4)]),
            (back_ref.at[pl.ds(start, 4)], out_ref.at[pl.ds(4, 4)]),
        ]
        for c in range(channels):
            pairs.append((feat_ref.at[c, row], edge_ref.at[n * channels + c]))
        for m, (source, target) in enumerate(pairs):
            copies.append(
                pltpu.make_async_copy(source, target, sems.at[n * (2 + channels) + m])
            )
    for copy in copies:
        copy.start()
    for copy in copies:
        copy.wait()
    for c in range(channels):
        up_ref[8 + c] = edge_ref[c].astype(F32)
        down_ref[8 + c] = edge_ref[channels + c].astype(F32)


def wave_rows(size_x):
    return size_x * 12


def pack_waves(fwd_ref, back_ref, upward, out_ref, first, edge_ref, low_ref):
    size_x, size_y, depth = fwd_ref.shape
    start, near = (size_y - 4, 2) if upward else (0, 0)
    edge_ref[:, 0:4] = fwd_ref[:, start : start + 4]
    edge_ref[:, 4:8] = back_ref[:, start : start + 4]
    value = edge_ref[...].reshape(size_x * 8, depth)
    high = value.astype(BF16)
    out_ref[first : first + size_x * 8] = high
    edge_ref[...] = (value - high.astype(F32)).reshape(size_x, 8, depth)
    quarter = size_x // 4
    for q in range(4):
        part = slice(q * quarter, (q + 1) * quarter)
        low_ref[:, 4 * q : 4 * q + 2] = edge_ref[part, near : near + 2]
        low_ref[:, 4 * q + 2 : 4 * q + 4] = edge_ref[part, 4 + near : 6 + near]
    out_ref[first + size_x * 8 : first + size_x * 12] = (
        low_ref[...].reshape(size_x * 4, depth).astype(BF16)
    )


def unpack_waves(buffer_ref, upward, first, size_x, edge_ref, low_ref):
    depth = buffer_ref.shape[1]
    near = 2 if upward else 0
    quarter = size_x // 4
    edge_ref[...] = (
        buffer_ref[first : first + size_x * 8].astype(F32).reshape(size_x, 8, depth)
    )
    low_ref[...] = (
        buffer_ref[first + size_x * 8 : first + size_x * 12]
        .astype(F32)
        .reshape(quarter, 16, depth)
    )
    for q in range(4):
        part = slice(q * quarter, (q + 1) * quarter)
        edge_ref[part, near : near + 2] += low_ref[:, 4 * q : 4 * q + 2]
        edge_ref[part, 4 + near : 6 + near] += low_ref[:, 4 * q + 2 : 4 * q + 4]


def pack_y_body(
    feat_ref, fwd_ref, back_ref, low_ref, high_ref, up_ref, down_ref, plane_ref, edge_ref, rest_ref
):
    channels, size_x, size_y, depth = feat_ref.shape
    row = lax.broadcasted_iota(jnp.int32, (16, depth), 0)
    tails = [jnp.zeros((16, depth), F32), jnp.zeros((16, depth), F32)]
    for c in range(channels):
        plane_ref[...] = feat_ref[c].astype(F32)
        for n, (out_ref, y) in enumerate(((up_ref, size_y - 1), (down_ref, 0))):
            out_ref[c * size_x : (c + 1) * size_x] = plane_ref[:, y, :].astype(BF16)
            tails[n] = jnp.where(row == 2 * c, low_ref[8 + c, y : y + 1, :], tails[n])
            tails[n] = jnp.where(row == 2 * c + 1, high_ref[8 + c, y : y + 1, :], tails[n])
    first = channels * size_x
    for tail, out_ref in zip(tails, (up_ref, down_ref)):
        out_ref[first : first + 16] = tail.astype(BF16)
    pack_waves(fwd_ref, back_ref, True, up_ref, first + 16, edge_ref, rest_ref)
    pack_waves(fwd_ref, back_ref, False, down_ref, first + 16, edge_ref, rest_ref)


def fill_features(ext_ref, feat_ref, low_ref, high_ref):
    channels, size_x = feat_ref.shape[:2]
    for c in range(channels):
        ext_ref[c, 0] = low_ref[8 + c]
        ext_ref[c, 1 : 1 + size_x] = feat_ref[c].astype(F32)
        ext_ref[c, 1 + size_x] = high_ref[8 + c]


def conv_body(feat_ref, low_ref, high_ref, weight_ref, *refs):
    small_in, (out_ref, *small_out), ext_ref = refs[:3], refs[3:7], refs[7]
    for source, target in zip(small_in, small_out):
        target[...] = source[...]
    channels, size_x = feat_ref.shape[:2]
    fill_features(ext_ref, feat_ref, low_ref, high_ref)

    def one_row(i, carry):
        terms = [[None] * 3 for _ in range(3)]
        for c in range(channels):
            for dx in range(3):
                row = ext_ref[c, i + dx]
                for dy in range(3):
                    for dz in range(3):
                        part = weight_ref[c, 9 * dx + 3 * dy + dz] * row
                        old = terms[dy][dz]
                        terms[dy][dz] = part if old is None else old + part
        total = None
        for dy in range(3):
            part = (
                terms[dy][1]
                + shifted_lanes(terms[dy][0], -1)
                + shifted_lanes(terms[dy][2], 1)
            )
            if dy != 1:
                part = shifted_rows(part, dy - 1)
            total = part if total is None else total + part
        out_ref[i] = total
        return carry

    lax.fori_loop(0, size_x, one_row, 0)


def load_plane(plane_ref, buffer_ref, c, size_x, channels):
    plane_ref[8 : 8 + size_x] = buffer_ref[c * size_x : (c + 1) * size_x].astype(F32)
    tail = buffer_ref[channels * size_x : channels * size_x + 16].astype(F32)
    plane_ref[7:8] = tail[2 * c : 2 * c + 1]
    plane_ref[8 + size_x : 9 + size_x] = tail[2 * c + 1 : 2 * c + 2]


def conv_edge_body(
    main_ref, low_ref, high_ref, weight_ref, place_ref, keep_ref, give_ref, total_ref, plane_ref
):
    size_x, size_y, depth = main_ref.shape
    channels = weight_ref.shape[0]
    total_ref[...] = main_ref[...]
    for buffer_ref, dy, y in ((low_ref, 0, 0), (high_ref, 2, size_y - 1)):
        terms = [None] * 3
        for c in range(channels):
            load_plane(plane_ref, buffer_ref, c, size_x, channels)
            for dx in range(3):
                rows = plane_ref[7 + dx : 7 + dx + size_x]
                for dz in range(3):
                    part = weight_ref[c, 9 * dx + 3 * dy + dz] * rows
                    terms[dz] = part if terms[dz] is None else terms[dz] + part
        total = terms[1] + shifted_lanes(terms[0], -1) + shifted_lanes(terms[2], 1)
        total_ref[:, y : y + 1, :] += total.reshape(size_x, 1, depth)
    half = size_x // 2
    core = place_ref[3]
    keep_ref[...] = total_ref[pl.ds(core * half, half)]
    give_ref[...] = total_ref[pl.ds((1 - core) * half, half)]


def pair_body(keep_ref, got_ref, out_ref):
    total = keep_ref[...] + got_ref[...]
    for n in range(out_ref.shape[0]):
        out_ref[n] = total


def squash_body(parts_ref, out_ref):
    total = parts_ref[0]
    for n in range(1, parts_ref.shape[0]):
        total = total + parts_ref[n]
    out_ref[...] = jax.nn.sigmoid(total)


def update_body(parts_ref, damping_ref, out_ref):
    count, rows = parts_ref.shape[:2]
    half = rows // 2
    total = parts_ref[0]
    for n in range(1, count):
        total = total + parts_ref[n]
    update = total[:half] / (total[half:] + damping_ref[0])
    for n in range(count):
        out_ref[n] = update


def receiver_hits(receivers_ref, place_ref, plane_y, size_x, size_y):
    shift_y = plane_y.bit_length() - 1
    receivers = receivers_ref[...]
    place_x = lax.shift_right_logical(receivers, shift_y) - place_ref[0]
    place_y = (receivers & (plane_y - 1)) - place_ref[1]
    inside = (place_x >= 0) & (place_x < size_x) & (place_y >= 0) & (place_y < size_y)
    cell = jnp.where(inside, place_x * size_y + place_y, -1)
    cells = lax.broadcasted_iota(jnp.int32, (size_x * size_y, receivers.shape[1]), 0)
    return (cells == cell).astype(F32).astype(BF16)


def exact_product(parts, other, contract, parts_first):
    total = None
    for part in parts:
        pair = (part, other) if parts_first else (other, part)
        product = lax.dot_general(
            *pair, (contract, ((), ())), preferred_element_type=F32
        )
        total = product if total is None else total + product
    return total


def sample(fwd_ref, hit, trace_ref):
    size_x, size_y, depth = fwd_ref.shape
    field = fwd_ref[...].reshape(size_x * size_y, depth)
    total = exact_product(split3(field), hit, ((0,), (0,)), True)
    trace_ref[...] = total[RDEPTH : RDEPTH + 1, :]


def trace_body(plane_y, fwd_ref, place_ref, receivers_ref, trace_ref):
    size_x, size_y, _ = fwd_ref.shape
    sample(fwd_ref, receiver_hits(receivers_ref, place_ref, plane_y, size_x, size_y), trace_ref)


def inner_body(moment, plane_y, *refs):
    fwd_ref, back_ref, fwd_old_ref, back_old_ref = refs[:4]
    place_ref, receivers_ref, residual_ref = refs[4:7]
    refs = refs[7:]
    if moment == 0:
        x_low_ref, x_high_ref = refs[:2]
        refs = refs[2:]
    fwd_ahead_ref, back_ahead_ref, lap_fwd_ref, lap_back_ref = refs[:4]
    refs = refs[4:]
    if moment == 1:
        trace_ref = refs[0]
        refs = refs[1:]
    x_ref, y_ref, inject_ref = refs
    size_x, size_y, depth = fwd_ref.shape
    rows = 4
    hit = receiver_hits(receivers_ref, place_ref, plane_y, size_x, size_y)
    injected = jnp.where(
        lax.broadcasted_iota(jnp.int32, (depth, hit.shape[1]), 0) == RDEPTH,
        residual_ref[0, moment : moment + 1, :],
        0.0,
    )
    inject_ref[...] = exact_product(split3(injected), hit, ((1,), (1,)), False).reshape(
        size_x, size_y, depth
    )
    if moment == 1:
        sample(fwd_ref, hit, trace_ref)
    zero_x = jnp.zeros((4, size_y, depth), F32)
    y_ref[:, 0:8] = jnp.zeros((size_x, 8, depth), F32)
    y_ref[:, 8 + size_y : 16 + size_y] = jnp.zeros((size_x, 8, depth), F32)
    for first, ref, old_ref, ahead_ref, lap_ref in (
        (0, fwd_ref, fwd_old_ref, fwd_ahead_ref, lap_fwd_ref),
        (4, back_ref, back_old_ref, back_ahead_ref, lap_back_ref),
    ):
        x_ref[0:4] = zero_x if moment else x_low_ref[first : first + 4]
        x_ref[4 : 4 + size_x] = ref[...]
        x_ref[4 + size_x : 8 + size_x] = zero_x if moment else x_high_ref[first : first + 4]
        y_ref[:, 8 : 8 + size_y] = ref[...]

        def one_block(i, carry):
            start = i * rows
            here = pl.ds(start, rows)
            centre = ref[here]
            flat = centre.reshape(rows * size_y, depth)
            result = (3.0 * COEFFICIENTS[0]) * centre
            for k in range(1, 5):
                along_x = x_ref[pl.ds(start + 4 + k, rows)] + x_ref[pl.ds(start + 4 - k, rows)]
                along_y = (
                    y_ref[here, 8 + k : 8 + k + size_y, :] + y_ref[here, 8 - k : 8 - k + size_y, :]
                )
                along_z = shifted_lanes(flat, k) + shifted_lanes(flat, -k)
                result = result + COEFFICIENTS[k] * (
                    along_x + along_y + along_z.reshape(centre.shape)
                )
            if first:
                result = result + inject_ref[here]
            lap_ref[here] = result
            ahead_ref[here] = 2.0 * centre - old_ref[here]
            return carry

        lax.fori_loop(0, size_x // rows, one_block, 0)


def step_body(moment, plane_y, *refs):
    fwd_ahead_ref, back_ahead_ref, lap_fwd_ref, lap_back_ref = refs[:4]
    y_low_ref, y_high_ref, place_ref, wavelet_ref = refs[4:8]
    refs = refs[8:]
    if moment == 0:
        own_ref, other_ref = refs[:2]
        (fwd_new_ref, back_new_ref, lap_ref, squashed_ref) = refs[2:6]
        (x_up_ref, x_down_ref, y_up_ref, y_down_ref) = refs[6:10]
        refs = refs[10:]
        half = own_ref.shape[0]
        core = place_ref[3]
        squashed_ref[pl.ds(core * half, half)] = own_ref[...]
        squashed_ref[pl.ds((1 - core) * half, half)] = other_ref[...]
    else:
        squashed_ref, x_low_ref, x_high_ref, lap_old_ref, back_ref = refs[:5]
        (fwd_new_ref, back_new_ref, sums_ref) = refs[5:8]
        refs = refs[8:]
    edge_ref, rest_ref, *sides = refs
    size_x, size_y, depth = fwd_ahead_ref.shape
    start_row = y_low_ref.shape[0] - wave_rows(size_x)
    for n, (buffer_ref, upward) in enumerate(((y_low_ref, True), (y_high_ref, False))):
        unpack_waves(buffer_ref, upward, start_row, size_x, edge_ref, rest_ref)
        for m in range(2):
            side_ref = sides[2 * m + n]
            at, empty = (4, 8) if upward else (8, 0)
            side_ref[:, empty : empty + 8] = jnp.zeros((size_x, 8, depth), F32)
            side_ref[:, at : at + 4] = edge_ref[:, 4 * m : 4 * m + 4]

    anchor_x, anchor_y, source = place_ref[0], place_ref[1], place_ref[2]
    shift_y = plane_y.bit_length() - 1
    shift_z = depth.bit_length() - 1
    column = lax.shift_right_logical(source, shift_z)
    source_x = lax.shift_right_logical(column, shift_y) - anchor_x
    source_y = (column & (plane_y - 1)) - anchor_y
    source_z = source & (depth - 1)
    here = (source_x >= 0) & (source_x < size_x) & (source_y >= 0) & (source_y < size_y)
    spot = jnp.where(here, (source_x * size_y + source_y) * depth + source_z, -1)
    amplitude = wavelet_ref[0, moment]

    def edges(lap, m, start):
        block = slice(start, start + 4)
        low = high = None
        for k in range(1, 5):
            a = COEFFICIENTS[k] * sides[2 * m][block, 8 - k : 16 - k, :]
            b = COEFFICIENTS[k] * sides[2 * m + 1][block, k : 8 + k, :]
            low, high = (a, b) if low is None else (low + a, high + b)
        parts = [low, high]
        if size_y > 16:
            parts.insert(1, jnp.zeros((4, size_y - 16, depth), F32))
        lap = lap + jnp.concatenate(parts, axis=1)
        if moment == 0 or start not in (0, size_x - 4):
            return lap
        parts = []
        for j in range(4):
            total = None
            if start == 0:
                picks = [(k, x_low_ref, 4 * m + 4 + j - k) for k in range(j + 1, 5)]
            else:
                picks = [(k, x_high_ref, 4 * m + j + k - 4) for k in range(4 - j, 5)]
            for k, ref, row in picks:
                part = COEFFICIENTS[k] * ref[row]
                total = part if total is None else total + part
            parts.append(total)
        return lap + jnp.stack(parts)

    for start in range(0, size_x, 4):
        here = slice(start, start + 4)
        courant = 0.02 + 0.16 * squashed_ref[here]
        lap_fwd = edges(lap_fwd_ref[here], 0, start)
        lap_back = edges(lap_back_ref[here], 1, start)
        dims = lap_fwd.shape
        index = (
            lax.broadcasted_iota(jnp.int32, dims, 0) * (size_y * depth)
            + lax.broadcasted_iota(jnp.int32, dims, 1) * depth
            + lax.broadcasted_iota(jnp.int32, dims, 2)
        )
        added = jnp.where(index == spot - start * (size_y * depth), amplitude, 0.0)
        fwd_new_ref[here] = fwd_ahead_ref[here] + courant * (lap_fwd + added)
        back_new = back_ahead_ref[here] + courant * lap_back
        back_new_ref[here] = back_new
        if moment == 0:
            lap_ref[here] = lap_fwd
        else:
            rows = sums_ref.shape[1] // 2
            n, at = start // rows, start % rows
            lap_old = lap_old_ref[here]
            sums_ref[n, at : at + 4] = lap_old * back_ref[here] + lap_fwd * back_new
            sums_ref[n, rows + at : rows + at + 4] = lap_old * lap_old + lap_fwd * lap_fwd

    if moment == 0:
        x_up_ref[0:4] = fwd_new_ref[size_x - 4 : size_x]
        x_up_ref[4:8] = back_new_ref[size_x - 4 : size_x]
        x_down_ref[0:4] = fwd_new_ref[0:4]
        x_down_ref[4:8] = back_new_ref[0:4]
        pack_waves(fwd_new_ref, back_new_ref, True, y_up_ref, 0, edge_ref, rest_ref)
        pack_waves(fwd_new_ref, back_new_ref, False, y_down_ref, 0, edge_ref, rest_ref)


def gradient_body(
    update_ref,
    squashed_ref,
    feat_ref,
    x_low_ref,
    x_high_ref,
    y_low_ref,
    y_high_ref,
    first_ref,
    second_ref,
    out_ref,
    left_ref,
    right_ref,
    plane_ref,
    rows_ref,
):
    size_x, size_y, depth = update_ref.shape
    channels = feat_ref.shape[0]
    copies = out_ref.shape[0]
    cells = size_x * size_y

    def one_block(i, carry):
        for j in range(4):
            x = 4 * i + j
            squashed = squashed_ref[x]
            pulled = update_ref[x] * (0.16 * squashed * (1.0 - squashed))
            for dy in range(3):
                moved = pulled if dy == 1 else shifted_rows(pulled, 1 - dy)
                high = moved.astype(BF16)
                left_ref[2 * dy, x] = high
                left_ref[2 * dy + 1, x] = (moved - high.astype(F32)).astype(BF16)
            plane_ref[1, pl.ds(x, 1)] = pulled[0:1, :]
            plane_ref[2, pl.ds(x, 1)] = pulled[size_y - 1 : size_y, :]
        return carry

    lax.fori_loop(0, size_x // 4, one_block, 0)
    for c in range(channels):
        right_ref[0, 0] = x_low_ref[8 + c].astype(BF16)
        right_ref[0, 1:size_x] = feat_ref[c, 0 : size_x - 1]
        right_ref[1] = feat_ref[c]
        right_ref[2, 0 : size_x - 1] = feat_ref[c, 1:size_x]
        right_ref[2, size_x - 1] = x_high_ref[8 + c].astype(BF16)
        right = jnp.concatenate(
            [right_ref[dx].reshape(cells, depth) for dx in range(3)], axis=1
        )
        for dy in range(3):
            left = jnp.concatenate(
                [left_ref[2 * dy + part].reshape(cells, depth) for part in range(2)], axis=1
            )
            product = lax.dot_general(
                left, right, (((0,), (0,)), ((), ())), preferred_element_type=F32
            )
            ahead = lax.broadcasted_iota(jnp.int32, (depth, depth), 1) - (
                lax.broadcasted_iota(jnp.int32, (depth, depth), 0)
            )
            for dx in range(3):
                lanes = slice(dx * depth, (dx + 1) * depth)
                block = product[0:depth, lanes] + product[depth : 2 * depth, lanes]
                for dz in range(3):
                    at = c * 27 + 9 * dx + 3 * dy + dz
                    rows_ref[at : at + 1] = jnp.sum(
                        jnp.where(ahead == dz - 1, block, 0.0), axis=0, keepdims=True
                    )
    at = channels * 27
    rows_ref[at:] = jnp.zeros((rows_ref.shape[0] - at, depth), F32)

    for buffer_ref, dy, which in ((y_low_ref, 0, 1), (y_high_ref, 2, 2)):
        pulled = plane_ref[which, 0:size_x]
        along = [pulled if dz == 1 else shifted_lanes(pulled, 1 - dz) for dz in range(3)]
        for c in range(channels):
            load_plane(plane_ref.at[0], buffer_ref, c, size_x, channels)
            for dx in range(3):
                features = plane_ref[0, 7 + dx : 7 + dx + size_x]
                for dz in range(3):
                    at = c * 27 + 9 * dx + 3 * dy + dz
                    rows_ref[at : at + 1] += jnp.sum(
                        features * along[dz], axis=0, keepdims=True
                    )

    ones = jnp.ones((8, depth), BF16)
    sums = None
    for part in split3(rows_ref[...]):
        product = lax.dot_general(
            ones, part, (((1,), (1,)), ((), ())), preferred_element_type=F32
        )
        sums = product if sums is None else sums + product
    count = first_ref.shape[1]
    for n in range(copies):
        out_ref[n, :, 0:count] = first_ref[...]
        out_ref[n, :, count : 2 * count] = second_ref[...]
        out_ref[n, :, 2 * count : 2 * count + depth] = sums[0:1]


def total_body(shares_ref, trace_ref, grad_ref):
    copies = shares_ref.shape[0]
    count = trace_ref.shape[2]
    channels, offsets = grad_ref.shape
    total = shares_ref[0]
    for n in range(1, copies):
        total = total + shares_ref[n]
    trace_ref[0, 0:1, :] = total[:, 0:count]
    trace_ref[0, 1:2, :] = total[:, count : 2 * count]
    last = total[:, 2 * count :]
    lanes = last.shape[1]
    last = jnp.broadcast_to(last, (8, lanes))
    for c in range(channels):
        turned = last if c == 0 else pltpu.roll(last, lanes - c * offsets, 1)
        grad_ref[c : c + 1, :] = turned[0:1, 0:offsets]


def keep_body(value_ref, out_ref):
    out_ref[...] = value_ref[...]


def neighbours(up, down, axis):
    count = lax.axis_size(axis)
    low = lax.ppermute(up, axis, [(i, i + 1) for i in range(count - 1)])
    high = lax.ppermute(down, axis, [(i + 1, i) for i in range(count - 1)])
    return low, high


def per_device(
    features,
    conv_weight,
    fwd_prev,
    fwd_now,
    back_prev,
    back_now,
    sources,
    wavelet,
    receivers,
    residual,
    damping,
):
    channels, size_x, size_y, depth = features.shape
    shots = lax.axis_size("shot")
    rows = size_x // shots
    count = receivers.shape[1]
    plane_y = size_y * lax.axis_size("gy")
    blocks = lax.axis_size("gx") * lax.axis_size("gy")
    grid = (size_x, size_y, depth)
    fwd_prev, fwd_now, back_prev, back_now = (
        a.reshape(grid) for a in (fwd_prev, fwd_now, back_prev, back_now)
    )
    place = jnp.stack(
        [
            lax.axis_index("gx") * size_x,
            lax.axis_index("gy") * size_y,
            sources[0],
            lax.axis_index("shot") % 2,
        ]
    ).astype(jnp.int32)

    x_shape = shape(8 + channels, size_y, depth)
    with jax.named_scope("pack_x"):
        x_up, x_down = call(
            pack_x_body,
            [x_shape, x_shape],
            (features, fwd_now, back_now),
            [pl.BlockSpec(memory_space=pltpu.HBM)] * 3,
            scratch=[
                pltpu.VMEM((2 * channels, size_y, depth), BF16),
                pltpu.SemaphoreType.DMA((2 * (2 + channels),)),
            ],
            name="pack_x",
            limit=VMEM_WHOLE,
        )
    with jax.named_scope("halo_x"):
        x_low, x_high = neighbours(x_up, x_down, "gx")
    packing = [
        pltpu.VMEM((size_x, 8, depth), F32),
        pltpu.VMEM((size_x // 4, 16, depth), F32),
    ]
    y_shape = shape(channels * size_x + 16 + wave_rows(size_x), depth, dtype=BF16)
    with jax.named_scope("pack_y"):
        y_up, y_down = call(
            pack_y_body,
            [y_shape, y_shape],
            (features, fwd_now, back_now, x_low, x_high),
            [VM] * 5,
            scratch=[pltpu.VMEM(grid, F32)] + packing,
            name="pack_y",
        )
    with jax.named_scope("halo_y"):
        y_low, y_high = neighbours(y_up, y_down, "gy")
    ext = pltpu.VMEM((channels, size_x + 2, size_y, depth), F32)
    full = shape(*grid)
    inner_scratch = [
        pltpu.VMEM((size_x + 8, size_y, depth), F32),
        pltpu.VMEM((size_x, size_y + 16, depth), F32),
        pltpu.VMEM(grid, F32),
    ]
    step_scratch = packing + [pltpu.VMEM((size_x, 16, depth), F32)] * 4
    work = 60 * size_x * size_y * depth
    with jax.named_scope("inner_1"):
        inner_1 = call(
            functools.partial(inner_body, 0, plane_y),
            [full] * 4,
            (fwd_now, back_now, fwd_prev, back_prev, place, receivers, residual, x_low, x_high),
            [VM] * 4 + [SM] + [VM] * 4,
            scratch=inner_scratch,
            flops=work,
            name="inner_1",
        )
    half = size_x // 2
    chips = shots // 2
    half_shape = shape(half, size_y, depth)
    with jax.named_scope("conv"):
        small = (receivers, residual, wavelet)
        main, receivers, residual, wavelet = call(
            conv_body,
            [shape(*grid)] + [shape(*a.shape, dtype=a.dtype) for a in small],
            (features, x_low, x_high, conv_weight) + small,
            [VM, VM, VM, SM] + [VM] * 3,
            scratch=[ext],
            flops=54 * channels * size_x * size_y * depth,
            name="conv",
        )
        main, *inner_1 = lax.optimization_barrier((main, *inner_1))
        keep, give = call(
            conv_edge_body,
            [half_shape] * 2,
            (main, y_low, y_high, conv_weight, place),
            [VM, VM, VM, SM, SM],
            scratch=[pltpu.VMEM(grid, F32), pltpu.VMEM((size_x + 16, depth), F32)],
            name="conv_edge",
        )
    partner = [(i, i ^ 1) for i in range(shots)]
    with jax.named_scope("squash"):
        pair = call(
            pair_body,
            [shape(chips, half, size_y, depth)],
            (keep, lax.ppermute(give, "shot", partner)),
            [VM, VM],
            name="pair",
        )
        if chips > 1:
            groups = [list(range(core, shots, 2)) for core in range(2)]
            pair = lax.all_to_all(
                pair.reshape(chips * half, size_y, depth),
                "shot",
                0,
                0,
                tiled=True,
                axis_index_groups=groups,
            )
        own = call(
            squash_body,
            [half_shape],
            (pair.reshape(chips, half, size_y, depth),),
            [VM],
            name="squash",
        )
        other = lax.ppermute(own, "shot", partner)

    with jax.named_scope("step_1"):
        fwd_1, back_1, lap_1, squashed, x_up, x_down, y_up, y_down = call(
            functools.partial(step_body, 0, plane_y),
            [full] * 4
            + [shape(8, size_y, depth)] * 2
            + [shape(wave_rows(size_x), depth, dtype=BF16)] * 2,
            (
                *inner_1,
                y_low,
                y_high,
                place,
                wavelet,
                own,
                other,
            ),
            [VM] * 6 + [SM] * 2 + [VM] * 2,
            scratch=step_scratch,
            name="step_1",
        )
    with jax.named_scope("halo_2"):
        x_low_2, x_high_2 = neighbours(x_up, x_down, "gx")
        y_low_2, y_high_2 = neighbours(y_up, y_down, "gy")
    with jax.named_scope("inner_2"):
        fwd_ahead, back_ahead, lap_fwd, lap_back, trace_1 = call(
            functools.partial(inner_body, 1, plane_y),
            [full] * 4 + [shape(1, count)],
            (fwd_1, back_1, fwd_now, back_now, place, receivers, residual),
            [VM] * 4 + [SM] + [VM] * 2,
            scratch=inner_scratch,
            flops=work,
            name="inner_2",
        )
    with jax.named_scope("step_2"):
        fwd_2, back_2, sums = call(
            functools.partial(step_body, 1, plane_y),
            [full, full, shape(shots, 2 * rows, size_y, depth)],
            (
                fwd_ahead,
                back_ahead,
                lap_fwd,
                lap_back,
                y_low_2,
                y_high_2,
                place,
                wavelet,
                squashed,
                x_low_2,
                x_high_2,
                lap_1,
                back_1,
            ),
            [VM] * 6 + [SM] * 2 + [VM] * 5,
            scratch=step_scratch,
            name="step_2",
        )
    with jax.named_scope("traces"):
        trace_2 = call(
            functools.partial(trace_body, plane_y),
            [shape(1, count)],
            (fwd_2, place, receivers),
            [VM, SM, VM],
            name="trace_2",
        )
    with jax.named_scope("update"):
        sums = lax.all_to_all(
            sums.reshape(shots * 2 * rows, size_y, depth), "shot", 0, 0, tiled=True
        )
        update = call(
            update_body,
            [shape(shots, rows, size_y, depth)],
            (sums.reshape(shots, 2 * rows, size_y, depth), damping),
            [VM, SM],
            name="update",
        )
        update = lax.all_to_all(update.reshape(grid), "shot", 0, 0, tiled=True)
    with jax.named_scope("gradient"):
        share = call(
            gradient_body,
            [shape(blocks, 1, 2 * count + depth)],
            (update, squashed, features, x_low, x_high, y_low, y_high, trace_1, trace_2),
            [VM] * 9,
            scratch=[
                pltpu.VMEM((6,) + grid, BF16),
                pltpu.VMEM((3,) + grid, BF16),
                pltpu.VMEM((3, size_x + 16, depth), F32),
                pltpu.VMEM((128, depth), F32),
            ],
            flops=54 * channels * size_x * size_y * depth,
            name="gradient",
        )
        share, update = lax.optimization_barrier((share, update))
        shares = lax.all_to_all(share, ("gx", "gy"), 0, 0, tiled=True)
        shares = shares.reshape(blocks, 1, 2 * count + depth)
        traces, weight_grad = call(
            total_body,
            [shape(1, 2, count), shape(channels, 27)],
            (shares,),
            [VM],
            name="total",
        )
        update = call(keep_body, [full], (update,), [VM], name="keep")
    return (fwd_2[None], back_2[None], traces, update, weight_grad)


def solution(mesh):
    in_specs = (
        P("shot", "gx", "gy", None),
        P("shot", None),
        P("shot", "gx", "gy", None),
        P("shot", "gx", "gy", None),
        P("shot", "gx", "gy", None),
        P("shot", "gx", "gy", None),
        P("shot"),
        P("shot", None),
        P("shot", None),
        P("shot", None, None),
        P(),
    )
    out_specs = (
        P("shot", "gx", "gy", None),
        P("shot", "gx", "gy", None),
        P("shot", None, None),
        P("gx", "gy", None),
        P("shot", None),
    )
    return jax.shard_map(
        per_device, mesh=mesh, in_specs=in_specs, out_specs=out_specs, check_vma=False
    )
```

```python
import functools

import jax
import jax.numpy as jnp
from jax import lax
from jax.experimental import pallas as pl
from jax.experimental.pallas import tpu as pltpu
from jax.sharding import PartitionSpec as P

RDEPTH = 3
COEFFICIENTS = (-205.0 / 72.0, 8.0 / 5.0, -1.0 / 5.0, 8.0 / 315.0, -1.0 / 560.0)
F32 = jnp.float32
BF16 = jnp.bfloat16
VMEM_LIMIT = 48 * 1024 * 1024
VMEM_WHOLE = 63 * 1024 * 1024

VM = pl.BlockSpec(memory_space=pltpu.VMEM)
SM = pl.BlockSpec(memory_space=pltpu.SMEM)


def call(body, outs, ins, specs, scratch=(), flops=1_000_000, name=None, limit=VMEM_LIMIT):
    moved = sum(a.size * a.dtype.itemsize for a in ins) + sum(
        o.size * jnp.dtype(o.dtype).itemsize for o in outs
    )
    single = len(outs) == 1
    return pl.pallas_call(
        body,
        out_shape=outs[0] if single else tuple(outs),
        in_specs=specs,
        out_specs=VM if single else tuple(VM for _ in outs),
        scratch_shapes=list(scratch),
        compiler_params=pltpu.CompilerParams(vmem_limit_bytes=limit),
        cost_estimate=pl.CostEstimate(flops=flops, bytes_accessed=moved, transcendentals=0),
        name=name,
    )(*ins)


def shape(*dims, dtype=F32):
    return jax.ShapeDtypeStruct(dims, dtype)


def split3(value):
    top = value.astype(BF16)
    rest = value - top.astype(F32)
    middle = rest.astype(BF16)
    low = (rest - middle.astype(F32)).astype(BF16)
    return (top, middle, low)


def shifted_lanes(value, by):
    depth = value.shape[1]
    lane = lax.broadcasted_iota(jnp.int32, value.shape, 1)
    if by > 0:
        return jnp.where(lane < depth - by, pltpu.roll(value, depth - by, 1), 0.0)
    return jnp.where(lane >= -by, pltpu.roll(value, -by, 1), 0.0)


def shifted_rows(value, by):
    count = value.shape[0]
    row = lax.broadcasted_iota(jnp.int32, value.shape, 0)
    if by > 0:
        return jnp.where(row < count - by, pltpu.roll(value, count - by, 0), 0.0)
    return jnp.where(row >= -by, pltpu.roll(value, -by, 0), 0.0)


def pack_x_body(feat_ref, fwd_ref, back_ref, up_ref, down_ref, edge_ref, sems):
    channels, size_x = feat_ref.shape[:2]
    copies = []
    for n, (out_ref, start, row) in enumerate(
        ((up_ref, size_x - 4, size_x - 1), (down_ref, 0, 0))
    ):
        pairs = [
            (fwd_ref.at[pl.ds(start, 4)], out_ref.at[pl.ds(0, 4)]),
            (back_ref.at[pl.ds(start, 4)], out_ref.at[pl.ds(4, 4)]),
        ]
        for c in range(channels):
            pairs.append((feat_ref.at[c, row], edge_ref.at[n * channels + c]))
        for m, (source, target) in enumerate(pairs):
            copies.append(
                pltpu.make_async_copy(source, target, sems.at[n * (2 + channels) + m])
            )
    for copy in copies:
        copy.start()
    for copy in copies:
        copy.wait()
    for c in range(channels):
        up_ref[8 + c] = edge_ref[c].astype(F32)
        down_ref[8 + c] = edge_ref[channels + c].astype(F32)


def wave_rows(size_x):
    return size_x * 12


def pack_waves(fwd_ref, back_ref, upward, out_ref, first, edge_ref, low_ref):
    size_x, size_y, depth = fwd_ref.shape
    start, near = (size_y - 4, 2) if upward else (0, 0)
    edge_ref[:, 0:4] = fwd_ref[:, start : start + 4]
    edge_ref[:, 4:8] = back_ref[:, start : start + 4]
    value = edge_ref[...].reshape(size_x * 8, depth)
    high = value.astype(BF16)
    out_ref[first : first + size_x * 8] = high
    edge_ref[...] = (value - high.astype(F32)).reshape(size_x, 8, depth)
    quarter = size_x // 4
    for q in range(4):
        part = slice(q * quarter, (q + 1) * quarter)
        low_ref[:, 4 * q : 4 * q + 2] = edge_ref[part, near : near + 2]
        low_ref[:, 4 * q + 2 : 4 * q + 4] = edge_ref[part, 4 + near : 6 + near]
    out_ref[first + size_x * 8 : first + size_x * 12] = (
        low_ref[...].reshape(size_x * 4, depth).astype(BF16)
    )


def unpack_waves(buffer_ref, upward, first, size_x, edge_ref, low_ref):
    depth = buffer_ref.shape[1]
    near = 2 if upward else 0
    quarter = size_x // 4
    edge_ref[...] = (
        buffer_ref[first : first + size_x * 8].astype(F32).reshape(size_x, 8, depth)
    )
    low_ref[...] = (
        buffer_ref[first + size_x * 8 : first + size_x * 12]
        .astype(F32)
        .reshape(quarter, 16, depth)
    )
    for q in range(4):
        part = slice(q * quarter, (q + 1) * quarter)
        edge_ref[part, near : near + 2] += low_ref[:, 4 * q : 4 * q + 2]
        edge_ref[part, 4 + near : 6 + near] += low_ref[:, 4 * q + 2 : 4 * q + 4]


def pack_y_body(
    feat_ref, fwd_ref, back_ref, low_ref, high_ref, up_ref, down_ref, plane_ref, edge_ref, rest_ref
):
    channels, size_x, size_y, depth = feat_ref.shape
    row = lax.broadcasted_iota(jnp.int32, (16, depth), 0)
    tails = [jnp.zeros((16, depth), F32), jnp.zeros((16, depth), F32)]
    for c in range(channels):
        plane_ref[...] = feat_ref[c].astype(F32)
        for n, (out_ref, y) in enumerate(((up_ref, size_y - 1), (down_ref, 0))):
            out_ref[c * size_x : (c + 1) * size_x] = plane_ref[:, y, :].astype(BF16)
            tails[n] = jnp.where(row == 2 * c, low_ref[8 + c, y : y + 1, :], tails[n])
            tails[n] = jnp.where(row == 2 * c + 1, high_ref[8 + c, y : y + 1, :], tails[n])
    first = channels * size_x
    for tail, out_ref in zip(tails, (up_ref, down_ref)):
        out_ref[first : first + 16] = tail.astype(BF16)
    pack_waves(fwd_ref, back_ref, True, up_ref, first + 16, edge_ref, rest_ref)
    pack_waves(fwd_ref, back_ref, False, down_ref, first + 16, edge_ref, rest_ref)


def fill_features(ext_ref, feat_ref, low_ref, high_ref):
    channels, size_x = feat_ref.shape[:2]
    for c in range(channels):
        ext_ref[c, 0] = low_ref[8 + c]
        ext_ref[c, 1 : 1 + size_x] = feat_ref[c].astype(F32)
        ext_ref[c, 1 + size_x] = high_ref[8 + c]


def conv_body(feat_ref, low_ref, high_ref, weight_ref, place_ref, *refs):
    small_in, (keep_ref, give_ref, *small_out), (ext_ref, total_ref) = (
        refs[:3],
        refs[3:8],
        refs[8:],
    )
    for source, target in zip(small_in, small_out):
        target[...] = source[...]
    channels, size_x = feat_ref.shape[:2]
    fill_features(ext_ref, feat_ref, low_ref, high_ref)
    together = 2

    def some_rows(i, carry):
        start = i * together
        terms = [[[None] * 3 for _ in range(3)] for _ in range(together)]
        for c in range(channels):
            inputs = [ext_ref[c, start + r] for r in range(together + 2)]
            for dx in range(3):
                for dy in range(3):
                    for dz in range(3):
                        weight = weight_ref[c, 9 * dx + 3 * dy + dz]
                        for r in range(together):
                            part = weight * inputs[r + dx]
                            old = terms[r][dy][dz]
                            terms[r][dy][dz] = part if old is None else old + part
        for r in range(together):
            total = None
            for dy in range(3):
                part = (
                    terms[r][dy][1]
                    + shifted_lanes(terms[r][dy][0], -1)
                    + shifted_lanes(terms[r][dy][2], 1)
                )
                if dy != 1:
                    part = shifted_rows(part, dy - 1)
                total = part if total is None else total + part
            total_ref[start + r] = total
        return carry

    lax.fori_loop(0, size_x // together, some_rows, 0)
    half = size_x // 2
    core = place_ref[3]
    keep_ref[...] = total_ref[pl.ds(core * half, half)]
    give_ref[...] = total_ref[pl.ds((1 - core) * half, half)]


def load_plane(plane_ref, buffer_ref, c, size_x, channels):
    plane_ref[8 : 8 + size_x] = buffer_ref[c * size_x : (c + 1) * size_x].astype(F32)
    tail = buffer_ref[channels * size_x : channels * size_x + 16].astype(F32)
    plane_ref[7:8] = tail[2 * c : 2 * c + 1]
    plane_ref[8 + size_x : 9 + size_x] = tail[2 * c + 1 : 2 * c + 2]


def conv_edge_body(low_ref, high_ref, weight_ref, out_ref, plane_ref):
    copies, both_x, depth = out_ref.shape
    size_x = both_x // 2
    channels = weight_ref.shape[0]
    for side, (buffer_ref, dy) in enumerate(((low_ref, 0), (high_ref, 2))):
        terms = [None] * 3
        for c in range(channels):
            load_plane(plane_ref, buffer_ref, c, size_x, channels)
            for dx in range(3):
                rows = plane_ref[7 + dx : 7 + dx + size_x]
                for dz in range(3):
                    part = weight_ref[c, 9 * dx + 3 * dy + dz] * rows
                    terms[dz] = part if terms[dz] is None else terms[dz] + part
        total = terms[1] + shifted_lanes(terms[0], -1) + shifted_lanes(terms[2], 1)
        for n in range(copies):
            out_ref[n, side * size_x : (side + 1) * size_x] = total


def pair_body(keep_ref, got_ref, out_ref):
    total = keep_ref[...] + got_ref[...]
    for n in range(out_ref.shape[0]):
        out_ref[n] = total


def sum_body(parts_ref, out_ref):
    total = parts_ref[0]
    for n in range(1, parts_ref.shape[0]):
        total = total + parts_ref[n]
    out_ref[...] = total


def update_body(parts_ref, damping_ref, out_ref):
    count, rows = parts_ref.shape[:2]
    half = rows // 2
    total = parts_ref[0]
    for n in range(1, count):
        total = total + parts_ref[n]
    update = total[:half] / (total[half:] + damping_ref[0])
    for n in range(count):
        out_ref[n] = update


def receiver_hits(receivers_ref, place_ref, plane_y, size_x, size_y):
    shift_y = plane_y.bit_length() - 1
    receivers = receivers_ref[...]
    place_x = lax.shift_right_logical(receivers, shift_y) - place_ref[0]
    place_y = (receivers & (plane_y - 1)) - place_ref[1]
    inside = (place_x >= 0) & (place_x < size_x) & (place_y >= 0) & (place_y < size_y)
    cell = jnp.where(inside, place_x * size_y + place_y, -1)
    cells = lax.broadcasted_iota(jnp.int32, (size_x * size_y, receivers.shape[1]), 0)
    return (cells == cell).astype(F32).astype(BF16)


def exact_product(parts, other, contract, parts_first):
    total = None
    for part in parts:
        pair = (part, other) if parts_first else (other, part)
        product = lax.dot_general(
            *pair, (contract, ((), ())), preferred_element_type=F32
        )
        total = product if total is None else total + product
    return total


def sample(fwd_ref, hit, trace_ref):
    size_x, size_y, depth = fwd_ref.shape
    field = fwd_ref[...].reshape(size_x * size_y, depth)
    total = exact_product(split3(field), hit, ((0,), (0,)), True)
    trace_ref[...] = total[RDEPTH : RDEPTH + 1, :]


def trace_body(plane_y, fwd_ref, place_ref, receivers_ref, trace_ref):
    size_x, size_y, _ = fwd_ref.shape
    sample(fwd_ref, receiver_hits(receivers_ref, place_ref, plane_y, size_x, size_y), trace_ref)


def inner_body(moment, plane_y, *refs):
    fwd_ref, back_ref, fwd_old_ref, back_old_ref = refs[:4]
    place_ref, receivers_ref, residual_ref = refs[4:7]
    refs = refs[7:]
    if moment == 0:
        x_low_ref, x_high_ref = refs[:2]
        refs = refs[2:]
    fwd_ahead_ref, back_ahead_ref, lap_fwd_ref, lap_back_ref = refs[:4]
    refs = refs[4:]
    if moment == 1:
        trace_ref = refs[0]
        refs = refs[1:]
    x_ref, y_ref, inject_ref = refs
    size_x, size_y, depth = fwd_ref.shape
    rows = 4
    hit = receiver_hits(receivers_ref, place_ref, plane_y, size_x, size_y)
    injected = jnp.where(
        lax.broadcasted_iota(jnp.int32, (depth, hit.shape[1]), 0) == RDEPTH,
        residual_ref[0, moment : moment + 1, :],
        0.0,
    )
    inject_ref[...] = exact_product(split3(injected), hit, ((1,), (1,)), False).reshape(
        size_x, size_y, depth
    )
    if moment == 1:
        sample(fwd_ref, hit, trace_ref)
    zero_x = jnp.zeros((4, size_y, depth), F32)
    y_ref[:, 0:8] = jnp.zeros((size_x, 8, depth), F32)
    y_ref[:, 8 + size_y : 16 + size_y] = jnp.zeros((size_x, 8, depth), F32)
    for first, ref, old_ref, ahead_ref, lap_ref in (
        (0, fwd_ref, fwd_old_ref, fwd_ahead_ref, lap_fwd_ref),
        (4, back_ref, back_old_ref, back_ahead_ref, lap_back_ref),
    ):
        x_ref[0:4] = zero_x if moment else x_low_ref[first : first + 4]
        x_ref[4 : 4 + size_x] = ref[...]
        x_ref[4 + size_x : 8 + size_x] = zero_x if moment else x_high_ref[first : first + 4]
        y_ref[:, 8 : 8 + size_y] = ref[...]

        def one_block(i, carry):
            start = i * rows
            here = pl.ds(start, rows)
            centre = ref[here]
            flat = centre.reshape(rows * size_y, depth)
            result = (3.0 * COEFFICIENTS[0]) * centre
            for k in range(1, 5):
                along_x = x_ref[pl.ds(start + 4 + k, rows)] + x_ref[pl.ds(start + 4 - k, rows)]
                along_y = (
                    y_ref[here, 8 + k : 8 + k + size_y, :] + y_ref[here, 8 - k : 8 - k + size_y, :]
                )
                along_z = shifted_lanes(flat, k) + shifted_lanes(flat, -k)
                result = result + COEFFICIENTS[k] * (
                    along_x + along_y + along_z.reshape(centre.shape)
                )
            if first:
                result = result + inject_ref[here]
            lap_ref[here] = result
            ahead_ref[here] = 2.0 * centre - old_ref[here]
            return carry

        lax.fori_loop(0, size_x // rows, one_block, 0)


def step_body(moment, plane_y, *refs):
    fwd_ahead_ref, back_ahead_ref, lap_fwd_ref, lap_back_ref = refs[:4]
    y_low_ref, y_high_ref, place_ref, wavelet_ref = refs[4:8]
    refs = refs[8:]
    if moment == 0:
        own_ref, other_ref, rims_ref = refs[:3]
        (fwd_new_ref, back_new_ref, lap_ref, squashed_ref) = refs[3:7]
        (x_up_ref, x_down_ref, y_up_ref, y_down_ref) = refs[7:11]
        refs = refs[11:]
        half = own_ref.shape[0]
        core = place_ref[3]
        squashed_ref[pl.ds(core * half, half)] = own_ref[...]
        squashed_ref[pl.ds((1 - core) * half, half)] = other_ref[...]
        size_x, size_y, depth = squashed_ref.shape
        rims = rims_ref[0]
        for n in range(1, rims_ref.shape[0]):
            rims = rims + rims_ref[n]
        squashed_ref[:, 0:1, :] += rims[:size_x].reshape(size_x, 1, depth)
        squashed_ref[:, size_y - 1 : size_y, :] += rims[size_x:].reshape(size_x, 1, depth)
    else:
        squashed_ref, x_low_ref, x_high_ref, lap_old_ref, back_ref = refs[:5]
        (fwd_new_ref, back_new_ref, sums_ref) = refs[5:8]
        refs = refs[8:]
    edge_ref, rest_ref, *sides = refs
    size_x, size_y, depth = fwd_ahead_ref.shape
    start_row = y_low_ref.shape[0] - wave_rows(size_x)
    for n, (buffer_ref, upward) in enumerate(((y_low_ref, True), (y_high_ref, False))):
        unpack_waves(buffer_ref, upward, start_row, size_x, edge_ref, rest_ref)
        for m in range(2):
            side_ref = sides[2 * m + n]
            at, empty = (4, 8) if upward else (8, 0)
            side_ref[:, empty : empty + 8] = jnp.zeros((size_x, 8, depth), F32)
            side_ref[:, at : at + 4] = edge_ref[:, 4 * m : 4 * m + 4]

    anchor_x, anchor_y, source = place_ref[0], place_ref[1], place_ref[2]
    shift_y = plane_y.bit_length() - 1
    shift_z = depth.bit_length() - 1
    column = lax.shift_right_logical(source, shift_z)
    source_x = lax.shift_right_logical(column, shift_y) - anchor_x
    source_y = (column & (plane_y - 1)) - anchor_y
    source_z = source & (depth - 1)
    here = (source_x >= 0) & (source_x < size_x) & (source_y >= 0) & (source_y < size_y)
    spot = jnp.where(here, (source_x * size_y + source_y) * depth + source_z, -1)
    amplitude = wavelet_ref[0, moment]

    def edges(lap, m, start):
        block = slice(start, start + 4)
        low = high = None
        for k in range(1, 5):
            a = COEFFICIENTS[k] * sides[2 * m][block, 8 - k : 16 - k, :]
            b = COEFFICIENTS[k] * sides[2 * m + 1][block, k : 8 + k, :]
            low, high = (a, b) if low is None else (low + a, high + b)
        parts = [low, high]
        if size_y > 16:
            parts.insert(1, jnp.zeros((4, size_y - 16, depth), F32))
        lap = lap + jnp.concatenate(parts, axis=1)
        if moment == 0 or start not in (0, size_x - 4):
            return lap
        parts = []
        for j in range(4):
            total = None
            if start == 0:
                picks = [(k, x_low_ref, 4 * m + 4 + j - k) for k in range(j + 1, 5)]
            else:
                picks = [(k, x_high_ref, 4 * m + j + k - 4) for k in range(4 - j, 5)]
            for k, ref, row in picks:
                part = COEFFICIENTS[k] * ref[row]
                total = part if total is None else total + part
            parts.append(total)
        return lap + jnp.stack(parts)

    for start in range(0, size_x, 4):
        here = slice(start, start + 4)
        squashed = squashed_ref[here]
        if moment == 0:
            squashed = jax.nn.sigmoid(squashed)
            squashed_ref[here] = squashed
        courant = 0.02 + 0.16 * squashed
        lap_fwd = edges(lap_fwd_ref[here], 0, start)
        lap_back = edges(lap_back_ref[here], 1, start)
        dims = lap_fwd.shape
        index = (
            lax.broadcasted_iota(jnp.int32, dims, 0) * (size_y * depth)
            + lax.broadcasted_iota(jnp.int32, dims, 1) * depth
            + lax.broadcasted_iota(jnp.int32, dims, 2)
        )
        added = jnp.where(index == spot - start * (size_y * depth), amplitude, 0.0)
        fwd_new_ref[here] = fwd_ahead_ref[here] + courant * (lap_fwd + added)
        back_new = back_ahead_ref[here] + courant * lap_back
        back_new_ref[here] = back_new
        if moment == 0:
            lap_ref[here] = lap_fwd
        else:
            rows = sums_ref.shape[1] // 2
            n, at = start // rows, start % rows
            lap_old = lap_old_ref[here]
            sums_ref[n, at : at + 4] = lap_old * back_ref[here] + lap_fwd * back_new
            sums_ref[n, rows + at : rows + at + 4] = lap_old * lap_old + lap_fwd * lap_fwd

    if moment == 0:
        x_up_ref[0:4] = fwd_new_ref[size_x - 4 : size_x]
        x_up_ref[4:8] = back_new_ref[size_x - 4 : size_x]
        x_down_ref[0:4] = fwd_new_ref[0:4]
        x_down_ref[4:8] = back_new_ref[0:4]
        pack_waves(fwd_new_ref, back_new_ref, True, y_up_ref, 0, edge_ref, rest_ref)
        pack_waves(fwd_new_ref, back_new_ref, False, y_down_ref, 0, edge_ref, rest_ref)


def gradient_body(
    update_ref,
    squashed_ref,
    feat_ref,
    x_low_ref,
    x_high_ref,
    y_low_ref,
    y_high_ref,
    first_ref,
    second_ref,
    out_ref,
    left_ref,
    right_ref,
    plane_ref,
    rows_ref,
):
    size_x, size_y, depth = update_ref.shape
    channels = feat_ref.shape[0]
    copies = out_ref.shape[0]
    cells = size_x * size_y

    def one_block(i, carry):
        for j in range(4):
            x = 4 * i + j
            squashed = squashed_ref[x]
            pulled = update_ref[x] * (0.16 * squashed * (1.0 - squashed))
            for dy in range(3):
                moved = pulled if dy == 1 else shifted_rows(pulled, 1 - dy)
                high = moved.astype(BF16)
                left_ref[2 * dy, x] = high
                left_ref[2 * dy + 1, x] = (moved - high.astype(F32)).astype(BF16)
            plane_ref[1, pl.ds(x, 1)] = pulled[0:1, :]
            plane_ref[2, pl.ds(x, 1)] = pulled[size_y - 1 : size_y, :]
        return carry

    lax.fori_loop(0, size_x // 4, one_block, 0)
    for c in range(channels):
        right_ref[0, 0] = x_low_ref[8 + c].astype(BF16)
        right_ref[0, 1:size_x] = feat_ref[c, 0 : size_x - 1]
        right_ref[1] = feat_ref[c]
        right_ref[2, 0 : size_x - 1] = feat_ref[c, 1:size_x]
        right_ref[2, size_x - 1] = x_high_ref[8 + c].astype(BF16)
        right = jnp.concatenate(
            [right_ref[dx].reshape(cells, depth) for dx in range(3)], axis=1
        )
        for dy in range(3):
            left = jnp.concatenate(
                [left_ref[2 * dy + part].reshape(cells, depth) for part in range(2)], axis=1
            )
            product = lax.dot_general(
                left, right, (((0,), (0,)), ((), ())), preferred_element_type=F32
            )
            ahead = lax.broadcasted_iota(jnp.int32, (depth, depth), 1) - (
                lax.broadcasted_iota(jnp.int32, (depth, depth), 0)
            )
            for dx in range(3):
                lanes = slice(dx * depth, (dx + 1) * depth)
                block = product[0:depth, lanes] + product[depth : 2 * depth, lanes]
                for dz in range(3):
                    at = c * 27 + 9 * dx + 3 * dy + dz
                    rows_ref[at : at + 1] = jnp.sum(
                        jnp.where(ahead == dz - 1, block, 0.0), axis=0, keepdims=True
                    )
    at = channels * 27
    rows_ref[at:] = jnp.zeros((rows_ref.shape[0] - at, depth), F32)

    for buffer_ref, dy, which in ((y_low_ref, 0, 1), (y_high_ref, 2, 2)):
        pulled = plane_ref[which, 0:size_x]
        along = [pulled if dz == 1 else shifted_lanes(pulled, 1 - dz) for dz in range(3)]
        for c in range(channels):
            load_plane(plane_ref.at[0], buffer_ref, c, size_x, channels)
            for dx in range(3):
                features = plane_ref[0, 7 + dx : 7 + dx + size_x]
                for dz in range(3):
                    at = c * 27 + 9 * dx + 3 * dy + dz
                    rows_ref[at : at + 1] += jnp.sum(
                        features * along[dz], axis=0, keepdims=True
                    )

    ones = jnp.ones((8, depth), BF16)
    sums = None
    for part in split3(rows_ref[...]):
        product = lax.dot_general(
            ones, part, (((1,), (1,)), ((), ())), preferred_element_type=F32
        )
        sums = product if sums is None else sums + product
    count = first_ref.shape[1]
    for n in range(copies):
        out_ref[n, :, 0:count] = first_ref[...]
        out_ref[n, :, count : 2 * count] = second_ref[...]
        out_ref[n, :, 2 * count : 2 * count + depth] = sums[0:1]


def total_body(shares_ref, trace_ref, grad_ref):
    copies = shares_ref.shape[0]
    count = trace_ref.shape[2]
    channels, offsets = grad_ref.shape
    total = shares_ref[0]
    for n in range(1, copies):
        total = total + shares_ref[n]
    trace_ref[0, 0:1, :] = total[:, 0:count]
    trace_ref[0, 1:2, :] = total[:, count : 2 * count]
    last = total[:, 2 * count :]
    lanes = last.shape[1]
    last = jnp.broadcast_to(last, (8, lanes))
    for c in range(channels):
        turned = last if c == 0 else pltpu.roll(last, lanes - c * offsets, 1)
        grad_ref[c : c + 1, :] = turned[0:1, 0:offsets]


def keep_body(value_ref, out_ref):
    out_ref[...] = value_ref[...]


def neighbours(up, down, axis):
    count = lax.axis_size(axis)
    low = lax.ppermute(up, axis, [(i, i + 1) for i in range(count - 1)])
    high = lax.ppermute(down, axis, [(i + 1, i) for i in range(count - 1)])
    return low, high


def per_device(
    features,
    conv_weight,
    fwd_prev,
    fwd_now,
    back_prev,
    back_now,
    sources,
    wavelet,
    receivers,
    residual,
    damping,
):
    channels, size_x, size_y, depth = features.shape
    shots = lax.axis_size("shot")
    rows = size_x // shots
    count = receivers.shape[1]
    plane_y = size_y * lax.axis_size("gy")
    blocks = lax.axis_size("gx") * lax.axis_size("gy")
    grid = (size_x, size_y, depth)
    fwd_prev, fwd_now, back_prev, back_now = (
        a.reshape(grid) for a in (fwd_prev, fwd_now, back_prev, back_now)
    )
    place = jnp.stack(
        [
            lax.axis_index("gx") * size_x,
            lax.axis_index("gy") * size_y,
            sources[0],
            lax.axis_index("shot") % 2,
        ]
    ).astype(jnp.int32)

    x_shape = shape(8 + channels, size_y, depth)
    with jax.named_scope("pack_x"):
        x_up, x_down = call(
            pack_x_body,
            [x_shape, x_shape],
            (features, fwd_now, back_now),
            [pl.BlockSpec(memory_space=pltpu.HBM)] * 3,
            scratch=[
                pltpu.VMEM((2 * channels, size_y, depth), BF16),
                pltpu.SemaphoreType.DMA((2 * (2 + channels),)),
            ],
            name="pack_x",
            limit=VMEM_WHOLE,
        )
    with jax.named_scope("halo_x"):
        x_low, x_high = neighbours(x_up, x_down, "gx")
    packing = [
        pltpu.VMEM((size_x, 8, depth), F32),
        pltpu.VMEM((size_x // 4, 16, depth), F32),
    ]
    y_shape = shape(channels * size_x + 16 + wave_rows(size_x), depth, dtype=BF16)
    with jax.named_scope("pack_y"):
        y_up, y_down = call(
            pack_y_body,
            [y_shape, y_shape],
            (features, fwd_now, back_now, x_low, x_high),
            [VM] * 5,
            scratch=[pltpu.VMEM(grid, F32)] + packing,
            name="pack_y",
        )
    with jax.named_scope("halo_y"):
        y_low, y_high = neighbours(y_up, y_down, "gy")
    ext = pltpu.VMEM((channels, size_x + 2, size_y, depth), F32)
    full = shape(*grid)
    inner_scratch = [
        pltpu.VMEM((size_x + 8, size_y, depth), F32),
        pltpu.VMEM((size_x, size_y + 16, depth), F32),
        pltpu.VMEM(grid, F32),
    ]
    step_scratch = packing + [pltpu.VMEM((size_x, 16, depth), F32)] * 4
    work = 60 * size_x * size_y * depth
    with jax.named_scope("inner_1"):
        inner_1 = call(
            functools.partial(inner_body, 0, plane_y),
            [full] * 4,
            (fwd_now, back_now, fwd_prev, back_prev, place, receivers, residual, x_low, x_high),
            [VM] * 4 + [SM] + [VM] * 4,
            scratch=inner_scratch,
            flops=work,
            name="inner_1",
        )
    half = size_x // 2
    chips = shots // 2
    half_shape = shape(half, size_y, depth)
    partner = [(i, i ^ 1) for i in range(shots)]
    with jax.named_scope("conv"):
        small = (receivers, residual, wavelet)
        keep, give, receivers, residual, wavelet = call(
            conv_body,
            [half_shape] * 2 + [shape(*a.shape, dtype=a.dtype) for a in small],
            (features, x_low, x_high, conv_weight, place) + small,
            [VM, VM, VM, SM, SM] + [VM] * 3,
            scratch=[ext, pltpu.VMEM(grid, F32)],
            flops=54 * channels * size_x * size_y * depth,
            name="conv",
        )
    with jax.named_scope("raw"):
        pair = call(
            pair_body,
            [shape(chips, half, size_y, depth)],
            (keep, lax.ppermute(give, "shot", partner)),
            [VM, VM],
            name="pair",
        )
        if chips > 1:
            groups = [list(range(core, shots, 2)) for core in range(2)]
            pair = lax.all_to_all(
                pair.reshape(chips * half, size_y, depth),
                "shot",
                0,
                0,
                tiled=True,
                axis_index_groups=groups,
            )
        own = call(
            sum_body,
            [half_shape],
            (pair.reshape(chips, half, size_y, depth),),
            [VM],
            name="raw",
        )
        other = lax.ppermute(own, "shot", partner)
    with jax.named_scope("rims"):
        weights, own, other, *inner_1 = lax.optimization_barrier(
            (conv_weight, own, other, *inner_1)
        )
        rims = call(
            conv_edge_body,
            [shape(shots, 2 * size_x, depth)],
            (y_low, y_high, weights),
            [VM, VM, SM],
            scratch=[pltpu.VMEM((size_x + 16, depth), F32)],
            name="conv_edge",
        )
        rims = lax.all_to_all(
            rims.reshape(shots * 2 * size_x, depth), "shot", 0, 0, tiled=True
        ).reshape(shots, 2 * size_x, depth)

    with jax.named_scope("step_1"):
        fwd_1, back_1, lap_1, squashed, x_up, x_down, y_up, y_down = call(
            functools.partial(step_body, 0, plane_y),
            [full] * 4
            + [shape(8, size_y, depth)] * 2
            + [shape(wave_rows(size_x), depth, dtype=BF16)] * 2,
            (
                *inner_1,
                y_low,
                y_high,
                place,
                wavelet,
                own,
                other,
                rims,
            ),
            [VM] * 6 + [SM] * 2 + [VM] * 3,
            scratch=step_scratch,
            name="step_1",
        )
    with jax.named_scope("halo_2"):
        x_low_2, x_high_2 = neighbours(x_up, x_down, "gx")
        y_low_2, y_high_2 = neighbours(y_up, y_down, "gy")
    with jax.named_scope("inner_2"):
        fwd_ahead, back_ahead, lap_fwd, lap_back, trace_1 = call(
            functools.partial(inner_body, 1, plane_y),
            [full] * 4 + [shape(1, count)],
            (fwd_1, back_1, fwd_now, back_now, place, receivers, residual),
            [VM] * 4 + [SM] + [VM] * 2,
            scratch=inner_scratch,
            flops=work,
            name="inner_2",
        )
    with jax.named_scope("step_2"):
        fwd_2, back_2, sums = call(
            functools.partial(step_body, 1, plane_y),
            [full, full, shape(shots, 2 * rows, size_y, depth)],
            (
                fwd_ahead,
                back_ahead,
                lap_fwd,
                lap_back,
                y_low_2,
                y_high_2,
                place,
                wavelet,
                squashed,
                x_low_2,
                x_high_2,
                lap_1,
                back_1,
            ),
            [VM] * 6 + [SM] * 2 + [VM] * 5,
            scratch=step_scratch,
            name="step_2",
        )
    with jax.named_scope("traces"):
        trace_2 = call(
            functools.partial(trace_body, plane_y),
            [shape(1, count)],
            (fwd_2, place, receivers),
            [VM, SM, VM],
            name="trace_2",
        )
    with jax.named_scope("update"):
        sums = lax.all_to_all(
            sums.reshape(shots * 2 * rows, size_y, depth), "shot", 0, 0, tiled=True
        )
        update = call(
            update_body,
            [shape(shots, rows, size_y, depth)],
            (sums.reshape(shots, 2 * rows, size_y, depth), damping),
            [VM, SM],
            name="update",
        )
        update = lax.all_to_all(update.reshape(grid), "shot", 0, 0, tiled=True)
    with jax.named_scope("gradient"):
        share = call(
            gradient_body,
            [shape(blocks, 1, 2 * count + depth)],
            (update, squashed, features, x_low, x_high, y_low, y_high, trace_1, trace_2),
            [VM] * 9,
            scratch=[
                pltpu.VMEM((6,) + grid, BF16),
                pltpu.VMEM((3,) + grid, BF16),
                pltpu.VMEM((3, size_x + 16, depth), F32),
                pltpu.VMEM((128, depth), F32),
            ],
            flops=54 * channels * size_x * size_y * depth,
            name="gradient",
        )
        share, update = lax.optimization_barrier((share, update))
        shares = lax.all_to_all(share, ("gx", "gy"), 0, 0, tiled=True)
        shares = shares.reshape(blocks, 1, 2 * count + depth)
        traces, weight_grad = call(
            total_body,
            [shape(1, 2, count), shape(channels, 27)],
            (shares,),
            [VM],
            name="total",
        )
        update = call(keep_body, [full], (update,), [VM], name="keep")
    return (fwd_2[None], back_2[None], traces, update, weight_grad)


def solution(mesh):
    in_specs = (
        P("shot", "gx", "gy", None),
        P("shot", None),
        P("shot", "gx", "gy", None),
        P("shot", "gx", "gy", None),
        P("shot", "gx", "gy", None),
        P("shot", "gx", "gy", None),
        P("shot"),
        P("shot", None),
        P("shot", None),
        P("shot", None, None),
        P(),
    )
    out_specs = (
        P("shot", "gx", "gy", None),
        P("shot", "gx", "gy", None),
        P("shot", None, None),
        P("gx", "gy", None),
        P("shot", None),
    )
    return jax.shard_map(
        per_device, mesh=mesh, in_specs=in_specs, out_specs=out_specs, check_vma=False
    )
```

```python
import functools

import jax
import jax.numpy as jnp
from jax import lax
from jax.experimental import pallas as pl
from jax.experimental.pallas import tpu as pltpu
from jax.sharding import PartitionSpec as P

RDEPTH = 3
COEFFICIENTS = (-205.0 / 72.0, 8.0 / 5.0, -1.0 / 5.0, 8.0 / 315.0, -1.0 / 560.0)
F32 = jnp.float32
BF16 = jnp.bfloat16
VMEM_LIMIT = 48 * 1024 * 1024
VMEM_WHOLE = 63 * 1024 * 1024

VM = pl.BlockSpec(memory_space=pltpu.VMEM)
SM = pl.BlockSpec(memory_space=pltpu.SMEM)


def call(body, outs, ins, specs, scratch=(), flops=1_000_000, name=None, limit=VMEM_LIMIT):
    moved = sum(a.size * a.dtype.itemsize for a in ins) + sum(
        o.size * jnp.dtype(o.dtype).itemsize for o in outs
    )
    single = len(outs) == 1
    return pl.pallas_call(
        body,
        out_shape=outs[0] if single else tuple(outs),
        in_specs=specs,
        out_specs=VM if single else tuple(VM for _ in outs),
        scratch_shapes=list(scratch),
        compiler_params=pltpu.CompilerParams(vmem_limit_bytes=limit),
        cost_estimate=pl.CostEstimate(flops=flops, bytes_accessed=moved, transcendentals=0),
        name=name,
    )(*ins)


def shape(*dims, dtype=F32):
    return jax.ShapeDtypeStruct(dims, dtype)


def split3(value):
    top = value.astype(BF16)
    rest = value - top.astype(F32)
    middle = rest.astype(BF16)
    low = (rest - middle.astype(F32)).astype(BF16)
    return (top, middle, low)


def shifted_lanes(value, by):
    depth = value.shape[1]
    lane = lax.broadcasted_iota(jnp.int32, value.shape, 1)
    if by > 0:
        return jnp.where(lane < depth - by, pltpu.roll(value, depth - by, 1), 0.0)
    return jnp.where(lane >= -by, pltpu.roll(value, -by, 1), 0.0)


def shifted_rows(value, by):
    count = value.shape[0]
    row = lax.broadcasted_iota(jnp.int32, value.shape, 0)
    if by > 0:
        return jnp.where(row < count - by, pltpu.roll(value, count - by, 0), 0.0)
    return jnp.where(row >= -by, pltpu.roll(value, -by, 0), 0.0)


def pack_x_body(feat_ref, fwd_ref, back_ref, up_ref, down_ref, edge_ref, sems):
    channels, size_x = feat_ref.shape[:2]
    copies = []
    for n, (out_ref, start, row) in enumerate(
        ((up_ref, size_x - 4, size_x - 1), (down_ref, 0, 0))
    ):
        pairs = [
            (fwd_ref.at[pl.ds(start, 4)], out_ref.at[pl.ds(0, 4)]),
            (back_ref.at[pl.ds(start, 4)], out_ref.at[pl.ds(4, 4)]),
        ]
        for c in range(channels):
            pairs.append((feat_ref.at[c, row], edge_ref.at[n * channels + c]))
        for m, (source, target) in enumerate(pairs):
            copies.append(
                pltpu.make_async_copy(source, target, sems.at[n * (2 + channels) + m])
            )
    for copy in copies:
        copy.start()
    for copy in copies:
        copy.wait()
    for c in range(channels):
        up_ref[8 + c] = edge_ref[c].astype(F32)
        down_ref[8 + c] = edge_ref[channels + c].astype(F32)


def wave_rows(size_x):
    return size_x * 10


def row_mix(value, weights, upward):
    count = value.shape[0]
    place = lax.broadcasted_iota(jnp.int32, value.shape, 0) & 3
    distance = 3 - place if upward else place
    total = value
    for j, row in enumerate(weights, 1):
        factor = jnp.zeros(value.shape, F32)
        for n, weight in enumerate(row):
            if weight:
                factor = jnp.where(distance == n, float(weight), factor)
        total = total + factor * pltpu.roll(value, count - j if upward else j, 0)
    return total


def pack_waves(fwd_ref, back_ref, upward, out_ref, first, edge_ref, low_ref):
    size_x, size_y, depth = fwd_ref.shape
    start, near = (size_y - 4, 3) if upward else (0, 0)
    edge_ref[:, 0:4] = fwd_ref[:, start : start + 4]
    edge_ref[:, 4:8] = back_ref[:, start : start + 4]
    value = edge_ref[...].reshape(size_x * 8, depth)
    value = row_mix(value, ((0, -1, -2, -2), (0, 0, 1, 1)), upward)
    high = value.astype(BF16)
    out_ref[first : first + size_x * 8] = high
    edge_ref[...] = (value - high.astype(F32)).reshape(size_x, 8, depth)
    eighth = size_x // 8
    for q in range(8):
        part = slice(q * eighth, (q + 1) * eighth)
        low_ref[:, 2 * q : 2 * q + 1] = edge_ref[part, near : near + 1]
        low_ref[:, 2 * q + 1 : 2 * q + 2] = edge_ref[part, 4 + near : 5 + near]
    out_ref[first + size_x * 8 : first + size_x * 10] = (
        low_ref[...].reshape(size_x * 2, depth).astype(BF16)
    )


def unpack_waves(buffer_ref, upward, first, size_x, edge_ref, low_ref):
    depth = buffer_ref.shape[1]
    near = 3 if upward else 0
    eighth = size_x // 8
    edge_ref[...] = (
        buffer_ref[first : first + size_x * 8].astype(F32).reshape(size_x, 8, depth)
    )
    low_ref[...] = (
        buffer_ref[first + size_x * 8 : first + size_x * 10]
        .astype(F32)
        .reshape(eighth, 16, depth)
    )
    for q in range(8):
        part = slice(q * eighth, (q + 1) * eighth)
        edge_ref[part, near : near + 1] += low_ref[:, 2 * q : 2 * q + 1]
        edge_ref[part, 4 + near : 5 + near] += low_ref[:, 2 * q + 1 : 2 * q + 2]
    value = edge_ref[...].reshape(size_x * 8, depth)
    value = row_mix(value, ((0, 1, 2, 2), (0, 0, 1, 3), (0, 0, 0, 1)), upward)
    edge_ref[...] = value.reshape(size_x, 8, depth)


def pack_y_body(
    feat_ref, fwd_ref, back_ref, low_ref, high_ref, up_ref, down_ref, plane_ref, edge_ref, rest_ref
):
    channels, size_x, size_y, depth = feat_ref.shape
    row = lax.broadcasted_iota(jnp.int32, (16, depth), 0)
    tails = [jnp.zeros((16, depth), F32), jnp.zeros((16, depth), F32)]
    for c in range(channels):
        plane_ref[...] = feat_ref[c].astype(F32)
        for n, (out_ref, y) in enumerate(((up_ref, size_y - 1), (down_ref, 0))):
            out_ref[c * size_x : (c + 1) * size_x] = plane_ref[:, y, :].astype(BF16)
            tails[n] = jnp.where(row == 2 * c, low_ref[8 + c, y : y + 1, :], tails[n])
            tails[n] = jnp.where(row == 2 * c + 1, high_ref[8 + c, y : y + 1, :], tails[n])
    first = channels * size_x
    for tail, out_ref in zip(tails, (up_ref, down_ref)):
        out_ref[first : first + 16] = tail.astype(BF16)
    pack_waves(fwd_ref, back_ref, True, up_ref, first + 16, edge_ref, rest_ref)
    pack_waves(fwd_ref, back_ref, False, down_ref, first + 16, edge_ref, rest_ref)


def fill_features(ext_ref, feat_ref, low_ref, high_ref):
    channels, size_x = feat_ref.shape[:2]
    for c in range(channels):
        ext_ref[c, 0] = low_ref[8 + c]
        ext_ref[c, 1 : 1 + size_x] = feat_ref[c].astype(F32)
        ext_ref[c, 1 + size_x] = high_ref[8 + c]


def conv_body(feat_ref, low_ref, high_ref, weight_ref, *refs):
    small_in, (total_ref, *small_out), ext_ref = refs[:3], refs[3:7], refs[7]
    for source, target in zip(small_in, small_out):
        target[...] = source[...]
    channels, size_x = feat_ref.shape[:2]
    fill_features(ext_ref, feat_ref, low_ref, high_ref)
    together = 2

    def some_rows(i, carry):
        start = i * together
        terms = [[[None] * 3 for _ in range(3)] for _ in range(together)]
        for c in range(channels):
            inputs = [ext_ref[c, start + r] for r in range(together + 2)]
            for dx in range(3):
                for dy in range(3):
                    for dz in range(3):
                        weight = weight_ref[c, 9 * dx + 3 * dy + dz]
                        for r in range(together):
                            part = weight * inputs[r + dx]
                            old = terms[r][dy][dz]
                            terms[r][dy][dz] = part if old is None else old + part
        for r in range(together):
            total = None
            for dy in range(3):
                part = (
                    terms[r][dy][1]
                    + shifted_lanes(terms[r][dy][0], -1)
                    + shifted_lanes(terms[r][dy][2], 1)
                )
                if dy != 1:
                    part = shifted_rows(part, dy - 1)
                total = part if total is None else total + part
            total_ref[start + r] = total
        return carry

    lax.fori_loop(0, size_x // together, some_rows, 0)


def load_plane(plane_ref, buffer_ref, c, size_x, channels):
    plane_ref[8 : 8 + size_x] = buffer_ref[c * size_x : (c + 1) * size_x].astype(F32)
    tail = buffer_ref[channels * size_x : channels * size_x + 16].astype(F32)
    plane_ref[7:8] = tail[2 * c : 2 * c + 1]
    plane_ref[8 + size_x : 9 + size_x] = tail[2 * c + 1 : 2 * c + 2]


def conv_edge_body(parts_ref, low_ref, high_ref, weight_ref, out_ref, plane_ref):
    copies, rows, size_y, depth = parts_ref.shape
    size_x = copies * rows
    channels = weight_ref.shape[0]
    total = parts_ref[0]
    for n in range(1, copies):
        total = total + parts_ref[n]
    first = rows * size_y
    total = total.reshape(first, depth)
    for n in range(copies):
        out_ref[n, 0:first] = total
    for side, (buffer_ref, dy) in enumerate(((low_ref, 0), (high_ref, 2))):
        terms = [None] * 3
        for c in range(channels):
            load_plane(plane_ref, buffer_ref, c, size_x, channels)
            for dx in range(3):
                plane = plane_ref[7 + dx : 7 + dx + size_x]
                for dz in range(3):
                    part = weight_ref[c, 9 * dx + 3 * dy + dz] * plane
                    terms[dz] = part if terms[dz] is None else terms[dz] + part
        total = terms[1] + shifted_lanes(terms[0], -1) + shifted_lanes(terms[2], 1)
        at = first + side * size_x
        for n in range(copies):
            out_ref[n, at : at + size_x] = total


def update_body(parts_ref, damping_ref, out_ref):
    count, rows = parts_ref.shape[:2]
    half = rows // 2
    total = parts_ref[0]
    for n in range(1, count):
        total = total + parts_ref[n]
    update = total[:half] / (total[half:] + damping_ref[0])
    for n in range(count):
        out_ref[n] = update


def receiver_hits(receivers_ref, place_ref, plane_y, size_x, size_y):
    shift_y = plane_y.bit_length() - 1
    receivers = receivers_ref[...]
    place_x = lax.shift_right_logical(receivers, shift_y) - place_ref[0]
    place_y = (receivers & (plane_y - 1)) - place_ref[1]
    inside = (place_x >= 0) & (place_x < size_x) & (place_y >= 0) & (place_y < size_y)
    cell = jnp.where(inside, place_x * size_y + place_y, -1)
    cells = lax.broadcasted_iota(jnp.int32, (size_x * size_y, receivers.shape[1]), 0)
    return (cells == cell).astype(F32).astype(BF16)


def exact_product(parts, other, contract, parts_first):
    total = None
    for part in parts:
        pair = (part, other) if parts_first else (other, part)
        product = lax.dot_general(
            *pair, (contract, ((), ())), preferred_element_type=F32
        )
        total = product if total is None else total + product
    return total


def sample(fwd_ref, hit, trace_ref):
    size_x, size_y, depth = fwd_ref.shape
    field = fwd_ref[...].reshape(size_x * size_y, depth)
    total = exact_product(split3(field), hit, ((0,), (0,)), True)
    trace_ref[...] = total[RDEPTH : RDEPTH + 1, :]


def trace_body(plane_y, fwd_ref, place_ref, receivers_ref, trace_ref):
    size_x, size_y, _ = fwd_ref.shape
    sample(fwd_ref, receiver_hits(receivers_ref, place_ref, plane_y, size_x, size_y), trace_ref)


def inner_body(moment, plane_y, *refs):
    fwd_ref, back_ref, fwd_old_ref, back_old_ref = refs[:4]
    place_ref, receivers_ref, residual_ref = refs[4:7]
    refs = refs[7:]
    if moment == 0:
        x_low_ref, x_high_ref = refs[:2]
        refs = refs[2:]
    fwd_ahead_ref, back_ahead_ref, lap_fwd_ref, lap_back_ref = refs[:4]
    refs = refs[4:]
    if moment == 1:
        trace_ref = refs[0]
        refs = refs[1:]
    x_ref, y_ref, inject_ref = refs
    size_x, size_y, depth = fwd_ref.shape
    rows = 4
    hit = receiver_hits(receivers_ref, place_ref, plane_y, size_x, size_y)
    injected = jnp.where(
        lax.broadcasted_iota(jnp.int32, (depth, hit.shape[1]), 0) == RDEPTH,
        residual_ref[0, moment : moment + 1, :],
        0.0,
    )
    inject_ref[...] = exact_product(split3(injected), hit, ((1,), (1,)), False).reshape(
        size_x, size_y, depth
    )
    if moment == 1:
        sample(fwd_ref, hit, trace_ref)
    zero_x = jnp.zeros((4, size_y, depth), F32)
    y_ref[:, 0:8] = jnp.zeros((size_x, 8, depth), F32)
    y_ref[:, 8 + size_y : 16 + size_y] = jnp.zeros((size_x, 8, depth), F32)
    for first, ref, old_ref, ahead_ref, lap_ref in (
        (0, fwd_ref, fwd_old_ref, fwd_ahead_ref, lap_fwd_ref),
        (4, back_ref, back_old_ref, back_ahead_ref, lap_back_ref),
    ):
        x_ref[0:4] = zero_x if moment else x_low_ref[first : first + 4]
        x_ref[4 : 4 + size_x] = ref[...]
        x_ref[4 + size_x : 8 + size_x] = zero_x if moment else x_high_ref[first : first + 4]
        y_ref[:, 8 : 8 + size_y] = ref[...]

        def one_block(i, carry):
            start = i * rows
            here = pl.ds(start, rows)
            centre = ref[here]
            flat = centre.reshape(rows * size_y, depth)
            result = (3.0 * COEFFICIENTS[0]) * centre
            for k in range(1, 5):
                along_x = x_ref[pl.ds(start + 4 + k, rows)] + x_ref[pl.ds(start + 4 - k, rows)]
                along_y = (
                    y_ref[here, 8 + k : 8 + k + size_y, :] + y_ref[here, 8 - k : 8 - k + size_y, :]
                )
                along_z = shifted_lanes(flat, k) + shifted_lanes(flat, -k)
                result = result + COEFFICIENTS[k] * (
                    along_x + along_y + along_z.reshape(centre.shape)
                )
            if first:
                result = result + inject_ref[here]
            lap_ref[here] = result
            ahead_ref[here] = 2.0 * centre - old_ref[here]
            return carry

        lax.fori_loop(0, size_x // rows, one_block, 0)


def step_body(moment, plane_y, *refs):
    fwd_ahead_ref, back_ahead_ref, lap_fwd_ref, lap_back_ref = refs[:4]
    y_low_ref, y_high_ref, place_ref, wavelet_ref = refs[4:8]
    refs = refs[8:]
    if moment == 0:
        raw_ref = refs[0]
        (fwd_new_ref, back_new_ref, lap_ref, squashed_ref) = refs[1:5]
        (x_up_ref, x_down_ref, y_up_ref, y_down_ref) = refs[5:9]
        refs = refs[9:]
        size_x, size_y, depth = squashed_ref.shape
        shots = raw_ref.shape[0]
        rows = size_x // shots
        first = rows * size_y
        rims = None
        for n in range(shots):
            squashed_ref[n * rows : (n + 1) * rows] = raw_ref[n, 0:first].reshape(
                rows, size_y, depth
            )
            part = raw_ref[n, first:]
            rims = part if rims is None else rims + part
        squashed_ref[:, 0:1, :] += rims[:size_x].reshape(size_x, 1, depth)
        squashed_ref[:, size_y - 1 : size_y, :] += rims[size_x:].reshape(size_x, 1, depth)
    else:
        squashed_ref, x_low_ref, x_high_ref, lap_old_ref, back_ref = refs[:5]
        (fwd_new_ref, back_new_ref, sums_ref) = refs[5:8]
        refs = refs[8:]
    edge_ref, rest_ref, *sides = refs
    size_x, size_y, depth = fwd_ahead_ref.shape
    start_row = y_low_ref.shape[0] - wave_rows(size_x)
    for n, (buffer_ref, upward) in enumerate(((y_low_ref, True), (y_high_ref, False))):
        unpack_waves(buffer_ref, upward, start_row, size_x, edge_ref, rest_ref)
        for m in range(2):
            side_ref = sides[2 * m + n]
            at, empty = (4, 8) if upward else (8, 0)
            side_ref[:, empty : empty + 8] = jnp.zeros((size_x, 8, depth), F32)
            side_ref[:, at : at + 4] = edge_ref[:, 4 * m : 4 * m + 4]

    anchor_x, anchor_y, source = place_ref[0], place_ref[1], place_ref[2]
    shift_y = plane_y.bit_length() - 1
    shift_z = depth.bit_length() - 1
    column = lax.shift_right_logical(source, shift_z)
    source_x = lax.shift_right_logical(column, shift_y) - anchor_x
    source_y = (column & (plane_y - 1)) - anchor_y
    source_z = source & (depth - 1)
    here = (source_x >= 0) & (source_x < size_x) & (source_y >= 0) & (source_y < size_y)
    spot = jnp.where(here, (source_x * size_y + source_y) * depth + source_z, -1)
    amplitude = wavelet_ref[0, moment]

    def edges(lap, m, start):
        block = slice(start, start + 4)
        low = high = None
        for k in range(1, 5):
            a = COEFFICIENTS[k] * sides[2 * m][block, 8 - k : 16 - k, :]
            b = COEFFICIENTS[k] * sides[2 * m + 1][block, k : 8 + k, :]
            low, high = (a, b) if low is None else (low + a, high + b)
        parts = [low, high]
        if size_y > 16:
            parts.insert(1, jnp.zeros((4, size_y - 16, depth), F32))
        lap = lap + jnp.concatenate(parts, axis=1)
        if moment == 0 or start not in (0, size_x - 4):
            return lap
        parts = []
        for j in range(4):
            total = None
            if start == 0:
                picks = [(k, x_low_ref, 4 * m + 4 + j - k) for k in range(j + 1, 5)]
            else:
                picks = [(k, x_high_ref, 4 * m + j + k - 4) for k in range(4 - j, 5)]
            for k, ref, row in picks:
                part = COEFFICIENTS[k] * ref[row]
                total = part if total is None else total + part
            parts.append(total)
        return lap + jnp.stack(parts)

    for start in range(0, size_x, 4):
        here = slice(start, start + 4)
        squashed = squashed_ref[here]
        if moment == 0:
            squashed = jax.nn.sigmoid(squashed)
            squashed_ref[here] = squashed
        courant = 0.02 + 0.16 * squashed
        lap_fwd = edges(lap_fwd_ref[here], 0, start)
        lap_back = edges(lap_back_ref[here], 1, start)
        dims = lap_fwd.shape
        index = (
            lax.broadcasted_iota(jnp.int32, dims, 0) * (size_y * depth)
            + lax.broadcasted_iota(jnp.int32, dims, 1) * depth
            + lax.broadcasted_iota(jnp.int32, dims, 2)
        )
        added = jnp.where(index == spot - start * (size_y * depth), amplitude, 0.0)
        fwd_new_ref[here] = fwd_ahead_ref[here] + courant * (lap_fwd + added)
        back_new = back_ahead_ref[here] + courant * lap_back
        back_new_ref[here] = back_new
        if moment == 0:
            lap_ref[here] = lap_fwd
        else:
            rows = sums_ref.shape[1] // 2
            n, at = start // rows, start % rows
            lap_old = lap_old_ref[here]
            sums_ref[n, at : at + 4] = lap_old * back_ref[here] + lap_fwd * back_new
            sums_ref[n, rows + at : rows + at + 4] = lap_old * lap_old + lap_fwd * lap_fwd

    if moment == 0:
        x_up_ref[0:4] = fwd_new_ref[size_x - 4 : size_x]
        x_up_ref[4:8] = back_new_ref[size_x - 4 : size_x]
        x_down_ref[0:4] = fwd_new_ref[0:4]
        x_down_ref[4:8] = back_new_ref[0:4]
        pack_waves(fwd_new_ref, back_new_ref, True, y_up_ref, 0, edge_ref, rest_ref)
        pack_waves(fwd_new_ref, back_new_ref, False, y_down_ref, 0, edge_ref, rest_ref)


def gradient_body(
    update_ref,
    squashed_ref,
    feat_ref,
    x_low_ref,
    x_high_ref,
    y_low_ref,
    y_high_ref,
    first_ref,
    second_ref,
    out_ref,
    left_ref,
    right_ref,
    plane_ref,
    rows_ref,
):
    size_x, size_y, depth = update_ref.shape
    channels = feat_ref.shape[0]
    copies = out_ref.shape[0]
    cells = size_x * size_y

    def one_block(i, carry):
        for j in range(4):
            x = 4 * i + j
            squashed = squashed_ref[x]
            pulled = update_ref[x] * (0.16 * squashed * (1.0 - squashed))
            for dy in range(3):
                moved = pulled if dy == 1 else shifted_rows(pulled, 1 - dy)
                high = moved.astype(BF16)
                left_ref[2 * dy, x] = high
                left_ref[2 * dy + 1, x] = (moved - high.astype(F32)).astype(BF16)
            plane_ref[1, pl.ds(x, 1)] = pulled[0:1, :]
            plane_ref[2, pl.ds(x, 1)] = pulled[size_y - 1 : size_y, :]
        return carry

    lax.fori_loop(0, size_x // 4, one_block, 0)
    for c in range(channels):
        right_ref[0, 0] = x_low_ref[8 + c].astype(BF16)
        right_ref[0, 1:size_x] = feat_ref[c, 0 : size_x - 1]
        right_ref[1] = feat_ref[c]
        right_ref[2, 0 : size_x - 1] = feat_ref[c, 1:size_x]
        right_ref[2, size_x - 1] = x_high_ref[8 + c].astype(BF16)
        right = jnp.concatenate(
            [right_ref[dx].reshape(cells, depth) for dx in range(3)], axis=1
        )
        for dy in range(3):
            left = jnp.concatenate(
                [left_ref[2 * dy + part].reshape(cells, depth) for part in range(2)], axis=1
            )
            product = lax.dot_general(
                left, right, (((0,), (0,)), ((), ())), preferred_element_type=F32
            )
            ahead = lax.broadcasted_iota(jnp.int32, (depth, depth), 1) - (
                lax.broadcasted_iota(jnp.int32, (depth, depth), 0)
            )
            for dx in range(3):
                lanes = slice(dx * depth, (dx + 1) * depth)
                block = product[0:depth, lanes] + product[depth : 2 * depth, lanes]
                for dz in range(3):
                    at = c * 27 + 9 * dx + 3 * dy + dz
                    rows_ref[at : at + 1] = jnp.sum(
                        jnp.where(ahead == dz - 1, block, 0.0), axis=0, keepdims=True
                    )
    at = channels * 27
    rows_ref[at:] = jnp.zeros((rows_ref.shape[0] - at, depth), F32)

    for buffer_ref, dy, which in ((y_low_ref, 0, 1), (y_high_ref, 2, 2)):
        pulled = plane_ref[which, 0:size_x]
        along = [pulled if dz == 1 else shifted_lanes(pulled, 1 - dz) for dz in range(3)]
        for c in range(channels):
            load_plane(plane_ref.at[0], buffer_ref, c, size_x, channels)
            for dx in range(3):
                features = plane_ref[0, 7 + dx : 7 + dx + size_x]
                for dz in range(3):
                    at = c * 27 + 9 * dx + 3 * dy + dz
                    rows_ref[at : at + 1] += jnp.sum(
                        features * along[dz], axis=0, keepdims=True
                    )

    ones = jnp.ones((8, depth), BF16)
    sums = None
    for part in split3(rows_ref[...]):
        product = lax.dot_general(
            ones, part, (((1,), (1,)), ((), ())), preferred_element_type=F32
        )
        sums = product if sums is None else sums + product
    count = first_ref.shape[1]
    for n in range(copies):
        out_ref[n, :, 0:count] = first_ref[...]
        out_ref[n, :, count : 2 * count] = second_ref[...]
        out_ref[n, :, 2 * count : 2 * count + depth] = sums[0:1]


def total_body(shares_ref, trace_ref, grad_ref):
    copies = shares_ref.shape[0]
    count = trace_ref.shape[2]
    channels, offsets = grad_ref.shape
    total = shares_ref[0]
    for n in range(1, copies):
        total = total + shares_ref[n]
    trace_ref[0, 0:1, :] = total[:, 0:count]
    trace_ref[0, 1:2, :] = total[:, count : 2 * count]
    last = total[:, 2 * count :]
    lanes = last.shape[1]
    last = jnp.broadcast_to(last, (8, lanes))
    for c in range(channels):
        turned = last if c == 0 else pltpu.roll(last, lanes - c * offsets, 1)
        grad_ref[c : c + 1, :] = turned[0:1, 0:offsets]


def keep_body(value_ref, out_ref):
    out_ref[...] = value_ref[...]


def neighbours(up, down, axis):
    count = lax.axis_size(axis)
    low = lax.ppermute(up, axis, [(i, i + 1) for i in range(count - 1)])
    high = lax.ppermute(down, axis, [(i + 1, i) for i in range(count - 1)])
    return low, high


def per_device(
    features,
    conv_weight,
    fwd_prev,
    fwd_now,
    back_prev,
    back_now,
    sources,
    wavelet,
    receivers,
    residual,
    damping,
):
    channels, size_x, size_y, depth = features.shape
    shots = lax.axis_size("shot")
    rows = size_x // shots
    count = receivers.shape[1]
    plane_y = size_y * lax.axis_size("gy")
    blocks = lax.axis_size("gx") * lax.axis_size("gy")
    grid = (size_x, size_y, depth)
    fwd_prev, fwd_now, back_prev, back_now = (
        a.reshape(grid) for a in (fwd_prev, fwd_now, back_prev, back_now)
    )
    place = jnp.stack(
        [
            lax.axis_index("gx") * size_x,
            lax.axis_index("gy") * size_y,
            sources[0],
        ]
    ).astype(jnp.int32)

    x_shape = shape(8 + channels, size_y, depth)
    with jax.named_scope("pack_x"):
        x_up, x_down = call(
            pack_x_body,
            [x_shape, x_shape],
            (features, fwd_now, back_now),
            [pl.BlockSpec(memory_space=pltpu.HBM)] * 3,
            scratch=[
                pltpu.VMEM((2 * channels, size_y, depth), BF16),
                pltpu.SemaphoreType.DMA((2 * (2 + channels),)),
            ],
            name="pack_x",
            limit=VMEM_WHOLE,
        )
    with jax.named_scope("halo_x"):
        x_low, x_high = neighbours(x_up, x_down, "gx")
    packing = [
        pltpu.VMEM((size_x, 8, depth), F32),
        pltpu.VMEM((size_x // 8, 16, depth), F32),
    ]
    y_shape = shape(channels * size_x + 16 + wave_rows(size_x), depth, dtype=BF16)
    with jax.named_scope("pack_y"):
        y_up, y_down = call(
            pack_y_body,
            [y_shape, y_shape],
            (features, fwd_now, back_now, x_low, x_high),
            [VM] * 5,
            scratch=[pltpu.VMEM(grid, F32)] + packing,
            name="pack_y",
        )
    with jax.named_scope("halo_y"):
        y_low, y_high = neighbours(y_up, y_down, "gy")
    ext = pltpu.VMEM((channels, size_x + 2, size_y, depth), F32)
    full = shape(*grid)
    inner_scratch = [
        pltpu.VMEM((size_x + 8, size_y, depth), F32),
        pltpu.VMEM((size_x, size_y + 16, depth), F32),
        pltpu.VMEM(grid, F32),
    ]
    step_scratch = packing + [pltpu.VMEM((size_x, 16, depth), F32)] * 4
    work = 60 * size_x * size_y * depth
    with jax.named_scope("inner_1"):
        inner_1 = call(
            functools.partial(inner_body, 0, plane_y),
            [full] * 4,
            (fwd_now, back_now, fwd_prev, back_prev, place, receivers, residual, x_low, x_high),
            [VM] * 4 + [SM] + [VM] * 4,
            scratch=inner_scratch,
            flops=work,
            name="inner_1",
        )
    with jax.named_scope("conv"):
        small = (receivers, residual, wavelet)
        main, receivers, residual, wavelet = call(
            conv_body,
            [full] + [shape(*a.shape, dtype=a.dtype) for a in small],
            (features, x_low, x_high, conv_weight) + small,
            [VM, VM, VM, SM] + [VM] * 3,
            scratch=[ext],
            flops=54 * channels * size_x * size_y * depth,
            name="conv",
        )
    with jax.named_scope("raw"):
        parts = lax.all_to_all(main, "shot", 0, 0, tiled=True)
        parts, *inner_1 = lax.optimization_barrier((parts, *inner_1))
        each = rows * size_y + 2 * size_x
        raw = call(
            conv_edge_body,
            [shape(shots, each, depth)],
            (parts.reshape(shots, rows, size_y, depth), y_low, y_high, conv_weight),
            [VM] * 3 + [SM],
            scratch=[pltpu.VMEM((size_x + 16, depth), F32)],
            name="conv_edge",
        )
        raw = lax.all_to_all(raw.reshape(shots * each, depth), "shot", 0, 0, tiled=True)
        raw = raw.reshape(shots, each, depth)

    with jax.named_scope("step_1"):
        fwd_1, back_1, lap_1, squashed, x_up, x_down, y_up, y_down = call(
            functools.partial(step_body, 0, plane_y),
            [full] * 4
            + [shape(8, size_y, depth)] * 2
            + [shape(wave_rows(size_x), depth, dtype=BF16)] * 2,
            (
                *inner_1,
                y_low,
                y_high,
                place,
                wavelet,
                raw,
            ),
            [VM] * 6 + [SM] * 2 + [VM],
            scratch=step_scratch,
            name="step_1",
        )
    with jax.named_scope("halo_2"):
        x_low_2, x_high_2 = neighbours(x_up, x_down, "gx")
        y_low_2, y_high_2 = neighbours(y_up, y_down, "gy")
    with jax.named_scope("inner_2"):
        fwd_ahead, back_ahead, lap_fwd, lap_back, trace_1 = call(
            functools.partial(inner_body, 1, plane_y),
            [full] * 4 + [shape(1, count)],
            (fwd_1, back_1, fwd_now, back_now, place, receivers, residual),
            [VM] * 4 + [SM] + [VM] * 2,
            scratch=inner_scratch,
            flops=work,
            name="inner_2",
        )
    with jax.named_scope("step_2"):
        fwd_2, back_2, sums = call(
            functools.partial(step_body, 1, plane_y),
            [full, full, shape(shots, 2 * rows, size_y, depth)],
            (
                fwd_ahead,
                back_ahead,
                lap_fwd,
                lap_back,
                y_low_2,
                y_high_2,
                place,
                wavelet,
                squashed,
                x_low_2,
                x_high_2,
                lap_1,
                back_1,
            ),
            [VM] * 6 + [SM] * 2 + [VM] * 5,
            scratch=step_scratch,
            name="step_2",
        )
    with jax.named_scope("traces"):
        trace_2 = call(
            functools.partial(trace_body, plane_y),
            [shape(1, count)],
            (fwd_2, place, receivers),
            [VM, SM, VM],
            name="trace_2",
        )
    with jax.named_scope("update"):
        sums = lax.all_to_all(
            sums.reshape(shots * 2 * rows, size_y, depth), "shot", 0, 0, tiled=True
        )
        update = call(
            update_body,
            [shape(shots, rows, size_y, depth)],
            (sums.reshape(shots, 2 * rows, size_y, depth), damping),
            [VM, SM],
            name="update",
        )
        update = lax.all_to_all(update.reshape(grid), "shot", 0, 0, tiled=True)
    with jax.named_scope("gradient"):
        share = call(
            gradient_body,
            [shape(blocks, 1, 2 * count + depth)],
            (update, squashed, features, x_low, x_high, y_low, y_high, trace_1, trace_2),
            [VM] * 9,
            scratch=[
                pltpu.VMEM((6,) + grid, BF16),
                pltpu.VMEM((3,) + grid, BF16),
                pltpu.VMEM((3, size_x + 16, depth), F32),
                pltpu.VMEM((128, depth), F32),
            ],
            flops=54 * channels * size_x * size_y * depth,
            name="gradient",
        )
        share, update = lax.optimization_barrier((share, update))
        shares = lax.all_to_all(share, ("gx", "gy"), 0, 0, tiled=True)
        shares = shares.reshape(blocks, 1, 2 * count + depth)
        traces, weight_grad = call(
            total_body,
            [shape(1, 2, count), shape(channels, 27)],
            (shares,),
            [VM],
            name="total",
        )
        update = call(keep_body, [full], (update,), [VM], name="keep")
    return (fwd_2[None], back_2[None], traces, update, weight_grad)


def solution(mesh):
    in_specs = (
        P("shot", "gx", "gy", None),
        P("shot", None),
        P("shot", "gx", "gy", None),
        P("shot", "gx", "gy", None),
        P("shot", "gx", "gy", None),
        P("shot", "gx", "gy", None),
        P("shot"),
        P("shot", None),
        P("shot", None),
        P("shot", None, None),
        P(),
    )
    out_specs = (
        P("shot", "gx", "gy", None),
        P("shot", "gx", "gy", None),
        P("shot", None, None),
        P("gx", "gy", None),
        P("shot", None),
    )
    return jax.shard_map(
        per_device, mesh=mesh, in_specs=in_specs, out_specs=out_specs, check_vma=False
    )
```

```python
import functools

import jax
import jax.numpy as jnp
from jax import lax
from jax.experimental import pallas as pl
from jax.experimental.pallas import tpu as pltpu
from jax.sharding import PartitionSpec as P

RDEPTH = 3
COEFFICIENTS = (-205.0 / 72.0, 8.0 / 5.0, -1.0 / 5.0, 8.0 / 315.0, -1.0 / 560.0)
F32 = jnp.float32
BF16 = jnp.bfloat16
VMEM_LIMIT = 48 * 1024 * 1024
AHEAD = 50_000_000_000
VMEM_WHOLE = 63 * 1024 * 1024

VM = pl.BlockSpec(memory_space=pltpu.VMEM)
SM = pl.BlockSpec(memory_space=pltpu.SMEM)


def call(body, outs, ins, specs, scratch=(), flops=1_000_000, name=None, limit=VMEM_LIMIT):
    moved = sum(a.size * a.dtype.itemsize for a in ins) + sum(
        o.size * jnp.dtype(o.dtype).itemsize for o in outs
    )
    single = len(outs) == 1
    return pl.pallas_call(
        body,
        out_shape=outs[0] if single else tuple(outs),
        in_specs=specs,
        out_specs=VM if single else tuple(VM for _ in outs),
        scratch_shapes=list(scratch),
        compiler_params=pltpu.CompilerParams(vmem_limit_bytes=limit),
        cost_estimate=pl.CostEstimate(flops=flops, bytes_accessed=moved, transcendentals=0),
        name=name,
    )(*ins)


def shape(*dims, dtype=F32):
    return jax.ShapeDtypeStruct(dims, dtype)


def split3(value):
    top = value.astype(BF16)
    rest = value - top.astype(F32)
    middle = rest.astype(BF16)
    low = (rest - middle.astype(F32)).astype(BF16)
    return (top, middle, low)


def shifted_lanes(value, by):
    depth = value.shape[1]
    lane = lax.broadcasted_iota(jnp.int32, value.shape, 1)
    if by > 0:
        return jnp.where(lane < depth - by, pltpu.roll(value, depth - by, 1), 0.0)
    return jnp.where(lane >= -by, pltpu.roll(value, -by, 1), 0.0)


def shifted_rows(value, by):
    count = value.shape[0]
    row = lax.broadcasted_iota(jnp.int32, value.shape, 0)
    if by > 0:
        return jnp.where(row < count - by, pltpu.roll(value, count - by, 0), 0.0)
    return jnp.where(row >= -by, pltpu.roll(value, -by, 0), 0.0)


def pack_x_body(feat_ref, fwd_ref, back_ref, up_ref, down_ref, edge_ref, sems):
    channels, size_x = feat_ref.shape[:2]
    copies = []
    for n, (out_ref, start, row) in enumerate(
        ((up_ref, size_x - 4, size_x - 1), (down_ref, 0, 0))
    ):
        pairs = [
            (fwd_ref.at[pl.ds(start, 4)], out_ref.at[pl.ds(0, 4)]),
            (back_ref.at[pl.ds(start, 4)], out_ref.at[pl.ds(4, 4)]),
        ]
        for c in range(channels):
            pairs.append((feat_ref.at[c, row], edge_ref.at[n * channels + c]))
        for m, (source, target) in enumerate(pairs):
            copies.append(
                pltpu.make_async_copy(source, target, sems.at[n * (2 + channels) + m])
            )
    for copy in copies:
        copy.start()
    for copy in copies:
        copy.wait()
    for c in range(channels):
        up_ref[8 + c] = edge_ref[c].astype(F32)
        down_ref[8 + c] = edge_ref[channels + c].astype(F32)


def wave_rows(size_x):
    return size_x * 12


def pack_waves(fwd_ref, back_ref, upward, out_ref, first, edge_ref, low_ref):
    size_x, size_y, depth = fwd_ref.shape
    start, near = (size_y - 4, 2) if upward else (0, 0)
    edge_ref[:, 0:4] = fwd_ref[:, start : start + 4]
    edge_ref[:, 4:8] = back_ref[:, start : start + 4]
    value = edge_ref[...].reshape(size_x * 8, depth)
    high = value.astype(BF16)
    out_ref[first : first + size_x * 8] = high
    edge_ref[...] = (value - high.astype(F32)).reshape(size_x, 8, depth)
    quarter = size_x // 4
    for q in range(4):
        part = slice(q * quarter, (q + 1) * quarter)
        low_ref[:, 4 * q : 4 * q + 2] = edge_ref[part, near : near + 2]
        low_ref[:, 4 * q + 2 : 4 * q + 4] = edge_ref[part, 4 + near : 6 + near]
    out_ref[first + size_x * 8 : first + size_x * 12] = (
        low_ref[...].reshape(size_x * 4, depth).astype(BF16)
    )


def unpack_waves(buffer_ref, upward, first, size_x, edge_ref, low_ref):
    depth = buffer_ref.shape[1]
    near = 2 if upward else 0
    quarter = size_x // 4
    edge_ref[...] = (
        buffer_ref[first : first + size_x * 8].astype(F32).reshape(size_x, 8, depth)
    )
    low_ref[...] = (
        buffer_ref[first + size_x * 8 : first + size_x * 12]
        .astype(F32)
        .reshape(quarter, 16, depth)
    )
    for q in range(4):
        part = slice(q * quarter, (q + 1) * quarter)
        edge_ref[part, near : near + 2] += low_ref[:, 4 * q : 4 * q + 2]
        edge_ref[part, 4 + near : 6 + near] += low_ref[:, 4 * q + 2 : 4 * q + 4]


def pack_y_body(
    feat_ref, fwd_ref, back_ref, low_ref, high_ref, up_ref, down_ref, plane_ref, edge_ref, rest_ref
):
    channels, size_x, size_y, depth = feat_ref.shape
    row = lax.broadcasted_iota(jnp.int32, (16, depth), 0)
    tails = [jnp.zeros((16, depth), F32), jnp.zeros((16, depth), F32)]
    for c in range(channels):
        plane_ref[...] = feat_ref[c].astype(F32)
        for n, (out_ref, y) in enumerate(((up_ref, size_y - 1), (down_ref, 0))):
            out_ref[c * size_x : (c + 1) * size_x] = plane_ref[:, y, :].astype(BF16)
            tails[n] = jnp.where(row == 2 * c, low_ref[8 + c, y : y + 1, :], tails[n])
            tails[n] = jnp.where(row == 2 * c + 1, high_ref[8 + c, y : y + 1, :], tails[n])
    first = channels * size_x
    for tail, out_ref in zip(tails, (up_ref, down_ref)):
        out_ref[first : first + 16] = tail.astype(BF16)
    pack_waves(fwd_ref, back_ref, True, up_ref, first + 16, edge_ref, rest_ref)
    pack_waves(fwd_ref, back_ref, False, down_ref, first + 16, edge_ref, rest_ref)


def fill_features(ext_ref, feat_ref, low_ref, high_ref):
    channels, size_x = feat_ref.shape[:2]
    for c in range(channels):
        ext_ref[c, 0] = low_ref[8 + c]
        ext_ref[c, 1 : 1 + size_x] = feat_ref[c].astype(F32)
        ext_ref[c, 1 + size_x] = high_ref[8 + c]


def conv_body(feat_ref, low_ref, high_ref, weight_ref, *refs):
    small_in, (total_ref, *small_out), ext_ref = refs[:3], refs[3:7], refs[7]
    for source, target in zip(small_in, small_out):
        target[...] = source[...]
    channels, size_x = feat_ref.shape[:2]
    fill_features(ext_ref, feat_ref, low_ref, high_ref)
    together = 2

    def some_rows(i, carry):
        start = i * together
        terms = [[[None] * 3 for _ in range(3)] for _ in range(together)]
        for c in range(channels):
            inputs = [ext_ref[c, start + r] for r in range(together + 2)]
            for dx in range(3):
                for dy in range(3):
                    for dz in range(3):
                        weight = weight_ref[c, 9 * dx + 3 * dy + dz]
                        for r in range(together):
                            part = weight * inputs[r + dx]
                            old = terms[r][dy][dz]
                            terms[r][dy][dz] = part if old is None else old + part
        for r in range(together):
            total = None
            for dy in range(3):
                part = (
                    terms[r][dy][1]
                    + shifted_lanes(terms[r][dy][0], -1)
                    + shifted_lanes(terms[r][dy][2], 1)
                )
                if dy != 1:
                    part = shifted_rows(part, dy - 1)
                total = part if total is None else total + part
            total_ref[start + r] = total
        return carry

    lax.fori_loop(0, size_x // together, some_rows, 0)


def load_plane(plane_ref, buffer_ref, c, size_x, channels):
    plane_ref[8 : 8 + size_x] = buffer_ref[c * size_x : (c + 1) * size_x].astype(F32)
    tail = buffer_ref[channels * size_x : channels * size_x + 16].astype(F32)
    plane_ref[7:8] = tail[2 * c : 2 * c + 1]
    plane_ref[8 + size_x : 9 + size_x] = tail[2 * c + 1 : 2 * c + 2]


def conv_edge_body(low_ref, high_ref, weight_ref, out_ref, plane_ref):
    size_x = out_ref.shape[0] // 2
    channels = weight_ref.shape[0]
    for side, (buffer_ref, dy) in enumerate(((low_ref, 0), (high_ref, 2))):
        terms = [None] * 3
        for c in range(channels):
            load_plane(plane_ref, buffer_ref, c, size_x, channels)
            for dx in range(3):
                plane = plane_ref[7 + dx : 7 + dx + size_x]
                for dz in range(3):
                    part = weight_ref[c, 9 * dx + 3 * dy + dz] * plane
                    terms[dz] = part if terms[dz] is None else terms[dz] + part
        total = terms[1] + shifted_lanes(terms[0], -1) + shifted_lanes(terms[2], 1)
        out_ref[side * size_x : (side + 1) * size_x] = total


def raw_body(parts_ref, rims_ref, out_ref):
    copies, rows, size_y, depth = parts_ref.shape
    total = parts_ref[0]
    for n in range(1, copies):
        total = total + parts_ref[n]
    first = rows * size_y
    total = total.reshape(first, depth)
    rims = rims_ref[...]
    for n in range(copies):
        out_ref[n, 0:first] = total
        out_ref[n, first:] = rims


def update_body(parts_ref, damping_ref, out_ref):
    count, rows = parts_ref.shape[:2]
    half = rows // 2
    total = parts_ref[0]
    for n in range(1, count):
        total = total + parts_ref[n]
    update = total[:half] / (total[half:] + damping_ref[0])
    for n in range(count):
        out_ref[n] = update


def receiver_hits(receivers_ref, place_ref, plane_y, size_x, size_y):
    shift_y = plane_y.bit_length() - 1
    receivers = receivers_ref[...]
    place_x = lax.shift_right_logical(receivers, shift_y) - place_ref[0]
    place_y = (receivers & (plane_y - 1)) - place_ref[1]
    inside = (place_x >= 0) & (place_x < size_x) & (place_y >= 0) & (place_y < size_y)
    cell = jnp.where(inside, place_x * size_y + place_y, -1)
    cells = lax.broadcasted_iota(jnp.int32, (size_x * size_y, receivers.shape[1]), 0)
    return (cells == cell).astype(F32).astype(BF16)


def exact_product(parts, other, contract, parts_first):
    total = None
    for part in parts:
        pair = (part, other) if parts_first else (other, part)
        product = lax.dot_general(
            *pair, (contract, ((), ())), preferred_element_type=F32
        )
        total = product if total is None else total + product
    return total


def sample(fwd_ref, hit, trace_ref):
    size_x, size_y, depth = fwd_ref.shape
    field = fwd_ref[...].reshape(size_x * size_y, depth)
    total = exact_product(split3(field), hit, ((0,), (0,)), True)
    trace_ref[...] = total[RDEPTH : RDEPTH + 1, :]


def trace_body(plane_y, fwd_ref, place_ref, receivers_ref, trace_ref):
    size_x, size_y, _ = fwd_ref.shape
    sample(fwd_ref, receiver_hits(receivers_ref, place_ref, plane_y, size_x, size_y), trace_ref)


def inner_body(moment, plane_y, *refs):
    fwd_ref, back_ref, fwd_old_ref, back_old_ref = refs[:4]
    place_ref, receivers_ref, residual_ref = refs[4:7]
    refs = refs[7:]
    if moment == 0:
        x_low_ref, x_high_ref = refs[:2]
        refs = refs[2:]
    fwd_ahead_ref, back_ahead_ref, lap_fwd_ref, lap_back_ref = refs[:4]
    refs = refs[4:]
    if moment == 1:
        trace_ref = refs[0]
        refs = refs[1:]
    x_ref, y_ref, inject_ref = refs
    size_x, size_y, depth = fwd_ref.shape
    rows = 4
    hit = receiver_hits(receivers_ref, place_ref, plane_y, size_x, size_y)
    injected = jnp.where(
        lax.broadcasted_iota(jnp.int32, (depth, hit.shape[1]), 0) == RDEPTH,
        residual_ref[0, moment : moment + 1, :],
        0.0,
    )
    inject_ref[...] = exact_product(split3(injected), hit, ((1,), (1,)), False).reshape(
        size_x, size_y, depth
    )
    if moment == 1:
        sample(fwd_ref, hit, trace_ref)
    zero_x = jnp.zeros((4, size_y, depth), F32)
    y_ref[:, 0:8] = jnp.zeros((size_x, 8, depth), F32)
    y_ref[:, 8 + size_y : 16 + size_y] = jnp.zeros((size_x, 8, depth), F32)
    for first, ref, old_ref, ahead_ref, lap_ref in (
        (0, fwd_ref, fwd_old_ref, fwd_ahead_ref, lap_fwd_ref),
        (4, back_ref, back_old_ref, back_ahead_ref, lap_back_ref),
    ):
        x_ref[0:4] = zero_x if moment else x_low_ref[first : first + 4]
        x_ref[4 : 4 + size_x] = ref[...]
        x_ref[4 + size_x : 8 + size_x] = zero_x if moment else x_high_ref[first : first + 4]
        y_ref[:, 8 : 8 + size_y] = ref[...]

        def one_block(i, carry):
            start = i * rows
            here = pl.ds(start, rows)
            centre = ref[here]
            flat = centre.reshape(rows * size_y, depth)
            result = (3.0 * COEFFICIENTS[0]) * centre
            for k in range(1, 5):
                along_x = x_ref[pl.ds(start + 4 + k, rows)] + x_ref[pl.ds(start + 4 - k, rows)]
                along_y = (
                    y_ref[here, 8 + k : 8 + k + size_y, :] + y_ref[here, 8 - k : 8 - k + size_y, :]
                )
                along_z = shifted_lanes(flat, k) + shifted_lanes(flat, -k)
                result = result + COEFFICIENTS[k] * (
                    along_x + along_y + along_z.reshape(centre.shape)
                )
            if first:
                result = result + inject_ref[here]
            lap_ref[here] = result
            ahead_ref[here] = 2.0 * centre - old_ref[here]
            return carry

        lax.fori_loop(0, size_x // rows, one_block, 0)


def step_body(moment, plane_y, *refs):
    fwd_ahead_ref, back_ahead_ref, lap_fwd_ref, lap_back_ref = refs[:4]
    y_low_ref, y_high_ref, place_ref, wavelet_ref = refs[4:8]
    refs = refs[8:]
    if moment == 0:
        raw_ref = refs[0]
        (fwd_new_ref, back_new_ref, lap_ref, squashed_ref) = refs[1:5]
        (x_up_ref, x_down_ref, y_up_ref, y_down_ref) = refs[5:9]
        refs = refs[9:]
        size_x, size_y, depth = squashed_ref.shape
        shots = raw_ref.shape[0]
        rows = size_x // shots
        first = rows * size_y
        rims = None
        for n in range(shots):
            squashed_ref[n * rows : (n + 1) * rows] = raw_ref[n, 0:first].reshape(
                rows, size_y, depth
            )
            part = raw_ref[n, first:]
            rims = part if rims is None else rims + part
        squashed_ref[:, 0:1, :] += rims[:size_x].reshape(size_x, 1, depth)
        squashed_ref[:, size_y - 1 : size_y, :] += rims[size_x:].reshape(size_x, 1, depth)
    else:
        squashed_ref, x_low_ref, x_high_ref, lap_old_ref, back_ref = refs[:5]
        (fwd_new_ref, back_new_ref, sums_ref) = refs[5:8]
        refs = refs[8:]
    edge_ref, rest_ref, *sides = refs
    size_x, size_y, depth = fwd_ahead_ref.shape
    start_row = y_low_ref.shape[0] - wave_rows(size_x)
    for n, (buffer_ref, upward) in enumerate(((y_low_ref, True), (y_high_ref, False))):
        unpack_waves(buffer_ref, upward, start_row, size_x, edge_ref, rest_ref)
        for m in range(2):
            side_ref = sides[2 * m + n]
            at, empty = (4, 8) if upward else (8, 0)
            side_ref[:, empty : empty + 8] = jnp.zeros((size_x, 8, depth), F32)
            side_ref[:, at : at + 4] = edge_ref[:, 4 * m : 4 * m + 4]

    anchor_x, anchor_y, source = place_ref[0], place_ref[1], place_ref[2]
    shift_y = plane_y.bit_length() - 1
    shift_z = depth.bit_length() - 1
    column = lax.shift_right_logical(source, shift_z)
    source_x = lax.shift_right_logical(column, shift_y) - anchor_x
    source_y = (column & (plane_y - 1)) - anchor_y
    source_z = source & (depth - 1)
    here = (source_x >= 0) & (source_x < size_x) & (source_y >= 0) & (source_y < size_y)
    spot = jnp.where(here, (source_x * size_y + source_y) * depth + source_z, -1)
    amplitude = wavelet_ref[0, moment]

    def edges(lap, m, start):
        block = slice(start, start + 4)
        low = high = None
        for k in range(1, 5):
            a = COEFFICIENTS[k] * sides[2 * m][block, 8 - k : 16 - k, :]
            b = COEFFICIENTS[k] * sides[2 * m + 1][block, k : 8 + k, :]
            low, high = (a, b) if low is None else (low + a, high + b)
        parts = [low, high]
        if size_y > 16:
            parts.insert(1, jnp.zeros((4, size_y - 16, depth), F32))
        lap = lap + jnp.concatenate(parts, axis=1)
        if moment == 0 or start not in (0, size_x - 4):
            return lap
        parts = []
        for j in range(4):
            total = None
            if start == 0:
                picks = [(k, x_low_ref, 4 * m + 4 + j - k) for k in range(j + 1, 5)]
            else:
                picks = [(k, x_high_ref, 4 * m + j + k - 4) for k in range(4 - j, 5)]
            for k, ref, row in picks:
                part = COEFFICIENTS[k] * ref[row]
                total = part if total is None else total + part
            parts.append(total)
        return lap + jnp.stack(parts)

    for start in range(0, size_x, 4):
        here = slice(start, start + 4)
        squashed = squashed_ref[here]
        if moment == 0:
            squashed = jax.nn.sigmoid(squashed)
            squashed_ref[here] = squashed
        courant = 0.02 + 0.16 * squashed
        lap_fwd = edges(lap_fwd_ref[here], 0, start)
        lap_back = edges(lap_back_ref[here], 1, start)
        dims = lap_fwd.shape
        index = (
            lax.broadcasted_iota(jnp.int32, dims, 0) * (size_y * depth)
            + lax.broadcasted_iota(jnp.int32, dims, 1) * depth
            + lax.broadcasted_iota(jnp.int32, dims, 2)
        )
        added = jnp.where(index == spot - start * (size_y * depth), amplitude, 0.0)
        fwd_new_ref[here] = fwd_ahead_ref[here] + courant * (lap_fwd + added)
        back_new = back_ahead_ref[here] + courant * lap_back
        back_new_ref[here] = back_new
        if moment == 0:
            lap_ref[here] = lap_fwd
        else:
            rows = sums_ref.shape[1] // 2
            n, at = start // rows, start % rows
            lap_old = lap_old_ref[here]
            sums_ref[n, at : at + 4] = lap_old * back_ref[here] + lap_fwd * back_new
            sums_ref[n, rows + at : rows + at + 4] = lap_old * lap_old + lap_fwd * lap_fwd

    if moment == 0:
        x_up_ref[0:4] = fwd_new_ref[size_x - 4 : size_x]
        x_up_ref[4:8] = back_new_ref[size_x - 4 : size_x]
        x_down_ref[0:4] = fwd_new_ref[0:4]
        x_down_ref[4:8] = back_new_ref[0:4]
        pack_waves(fwd_new_ref, back_new_ref, True, y_up_ref, 0, edge_ref, rest_ref)
        pack_waves(fwd_new_ref, back_new_ref, False, y_down_ref, 0, edge_ref, rest_ref)


def gradient_body(
    update_ref,
    squashed_ref,
    feat_ref,
    x_low_ref,
    x_high_ref,
    y_low_ref,
    y_high_ref,
    first_ref,
    second_ref,
    out_ref,
    left_ref,
    right_ref,
    plane_ref,
    rows_ref,
):
    size_x, size_y, depth = update_ref.shape
    channels = feat_ref.shape[0]
    copies = out_ref.shape[0]
    cells = size_x * size_y

    def one_block(i, carry):
        for j in range(4):
            x = 4 * i + j
            squashed = squashed_ref[x]
            pulled = update_ref[x] * (0.16 * squashed * (1.0 - squashed))
            for dy in range(3):
                moved = pulled if dy == 1 else shifted_rows(pulled, 1 - dy)
                high = moved.astype(BF16)
                left_ref[2 * dy, x] = high
                left_ref[2 * dy + 1, x] = (moved - high.astype(F32)).astype(BF16)
            plane_ref[1, pl.ds(x, 1)] = pulled[0:1, :]
            plane_ref[2, pl.ds(x, 1)] = pulled[size_y - 1 : size_y, :]
        return carry

    lax.fori_loop(0, size_x // 4, one_block, 0)
    for c in range(channels):
        right_ref[0, 0] = x_low_ref[8 + c].astype(BF16)
        right_ref[0, 1:size_x] = feat_ref[c, 0 : size_x - 1]
        right_ref[1] = feat_ref[c]
        right_ref[2, 0 : size_x - 1] = feat_ref[c, 1:size_x]
        right_ref[2, size_x - 1] = x_high_ref[8 + c].astype(BF16)
        right = jnp.concatenate(
            [right_ref[dx].reshape(cells, depth) for dx in range(3)], axis=1
        )
        for dy in range(3):
            left = jnp.concatenate(
                [left_ref[2 * dy + part].reshape(cells, depth) for part in range(2)], axis=1
            )
            product = lax.dot_general(
                left, right, (((0,), (0,)), ((), ())), preferred_element_type=F32
            )
            ahead = lax.broadcasted_iota(jnp.int32, (depth, depth), 1) - (
                lax.broadcasted_iota(jnp.int32, (depth, depth), 0)
            )
            for dx in range(3):
                lanes = slice(dx * depth, (dx + 1) * depth)
                block = product[0:depth, lanes] + product[depth : 2 * depth, lanes]
                for dz in range(3):
                    at = c * 27 + 9 * dx + 3 * dy + dz
                    rows_ref[at : at + 1] = jnp.sum(
                        jnp.where(ahead == dz - 1, block, 0.0), axis=0, keepdims=True
                    )
    at = channels * 27
    rows_ref[at:] = jnp.zeros((rows_ref.shape[0] - at, depth), F32)

    for buffer_ref, dy, which in ((y_low_ref, 0, 1), (y_high_ref, 2, 2)):
        pulled = plane_ref[which, 0:size_x]
        along = [pulled if dz == 1 else shifted_lanes(pulled, 1 - dz) for dz in range(3)]
        for c in range(channels):
            load_plane(plane_ref.at[0], buffer_ref, c, size_x, channels)
            for dx in range(3):
                features = plane_ref[0, 7 + dx : 7 + dx + size_x]
                for dz in range(3):
                    at = c * 27 + 9 * dx + 3 * dy + dz
                    rows_ref[at : at + 1] += jnp.sum(
                        features * along[dz], axis=0, keepdims=True
                    )

    ones = jnp.ones((8, depth), BF16)
    sums = None
    for part in split3(rows_ref[...]):
        product = lax.dot_general(
            ones, part, (((1,), (1,)), ((), ())), preferred_element_type=F32
        )
        sums = product if sums is None else sums + product
    count = first_ref.shape[1]
    for n in range(copies):
        out_ref[n, :, 0:count] = first_ref[...]
        out_ref[n, :, count : 2 * count] = second_ref[...]
        out_ref[n, :, 2 * count : 2 * count + depth] = sums[0:1]


def total_body(shares_ref, trace_ref, grad_ref):
    copies = shares_ref.shape[0]
    count = trace_ref.shape[2]
    channels, offsets = grad_ref.shape
    total = shares_ref[0]
    for n in range(1, copies):
        total = total + shares_ref[n]
    trace_ref[0, 0:1, :] = total[:, 0:count]
    trace_ref[0, 1:2, :] = total[:, count : 2 * count]
    last = total[:, 2 * count :]
    lanes = last.shape[1]
    last = jnp.broadcast_to(last, (8, lanes))
    for c in range(channels):
        turned = last if c == 0 else pltpu.roll(last, lanes - c * offsets, 1)
        grad_ref[c : c + 1, :] = turned[0:1, 0:offsets]


def keep_body(value_ref, out_ref):
    out_ref[...] = value_ref[...]


def neighbours(up, down, axis):
    count = lax.axis_size(axis)
    low = lax.ppermute(up, axis, [(i, i + 1) for i in range(count - 1)])
    high = lax.ppermute(down, axis, [(i + 1, i) for i in range(count - 1)])
    return low, high


def per_device(
    features,
    conv_weight,
    fwd_prev,
    fwd_now,
    back_prev,
    back_now,
    sources,
    wavelet,
    receivers,
    residual,
    damping,
):
    channels, size_x, size_y, depth = features.shape
    shots = lax.axis_size("shot")
    rows = size_x // shots
    count = receivers.shape[1]
    plane_y = size_y * lax.axis_size("gy")
    blocks = lax.axis_size("gx") * lax.axis_size("gy")
    grid = (size_x, size_y, depth)
    fwd_prev, fwd_now, back_prev, back_now = (
        a.reshape(grid) for a in (fwd_prev, fwd_now, back_prev, back_now)
    )
    place = jnp.stack(
        [
            lax.axis_index("gx") * size_x,
            lax.axis_index("gy") * size_y,
            sources[0],
        ]
    ).astype(jnp.int32)

    x_shape = shape(8 + channels, size_y, depth)
    with jax.named_scope("pack_x"):
        x_up, x_down = call(
            pack_x_body,
            [x_shape, x_shape],
            (features, fwd_now, back_now),
            [pl.BlockSpec(memory_space=pltpu.HBM)] * 3,
            scratch=[
                pltpu.VMEM((2 * channels, size_y, depth), BF16),
                pltpu.SemaphoreType.DMA((2 * (2 + channels),)),
            ],
            name="pack_x",
            limit=VMEM_WHOLE,
        )
    with jax.named_scope("halo_x"):
        x_low, x_high = neighbours(x_up, x_down, "gx")
    packing = [
        pltpu.VMEM((size_x, 8, depth), F32),
        pltpu.VMEM((size_x // 4, 16, depth), F32),
    ]
    y_shape = shape(channels * size_x + 16 + wave_rows(size_x), depth, dtype=BF16)
    with jax.named_scope("pack_y"):
        y_up, y_down = call(
            pack_y_body,
            [y_shape, y_shape],
            (features, fwd_now, back_now, x_low, x_high),
            [VM] * 5,
            scratch=[pltpu.VMEM(grid, F32)] + packing,
            name="pack_y",
        )
    with jax.named_scope("halo_y"):
        y_low, y_high = neighbours(y_up, y_down, "gy")
    ext = pltpu.VMEM((channels, size_x + 2, size_y, depth), F32)
    full = shape(*grid)
    inner_scratch = [
        pltpu.VMEM((size_x + 8, size_y, depth), F32),
        pltpu.VMEM((size_x, size_y + 16, depth), F32),
        pltpu.VMEM(grid, F32),
    ]
    step_scratch = packing + [pltpu.VMEM((size_x, 16, depth), F32)] * 4
    work = 60 * size_x * size_y * depth
    with jax.named_scope("inner_1"):
        inner_1 = call(
            functools.partial(inner_body, 0, plane_y),
            [full] * 4,
            (fwd_now, back_now, fwd_prev, back_prev, place, receivers, residual, x_low, x_high),
            [VM] * 4 + [SM] + [VM] * 4,
            scratch=inner_scratch,
            flops=work,
            name="inner_1",
        )
    with jax.named_scope("conv"):
        small = (receivers, residual, wavelet)
        main, receivers, residual, wavelet = call(
            conv_body,
            [full] + [shape(*a.shape, dtype=a.dtype) for a in small],
            (features, x_low, x_high, conv_weight) + small,
            [VM, VM, VM, SM] + [VM] * 3,
            scratch=[ext],
            flops=54 * channels * size_x * size_y * depth,
            name="conv",
        )
    with jax.named_scope("raw"):
        parts = lax.all_to_all(main, "shot", 0, 0, tiled=True)
        y_low, *inner_1 = lax.optimization_barrier((y_low, *inner_1))
        rims = call(
            conv_edge_body,
            [shape(2 * size_x, depth)],
            (y_low, y_high, conv_weight),
            [VM] * 2 + [SM],
            scratch=[pltpu.VMEM((size_x + 16, depth), F32)],
            flops=AHEAD,
            name="conv_edge",
        )
        each = rows * size_y + 2 * size_x
        raw = call(
            raw_body,
            [shape(shots, each, depth)],
            (parts.reshape(shots, rows, size_y, depth), rims),
            [VM] * 2,
            name="raw",
        )
        raw = lax.all_to_all(raw.reshape(shots * each, depth), "shot", 0, 0, tiled=True)
        raw = raw.reshape(shots, each, depth)

    with jax.named_scope("step_1"):
        fwd_1, back_1, lap_1, squashed, x_up, x_down, y_up, y_down = call(
            functools.partial(step_body, 0, plane_y),
            [full] * 4
            + [shape(8, size_y, depth)] * 2
            + [shape(wave_rows(size_x), depth, dtype=BF16)] * 2,
            (
                *inner_1,
                y_low,
                y_high,
                place,
                wavelet,
                raw,
            ),
            [VM] * 6 + [SM] * 2 + [VM],
            scratch=step_scratch,
            name="step_1",
        )
    with jax.named_scope("halo_2"):
        x_low_2, x_high_2 = neighbours(x_up, x_down, "gx")
        y_low_2, y_high_2 = neighbours(y_up, y_down, "gy")
    with jax.named_scope("inner_2"):
        fwd_ahead, back_ahead, lap_fwd, lap_back, trace_1 = call(
            functools.partial(inner_body, 1, plane_y),
            [full] * 4 + [shape(1, count)],
            (fwd_1, back_1, fwd_now, back_now, place, receivers, residual),
            [VM] * 4 + [SM] + [VM] * 2,
            scratch=inner_scratch,
            flops=work,
            name="inner_2",
        )
    with jax.named_scope("step_2"):
        fwd_2, back_2, sums = call(
            functools.partial(step_body, 1, plane_y),
            [full, full, shape(shots, 2 * rows, size_y, depth)],
            (
                fwd_ahead,
                back_ahead,
                lap_fwd,
                lap_back,
                y_low_2,
                y_high_2,
                place,
                wavelet,
                squashed,
                x_low_2,
                x_high_2,
                lap_1,
                back_1,
            ),
            [VM] * 6 + [SM] * 2 + [VM] * 5,
            scratch=step_scratch,
            name="step_2",
        )
    with jax.named_scope("traces"):
        trace_2 = call(
            functools.partial(trace_body, plane_y),
            [shape(1, count)],
            (fwd_2, place, receivers),
            [VM, SM, VM],
            name="trace_2",
        )
    with jax.named_scope("update"):
        sums = lax.all_to_all(
            sums.reshape(shots * 2 * rows, size_y, depth), "shot", 0, 0, tiled=True
        )
        update = call(
            update_body,
            [shape(shots, rows, size_y, depth)],
            (sums.reshape(shots, 2 * rows, size_y, depth), damping),
            [VM, SM],
            name="update",
        )
        update = lax.all_to_all(update.reshape(grid), "shot", 0, 0, tiled=True)
    with jax.named_scope("gradient"):
        share = call(
            gradient_body,
            [shape(blocks, 1, 2 * count + depth)],
            (update, squashed, features, x_low, x_high, y_low, y_high, trace_1, trace_2),
            [VM] * 9,
            scratch=[
                pltpu.VMEM((6,) + grid, BF16),
                pltpu.VMEM((3,) + grid, BF16),
                pltpu.VMEM((3, size_x + 16, depth), F32),
                pltpu.VMEM((128, depth), F32),
            ],
            flops=54 * channels * size_x * size_y * depth,
            name="gradient",
        )
        share, update = lax.optimization_barrier((share, update))
        shares = lax.all_to_all(share, ("gx", "gy"), 0, 0, tiled=True)
        shares = shares.reshape(blocks, 1, 2 * count + depth)
        traces, weight_grad = call(
            total_body,
            [shape(1, 2, count), shape(channels, 27)],
            (shares,),
            [VM],
            name="total",
        )
        update = call(keep_body, [full], (update,), [VM], name="keep")
    return (fwd_2[None], back_2[None], traces, update, weight_grad)


def solution(mesh):
    in_specs = (
        P("shot", "gx", "gy", None),
        P("shot", None),
        P("shot", "gx", "gy", None),
        P("shot", "gx", "gy", None),
        P("shot", "gx", "gy", None),
        P("shot", "gx", "gy", None),
        P("shot"),
        P("shot", None),
        P("shot", None),
        P("shot", None, None),
        P(),
    )
    out_specs = (
        P("shot", "gx", "gy", None),
        P("shot", "gx", "gy", None),
        P("shot", None, None),
        P("gx", "gy", None),
        P("shot", None),
    )
    return jax.shard_map(
        per_device, mesh=mesh, in_specs=in_specs, out_specs=out_specs, check_vma=False
    )
```

```python
import functools

import jax
import jax.numpy as jnp
from jax import lax
from jax.experimental import pallas as pl
from jax.experimental.pallas import tpu as pltpu
from jax.sharding import PartitionSpec as P

RDEPTH = 3
COEFFICIENTS = (-205.0 / 72.0, 8.0 / 5.0, -1.0 / 5.0, 8.0 / 315.0, -1.0 / 560.0)
F32 = jnp.float32
BF16 = jnp.bfloat16
VMEM_LIMIT = 48 * 1024 * 1024
AHEAD = 50_000_000_000
VMEM_WHOLE = 63 * 1024 * 1024

VM = pl.BlockSpec(memory_space=pltpu.VMEM)
SM = pl.BlockSpec(memory_space=pltpu.SMEM)


def call(body, outs, ins, specs, scratch=(), flops=1_000_000, name=None, limit=VMEM_LIMIT):
    moved = sum(a.size * a.dtype.itemsize for a in ins) + sum(
        o.size * jnp.dtype(o.dtype).itemsize for o in outs
    )
    single = len(outs) == 1
    return pl.pallas_call(
        body,
        out_shape=outs[0] if single else tuple(outs),
        in_specs=specs,
        out_specs=VM if single else tuple(VM for _ in outs),
        scratch_shapes=list(scratch),
        compiler_params=pltpu.CompilerParams(vmem_limit_bytes=limit),
        cost_estimate=pl.CostEstimate(flops=flops, bytes_accessed=moved, transcendentals=0),
        name=name,
    )(*ins)


def shape(*dims, dtype=F32):
    return jax.ShapeDtypeStruct(dims, dtype)


def split3(value):
    top = value.astype(BF16)
    rest = value - top.astype(F32)
    middle = rest.astype(BF16)
    low = (rest - middle.astype(F32)).astype(BF16)
    return (top, middle, low)


def shifted_lanes(value, by):
    depth = value.shape[1]
    lane = lax.broadcasted_iota(jnp.int32, value.shape, 1)
    if by > 0:
        return jnp.where(lane < depth - by, pltpu.roll(value, depth - by, 1), 0.0)
    return jnp.where(lane >= -by, pltpu.roll(value, -by, 1), 0.0)


def shifted_rows(value, by):
    count = value.shape[0]
    row = lax.broadcasted_iota(jnp.int32, value.shape, 0)
    if by > 0:
        return jnp.where(row < count - by, pltpu.roll(value, count - by, 0), 0.0)
    return jnp.where(row >= -by, pltpu.roll(value, -by, 0), 0.0)


def pack_x_body(feat_ref, fwd_ref, back_ref, up_ref, down_ref, edge_ref, sems):
    channels, size_x = feat_ref.shape[:2]
    pairs = []
    for n, (out_ref, start, row) in enumerate(
        ((up_ref, size_x - 4, size_x - 1), (down_ref, 0, 0))
    ):
        pairs += [
            (feat_ref.at[:, row], edge_ref.at[n]),
            (fwd_ref.at[pl.ds(start, 4)], out_ref.at[pl.ds(0, 4)]),
            (back_ref.at[pl.ds(start, 4)], out_ref.at[pl.ds(4, 4)]),
        ]
    copies = [
        pltpu.make_async_copy(source, target, sems.at[n])
        for n, (source, target) in enumerate(pairs)
    ]
    for copy in copies:
        copy.start()
    for copy in copies:
        copy.wait()
    up_ref[8 : 8 + channels] = edge_ref[0].astype(F32)
    down_ref[8 : 8 + channels] = edge_ref[1].astype(F32)


def wave_rows(size_x):
    return size_x * 12


def pack_waves(fwd_ref, back_ref, upward, out_ref, first, edge_ref, low_ref):
    size_x, size_y, depth = fwd_ref.shape
    start, near = (size_y - 4, 2) if upward else (0, 0)
    edge_ref[:, 0:4] = fwd_ref[:, start : start + 4]
    edge_ref[:, 4:8] = back_ref[:, start : start + 4]
    value = edge_ref[...].reshape(size_x * 8, depth)
    high = value.astype(BF16)
    out_ref[first : first + size_x * 8] = high
    edge_ref[...] = (value - high.astype(F32)).reshape(size_x, 8, depth)
    quarter = size_x // 4
    for q in range(4):
        part = slice(q * quarter, (q + 1) * quarter)
        low_ref[:, 4 * q : 4 * q + 2] = edge_ref[part, near : near + 2]
        low_ref[:, 4 * q + 2 : 4 * q + 4] = edge_ref[part, 4 + near : 6 + near]
    out_ref[first + size_x * 8 : first + size_x * 12] = (
        low_ref[...].reshape(size_x * 4, depth).astype(BF16)
    )


def unpack_waves(buffer_ref, upward, first, size_x, edge_ref, low_ref):
    depth = buffer_ref.shape[1]
    near = 2 if upward else 0
    quarter = size_x // 4
    edge_ref[...] = (
        buffer_ref[first : first + size_x * 8].astype(F32).reshape(size_x, 8, depth)
    )
    low_ref[...] = (
        buffer_ref[first + size_x * 8 : first + size_x * 12]
        .astype(F32)
        .reshape(quarter, 16, depth)
    )
    for q in range(4):
        part = slice(q * quarter, (q + 1) * quarter)
        edge_ref[part, near : near + 2] += low_ref[:, 4 * q : 4 * q + 2]
        edge_ref[part, 4 + near : 6 + near] += low_ref[:, 4 * q + 2 : 4 * q + 4]


def pack_y_body(feat_ref, fwd_ref, back_ref, up_ref, down_ref, plane_ref, edge_ref, rest_ref):
    channels, size_x, size_y, depth = feat_ref.shape
    first = channels * size_x
    for c in range(channels):
        plane_ref[...] = feat_ref[c].astype(F32)
        for out_ref, y in ((up_ref, size_y - 1), (down_ref, 0)):
            out_ref[c * size_x : (c + 1) * size_x] = plane_ref[:, y, :].astype(BF16)
    for out_ref, upward in ((up_ref, True), (down_ref, False)):
        out_ref[first : first + 16] = jnp.zeros((16, depth), BF16)
        pack_waves(fwd_ref, back_ref, upward, out_ref, first + 16, edge_ref, rest_ref)


def corners_body(up_in_ref, down_in_ref, low_ref, high_ref, up_ref, down_ref):
    size_y, depth = low_ref.shape[1:]
    channels = low_ref.shape[0] - 8
    size_x = (up_ref.shape[0] - 16) // (channels + 12)
    first = channels * size_x
    row = lax.broadcasted_iota(jnp.int32, (16, depth), 0)
    for in_ref, out_ref, y in ((up_in_ref, up_ref, size_y - 1), (down_in_ref, down_ref, 0)):
        out_ref[0:first] = in_ref[0:first]
        out_ref[first + 16 :] = in_ref[first + 16 :]
        tail = jnp.zeros((16, depth), F32)
        for c in range(channels):
            tail = jnp.where(row == 2 * c, low_ref[8 + c, y : y + 1, :], tail)
            tail = jnp.where(row == 2 * c + 1, high_ref[8 + c, y : y + 1, :], tail)
        out_ref[first : first + 16] = tail.astype(BF16)


def fill_features(ext_ref, feat_ref, low_ref, high_ref):
    channels, size_x = feat_ref.shape[:2]
    for c in range(channels):
        ext_ref[c, 0] = low_ref[8 + c]
        ext_ref[c, 1 : 1 + size_x] = feat_ref[c].astype(F32)
        ext_ref[c, 1 + size_x] = high_ref[8 + c]


def conv_body(feat_ref, low_ref, high_ref, weight_ref, *refs):
    small_in, (total_ref, *small_out), ext_ref = refs[:3], refs[3:7], refs[7]
    for source, target in zip(small_in, small_out):
        target[...] = source[...]
    channels, size_x = feat_ref.shape[:2]
    fill_features(ext_ref, feat_ref, low_ref, high_ref)
    together = 2

    def some_rows(i, carry):
        start = i * together
        terms = [[[None] * 3 for _ in range(3)] for _ in range(together)]
        for c in range(channels):
            inputs = [ext_ref[c, start + r] for r in range(together + 2)]
            for dx in range(3):
                for dy in range(3):
                    for dz in range(3):
                        weight = weight_ref[c, 9 * dx + 3 * dy + dz]
                        for r in range(together):
                            part = weight * inputs[r + dx]
                            old = terms[r][dy][dz]
                            terms[r][dy][dz] = part if old is None else old + part
        for r in range(together):
            total = None
            for dy in range(3):
                part = (
                    terms[r][dy][1]
                    + shifted_lanes(terms[r][dy][0], -1)
                    + shifted_lanes(terms[r][dy][2], 1)
                )
                if dy != 1:
                    part = shifted_rows(part, dy - 1)
                total = part if total is None else total + part
            total_ref[start + r] = total
        return carry

    lax.fori_loop(0, size_x // together, some_rows, 0)


def load_plane(plane_ref, buffer_ref, c, size_x, channels):
    plane_ref[8 : 8 + size_x] = buffer_ref[c * size_x : (c + 1) * size_x].astype(F32)
    tail = buffer_ref[channels * size_x : channels * size_x + 16].astype(F32)
    plane_ref[7:8] = tail[2 * c : 2 * c + 1]
    plane_ref[8 + size_x : 9 + size_x] = tail[2 * c + 1 : 2 * c + 2]


def conv_edge_body(low_ref, high_ref, weight_ref, out_ref, plane_ref):
    size_x = out_ref.shape[0] // 2
    channels = weight_ref.shape[0]
    for side, (buffer_ref, dy) in enumerate(((low_ref, 0), (high_ref, 2))):
        terms = [None] * 3
        for c in range(channels):
            load_plane(plane_ref, buffer_ref, c, size_x, channels)
            for dx in range(3):
                plane = plane_ref[7 + dx : 7 + dx + size_x]
                for dz in range(3):
                    part = weight_ref[c, 9 * dx + 3 * dy + dz] * plane
                    terms[dz] = part if terms[dz] is None else terms[dz] + part
        total = terms[1] + shifted_lanes(terms[0], -1) + shifted_lanes(terms[2], 1)
        out_ref[side * size_x : (side + 1) * size_x] = total


def raw_body(parts_ref, rims_ref, out_ref):
    copies, rows, size_y, depth = parts_ref.shape
    total = parts_ref[0]
    for n in range(1, copies):
        total = total + parts_ref[n]
    first = rows * size_y
    total = total.reshape(first, depth)
    rims = rims_ref[...]
    for n in range(copies):
        out_ref[n, 0:first] = total
        out_ref[n, first:] = rims


def update_body(parts_ref, damping_ref, out_ref):
    count, rows = parts_ref.shape[:2]
    half = rows // 2
    total = parts_ref[0]
    for n in range(1, count):
        total = total + parts_ref[n]
    update = total[:half] / (total[half:] + damping_ref[0])
    for n in range(count):
        out_ref[n] = update


def receiver_hits(receivers_ref, place_ref, plane_y, size_x, size_y):
    shift_y = plane_y.bit_length() - 1
    receivers = receivers_ref[...]
    place_x = lax.shift_right_logical(receivers, shift_y) - place_ref[0]
    place_y = (receivers & (plane_y - 1)) - place_ref[1]
    inside = (place_x >= 0) & (place_x < size_x) & (place_y >= 0) & (place_y < size_y)
    cell = jnp.where(inside, place_x * size_y + place_y, -1)
    cells = lax.broadcasted_iota(jnp.int32, (size_x * size_y, receivers.shape[1]), 0)
    return (cells == cell).astype(F32).astype(BF16)


def exact_product(parts, other, contract, parts_first):
    total = None
    for part in parts:
        pair = (part, other) if parts_first else (other, part)
        product = lax.dot_general(
            *pair, (contract, ((), ())), preferred_element_type=F32
        )
        total = product if total is None else total + product
    return total


def sample(fwd_ref, hit, trace_ref):
    size_x, size_y, depth = fwd_ref.shape
    field = fwd_ref[...].reshape(size_x * size_y, depth)
    total = exact_product(split3(field), hit, ((0,), (0,)), True)
    trace_ref[...] = total[RDEPTH : RDEPTH + 1, :]


def trace_body(plane_y, first_ref, second_ref, place_ref, receivers_ref, *out_refs):
    size_x, size_y, _ = first_ref.shape
    hit = receiver_hits(receivers_ref, place_ref, plane_y, size_x, size_y)
    for fwd_ref, trace_ref in zip((first_ref, second_ref), out_refs):
        sample(fwd_ref, hit, trace_ref)


def inner_body(moment, plane_y, *refs):
    fwd_ref, back_ref, fwd_old_ref, back_old_ref = refs[:4]
    size_x, size_y, depth = fwd_ref.shape
    rows = 4
    if moment == 0:
        place_ref, receivers_ref, residual_ref, x_low_ref, x_high_ref = refs[4:9]
        fwd_ahead_ref, back_ahead_ref, lap_fwd_ref, lap_back_ref, later_ref = refs[9:14]
        x_ref, y_ref, inject_ref = refs[14:]
        hit = receiver_hits(receivers_ref, place_ref, plane_y, size_x, size_y)
        for n, out_ref in enumerate((inject_ref, later_ref)):
            injected = jnp.where(
                lax.broadcasted_iota(jnp.int32, (depth, hit.shape[1]), 0) == RDEPTH,
                residual_ref[0, n : n + 1, :],
                0.0,
            )
            out_ref[...] = exact_product(split3(injected), hit, ((1,), (1,)), False).reshape(
                size_x, size_y, depth
            )
    else:
        inject_ref = refs[4]
        fwd_ahead_ref, back_ahead_ref, lap_fwd_ref, lap_back_ref = refs[5:9]
        x_ref, y_ref = refs[9:]
    zero_x = jnp.zeros((4, size_y, depth), F32)
    y_ref[:, 0:8] = jnp.zeros((size_x, 8, depth), F32)
    y_ref[:, 8 + size_y : 16 + size_y] = jnp.zeros((size_x, 8, depth), F32)
    for first, ref, old_ref, ahead_ref, lap_ref in (
        (0, fwd_ref, fwd_old_ref, fwd_ahead_ref, lap_fwd_ref),
        (4, back_ref, back_old_ref, back_ahead_ref, lap_back_ref),
    ):
        x_ref[0:4] = zero_x if moment else x_low_ref[first : first + 4]
        x_ref[4 : 4 + size_x] = ref[...]
        x_ref[4 + size_x : 8 + size_x] = zero_x if moment else x_high_ref[first : first + 4]
        y_ref[:, 8 : 8 + size_y] = ref[...]

        def one_block(i, carry):
            start = i * rows
            here = pl.ds(start, rows)
            centre = ref[here]
            flat = centre.reshape(rows * size_y, depth)
            result = (3.0 * COEFFICIENTS[0]) * centre
            for k in range(1, 5):
                along_x = x_ref[pl.ds(start + 4 + k, rows)] + x_ref[pl.ds(start + 4 - k, rows)]
                along_y = (
                    y_ref[here, 8 + k : 8 + k + size_y, :] + y_ref[here, 8 - k : 8 - k + size_y, :]
                )
                along_z = shifted_lanes(flat, k) + shifted_lanes(flat, -k)
                result = result + COEFFICIENTS[k] * (
                    along_x + along_y + along_z.reshape(centre.shape)
                )
            if first:
                result = result + inject_ref[here]
            lap_ref[here] = result
            ahead_ref[here] = 2.0 * centre - old_ref[here]
            return carry

        lax.fori_loop(0, size_x // rows, one_block, 0)


def step_body(moment, plane_y, *refs):
    fwd_ahead_ref, back_ahead_ref, lap_fwd_ref, lap_back_ref = refs[:4]
    y_low_ref, y_high_ref, place_ref, wavelet_ref = refs[4:8]
    refs = refs[8:]
    if moment == 0:
        raw_ref = refs[0]
        (fwd_new_ref, back_new_ref, lap_ref, squashed_ref) = refs[1:5]
        (x_up_ref, x_down_ref, y_up_ref, y_down_ref) = refs[5:9]
        refs = refs[9:]
        size_x, size_y, depth = squashed_ref.shape
        shots = raw_ref.shape[0]
        rows = size_x // shots
        first = rows * size_y
        rims = None
        for n in range(shots):
            squashed_ref[n * rows : (n + 1) * rows] = raw_ref[n, 0:first].reshape(
                rows, size_y, depth
            )
            part = raw_ref[n, first:]
            rims = part if rims is None else rims + part
        squashed_ref[:, 0:1, :] += rims[:size_x].reshape(size_x, 1, depth)
        squashed_ref[:, size_y - 1 : size_y, :] += rims[size_x:].reshape(size_x, 1, depth)
    else:
        squashed_ref, x_low_ref, x_high_ref, lap_old_ref, back_ref = refs[:5]
        (fwd_new_ref, back_new_ref, sums_ref) = refs[5:8]
        refs = refs[8:]
    edge_ref, rest_ref, *sides = refs
    size_x, size_y, depth = fwd_ahead_ref.shape
    start_row = y_low_ref.shape[0] - wave_rows(size_x)
    for n, (buffer_ref, upward) in enumerate(((y_low_ref, True), (y_high_ref, False))):
        unpack_waves(buffer_ref, upward, start_row, size_x, edge_ref, rest_ref)
        for m in range(2):
            side_ref = sides[2 * m + n]
            at, empty = (4, 8) if upward else (8, 0)
            side_ref[:, empty : empty + 8] = jnp.zeros((size_x, 8, depth), F32)
            side_ref[:, at : at + 4] = edge_ref[:, 4 * m : 4 * m + 4]

    anchor_x, anchor_y, source = place_ref[0], place_ref[1], place_ref[2]
    shift_y = plane_y.bit_length() - 1
    shift_z = depth.bit_length() - 1
    column = lax.shift_right_logical(source, shift_z)
    source_x = lax.shift_right_logical(column, shift_y) - anchor_x
    source_y = (column & (plane_y - 1)) - anchor_y
    source_z = source & (depth - 1)
    here = (source_x >= 0) & (source_x < size_x) & (source_y >= 0) & (source_y < size_y)
    spot = jnp.where(here, (source_x * size_y + source_y) * depth + source_z, -1)
    amplitude = wavelet_ref[0, moment]

    def edges(lap, m, start):
        block = slice(start, start + 4)
        low = high = None
        for k in range(1, 5):
            a = COEFFICIENTS[k] * sides[2 * m][block, 8 - k : 16 - k, :]
            b = COEFFICIENTS[k] * sides[2 * m + 1][block, k : 8 + k, :]
            low, high = (a, b) if low is None else (low + a, high + b)
        parts = [low, high]
        if size_y > 16:
            parts.insert(1, jnp.zeros((4, size_y - 16, depth), F32))
        lap = lap + jnp.concatenate(parts, axis=1)
        if moment == 0 or start not in (0, size_x - 4):
            return lap
        parts = []
        for j in range(4):
            total = None
            if start == 0:
                picks = [(k, x_low_ref, 4 * m + 4 + j - k) for k in range(j + 1, 5)]
            else:
                picks = [(k, x_high_ref, 4 * m + j + k - 4) for k in range(4 - j, 5)]
            for k, ref, row in picks:
                part = COEFFICIENTS[k] * ref[row]
                total = part if total is None else total + part
            parts.append(total)
        return lap + jnp.stack(parts)

    for start in range(0, size_x, 4):
        here = slice(start, start + 4)
        squashed = squashed_ref[here]
        if moment == 0:
            squashed = jax.nn.sigmoid(squashed)
            squashed_ref[here] = squashed
        courant = 0.02 + 0.16 * squashed
        lap_fwd = edges(lap_fwd_ref[here], 0, start)
        lap_back = edges(lap_back_ref[here], 1, start)
        dims = lap_fwd.shape
        index = (
            lax.broadcasted_iota(jnp.int32, dims, 0) * (size_y * depth)
            + lax.broadcasted_iota(jnp.int32, dims, 1) * depth
            + lax.broadcasted_iota(jnp.int32, dims, 2)
        )
        added = jnp.where(index == spot - start * (size_y * depth), amplitude, 0.0)
        fwd_new_ref[here] = fwd_ahead_ref[here] + courant * (lap_fwd + added)
        back_new = back_ahead_ref[here] + courant * lap_back
        back_new_ref[here] = back_new
        if moment == 0:
            lap_ref[here] = lap_fwd
        else:
            rows = sums_ref.shape[1] // 2
            n, at = start // rows, start % rows
            lap_old = lap_old_ref[here]
            sums_ref[n, at : at + 4] = lap_old * back_ref[here] + lap_fwd * back_new
            sums_ref[n, rows + at : rows + at + 4] = lap_old * lap_old + lap_fwd * lap_fwd

    if moment == 0:
        x_up_ref[0:4] = fwd_new_ref[size_x - 4 : size_x]
        x_up_ref[4:8] = back_new_ref[size_x - 4 : size_x]
        x_down_ref[0:4] = fwd_new_ref[0:4]
        x_down_ref[4:8] = back_new_ref[0:4]
        pack_waves(fwd_new_ref, back_new_ref, True, y_up_ref, 0, edge_ref, rest_ref)
        pack_waves(fwd_new_ref, back_new_ref, False, y_down_ref, 0, edge_ref, rest_ref)


def gradient_body(
    update_ref,
    squashed_ref,
    feat_ref,
    x_low_ref,
    x_high_ref,
    y_low_ref,
    y_high_ref,
    first_ref,
    second_ref,
    out_ref,
    left_ref,
    right_ref,
    plane_ref,
    rows_ref,
):
    size_x, size_y, depth = update_ref.shape
    channels = feat_ref.shape[0]
    copies = out_ref.shape[0]
    cells = size_x * size_y

    def one_block(i, carry):
        for j in range(4):
            x = 4 * i + j
            squashed = squashed_ref[x]
            pulled = update_ref[x] * (0.16 * squashed * (1.0 - squashed))
            for dy in range(3):
                moved = pulled if dy == 1 else shifted_rows(pulled, 1 - dy)
                high = moved.astype(BF16)
                left_ref[2 * dy, x] = high
                left_ref[2 * dy + 1, x] = (moved - high.astype(F32)).astype(BF16)
            plane_ref[1, pl.ds(x, 1)] = pulled[0:1, :]
            plane_ref[2, pl.ds(x, 1)] = pulled[size_y - 1 : size_y, :]
        return carry

    lax.fori_loop(0, size_x // 4, one_block, 0)
    for c in range(channels):
        right_ref[0, 0] = x_low_ref[8 + c].astype(BF16)
        right_ref[0, 1:size_x] = feat_ref[c, 0 : size_x - 1]
        right_ref[1] = feat_ref[c]
        right_ref[2, 0 : size_x - 1] = feat_ref[c, 1:size_x]
        right_ref[2, size_x - 1] = x_high_ref[8 + c].astype(BF16)
        right = jnp.concatenate(
            [right_ref[dx].reshape(cells, depth) for dx in range(3)], axis=1
        )
        for dy in range(3):
            left = jnp.concatenate(
                [left_ref[2 * dy + part].reshape(cells, depth) for part in range(2)], axis=1
            )
            product = lax.dot_general(
                left, right, (((0,), (0,)), ((), ())), preferred_element_type=F32
            )
            ahead = lax.broadcasted_iota(jnp.int32, (depth, depth), 1) - (
                lax.broadcasted_iota(jnp.int32, (depth, depth), 0)
            )
            for dx in range(3):
                lanes = slice(dx * depth, (dx + 1) * depth)
                block = product[0:depth, lanes] + product[depth : 2 * depth, lanes]
                for dz in range(3):
                    at = c * 27 + 9 * dx + 3 * dy + dz
                    rows_ref[at : at + 1] = jnp.sum(
                        jnp.where(ahead == dz - 1, block, 0.0), axis=0, keepdims=True
                    )
    at = channels * 27
    rows_ref[at:] = jnp.zeros((rows_ref.shape[0] - at, depth), F32)

    for buffer_ref, dy, which in ((y_low_ref, 0, 1), (y_high_ref, 2, 2)):
        pulled = plane_ref[which, 0:size_x]
        along = [pulled if dz == 1 else shifted_lanes(pulled, 1 - dz) for dz in range(3)]
        for c in range(channels):
            load_plane(plane_ref.at[0], buffer_ref, c, size_x, channels)
            for dx in range(3):
                features = plane_ref[0, 7 + dx : 7 + dx + size_x]
                for dz in range(3):
                    at = c * 27 + 9 * dx + 3 * dy + dz
                    rows_ref[at : at + 1] += jnp.sum(
                        features * along[dz], axis=0, keepdims=True
                    )

    ones = jnp.ones((8, depth), BF16)
    sums = None
    for part in split3(rows_ref[...]):
        product = lax.dot_general(
            ones, part, (((1,), (1,)), ((), ())), preferred_element_type=F32
        )
        sums = product if sums is None else sums + product
    count = first_ref.shape[1]
    for n in range(copies):
        out_ref[n, :, 0:count] = first_ref[...]
        out_ref[n, :, count : 2 * count] = second_ref[...]
        out_ref[n, :, 2 * count : 2 * count + depth] = sums[0:1]


def total_body(shares_ref, trace_ref, grad_ref):
    copies = shares_ref.shape[0]
    count = trace_ref.shape[2]
    channels, offsets = grad_ref.shape
    total = shares_ref[0]
    for n in range(1, copies):
        total = total + shares_ref[n]
    trace_ref[0, 0:1, :] = total[:, 0:count]
    trace_ref[0, 1:2, :] = total[:, count : 2 * count]
    last = total[:, 2 * count :]
    lanes = last.shape[1]
    last = jnp.broadcast_to(last, (8, lanes))
    for c in range(channels):
        turned = last if c == 0 else pltpu.roll(last, lanes - c * offsets, 1)
        grad_ref[c : c + 1, :] = turned[0:1, 0:offsets]


def keep_body(value_ref, out_ref):
    out_ref[...] = value_ref[...]


def neighbours(up, down, axis):
    count = lax.axis_size(axis)
    low = lax.ppermute(up, axis, [(i, i + 1) for i in range(count - 1)])
    high = lax.ppermute(down, axis, [(i + 1, i) for i in range(count - 1)])
    return low, high


def per_device(
    features,
    conv_weight,
    fwd_prev,
    fwd_now,
    back_prev,
    back_now,
    sources,
    wavelet,
    receivers,
    residual,
    damping,
):
    channels, size_x, size_y, depth = features.shape
    shots = lax.axis_size("shot")
    rows = size_x // shots
    count = receivers.shape[1]
    plane_y = size_y * lax.axis_size("gy")
    blocks = lax.axis_size("gx") * lax.axis_size("gy")
    grid = (size_x, size_y, depth)
    fwd_prev, fwd_now, back_prev, back_now = (
        a.reshape(grid) for a in (fwd_prev, fwd_now, back_prev, back_now)
    )
    place = jnp.stack(
        [
            lax.axis_index("gx") * size_x,
            lax.axis_index("gy") * size_y,
            sources[0],
        ]
    ).astype(jnp.int32)

    x_shape = shape(8 + channels, size_y, depth)
    with jax.named_scope("pack_x"):
        x_up, x_down = call(
            pack_x_body,
            [x_shape, x_shape],
            (features, fwd_now, back_now),
            [pl.BlockSpec(memory_space=pltpu.HBM)] * 3,
            scratch=[
                pltpu.VMEM((2, channels, size_y, depth), BF16),
                pltpu.SemaphoreType.DMA((6,)),
            ],
            name="pack_x",
            limit=VMEM_WHOLE,
        )
    packing = [
        pltpu.VMEM((size_x, 8, depth), F32),
        pltpu.VMEM((size_x // 4, 16, depth), F32),
    ]
    y_shape = shape(channels * size_x + 16 + wave_rows(size_x), depth, dtype=BF16)
    with jax.named_scope("pack_y"):
        y_up, y_down = call(
            pack_y_body,
            [y_shape, y_shape],
            (features, fwd_now, back_now),
            [VM] * 3,
            scratch=[pltpu.VMEM(grid, F32)] + packing,
            name="pack_y",
        )
    with jax.named_scope("halo_x"):
        x_low, x_high = neighbours(x_up, x_down, "gx")
    with jax.named_scope("corners"):
        y_up, y_down = call(
            corners_body,
            [y_shape, y_shape],
            (y_up, y_down, x_low, x_high),
            [VM] * 4,
            name="corners",
        )
    with jax.named_scope("halo_y"):
        y_low, y_high = neighbours(y_up, y_down, "gy")
    ext = pltpu.VMEM((channels, size_x + 2, size_y, depth), F32)
    full = shape(*grid)
    inner_scratch = [
        pltpu.VMEM((size_x + 8, size_y, depth), F32),
        pltpu.VMEM((size_x, size_y + 16, depth), F32),
        pltpu.VMEM(grid, F32),
    ]
    step_scratch = packing + [pltpu.VMEM((size_x, 16, depth), F32)] * 4
    work = 60 * size_x * size_y * depth
    with jax.named_scope("inner_1"):
        inner_1 = call(
            functools.partial(inner_body, 0, plane_y),
            [full] * 5,
            (fwd_now, back_now, fwd_prev, back_prev, place, receivers, residual, x_low, x_high),
            [VM] * 4 + [SM] + [VM] * 4,
            scratch=inner_scratch,
            flops=work,
            name="inner_1",
        )
    with jax.named_scope("conv"):
        small = (receivers, residual, wavelet)
        main, receivers, residual, wavelet = call(
            conv_body,
            [full] + [shape(*a.shape, dtype=a.dtype) for a in small],
            (features, x_low, x_high, conv_weight) + small,
            [VM, VM, VM, SM] + [VM] * 3,
            scratch=[ext],
            flops=54 * channels * size_x * size_y * depth,
            name="conv",
        )
    with jax.named_scope("raw"):
        parts = lax.all_to_all(main, "shot", 0, 0, tiled=True)
        y_low, *inner_1 = lax.optimization_barrier((y_low, *inner_1))
        rims = call(
            conv_edge_body,
            [shape(2 * size_x, depth)],
            (y_low, y_high, conv_weight),
            [VM] * 2 + [SM],
            scratch=[pltpu.VMEM((size_x + 16, depth), F32)],
            flops=AHEAD,
            name="conv_edge",
        )
        each = rows * size_y + 2 * size_x
        raw = call(
            raw_body,
            [shape(shots, each, depth)],
            (parts.reshape(shots, rows, size_y, depth), rims),
            [VM] * 2,
            name="raw",
        )
        raw = lax.all_to_all(raw.reshape(shots * each, depth), "shot", 0, 0, tiled=True)
        raw = raw.reshape(shots, each, depth)

    with jax.named_scope("step_1"):
        fwd_1, back_1, lap_1, squashed, x_up, x_down, y_up, y_down = call(
            functools.partial(step_body, 0, plane_y),
            [full] * 4
            + [shape(8, size_y, depth)] * 2
            + [shape(wave_rows(size_x), depth, dtype=BF16)] * 2,
            (
                *inner_1[:4],
                y_low,
                y_high,
                place,
                wavelet,
                raw,
            ),
            [VM] * 6 + [SM] * 2 + [VM],
            scratch=step_scratch,
            name="step_1",
        )
    with jax.named_scope("halo_2"):
        x_low_2, x_high_2 = neighbours(x_up, x_down, "gx")
        y_low_2, y_high_2 = neighbours(y_up, y_down, "gy")
    with jax.named_scope("inner_2"):
        fwd_ahead, back_ahead, lap_fwd, lap_back = call(
            functools.partial(inner_body, 1, plane_y),
            [full] * 4,
            (fwd_1, back_1, fwd_now, back_now, inner_1[4]),
            [VM] * 5,
            scratch=inner_scratch[:2],
            flops=work,
            name="inner_2",
        )
    with jax.named_scope("step_2"):
        fwd_2, back_2, sums = call(
            functools.partial(step_body, 1, plane_y),
            [full, full, shape(shots, 2 * rows, size_y, depth)],
            (
                fwd_ahead,
                back_ahead,
                lap_fwd,
                lap_back,
                y_low_2,
                y_high_2,
                place,
                wavelet,
                squashed,
                x_low_2,
                x_high_2,
                lap_1,
                back_1,
            ),
            [VM] * 6 + [SM] * 2 + [VM] * 5,
            scratch=step_scratch,
            name="step_2",
        )
    with jax.named_scope("traces"):
        trace_1, trace_2 = call(
            functools.partial(trace_body, plane_y),
            [shape(1, count)] * 2,
            (fwd_1, fwd_2, place, receivers),
            [VM, VM, SM, VM],
            name="traces",
        )
    with jax.named_scope("update"):
        sums = lax.all_to_all(
            sums.reshape(shots * 2 * rows, size_y, depth), "shot", 0, 0, tiled=True
        )
        update = call(
            update_body,
            [shape(shots, rows, size_y, depth)],
            (sums.reshape(shots, 2 * rows, size_y, depth), damping),
            [VM, SM],
            name="update",
        )
        update = lax.all_to_all(update.reshape(grid), "shot", 0, 0, tiled=True)
    with jax.named_scope("gradient"):
        share = call(
            gradient_body,
            [shape(blocks, 1, 2 * count + depth)],
            (update, squashed, features, x_low, x_high, y_low, y_high, trace_1, trace_2),
            [VM] * 9,
            scratch=[
                pltpu.VMEM((6,) + grid, BF16),
                pltpu.VMEM((3,) + grid, BF16),
                pltpu.VMEM((3, size_x + 16, depth), F32),
                pltpu.VMEM((128, depth), F32),
            ],
            flops=54 * channels * size_x * size_y * depth,
            name="gradient",
        )
        share, update = lax.optimization_barrier((share, update))
        shares = lax.all_to_all(share, ("gx", "gy"), 0, 0, tiled=True)
        shares = shares.reshape(blocks, 1, 2 * count + depth)
        traces, weight_grad = call(
            total_body,
            [shape(1, 2, count), shape(channels, 27)],
            (shares,),
            [VM],
            name="total",
        )
        update = call(keep_body, [full], (update,), [VM], name="keep")
    return (fwd_2[None], back_2[None], traces, update, weight_grad)


def solution(mesh):
    in_specs = (
        P("shot", "gx", "gy", None),
        P("shot", None),
        P("shot", "gx", "gy", None),
        P("shot", "gx", "gy", None),
        P("shot", "gx", "gy", None),
        P("shot", "gx", "gy", None),
        P("shot"),
        P("shot", None),
        P("shot", None),
        P("shot", None, None),
        P(),
    )
    out_specs = (
        P("shot", "gx", "gy", None),
        P("shot", "gx", "gy", None),
        P("shot", None, None),
        P("gx", "gy", None),
        P("shot", None),
    )
    return jax.shard_map(
        per_device, mesh=mesh, in_specs=in_specs, out_specs=out_specs, check_vma=False
    )
```

```python
import functools

import jax
import jax.numpy as jnp
from jax import lax
from jax.experimental import pallas as pl
from jax.experimental.pallas import tpu as pltpu
from jax.sharding import PartitionSpec as P

RDEPTH = 3
COEFFICIENTS = (-205.0 / 72.0, 8.0 / 5.0, -1.0 / 5.0, 8.0 / 315.0, -1.0 / 560.0)
F32 = jnp.float32
BF16 = jnp.bfloat16
VMEM_LIMIT = 48 * 1024 * 1024
AHEAD = 50_000_000_000
VMEM_WHOLE = 63 * 1024 * 1024

VM = pl.BlockSpec(memory_space=pltpu.VMEM)
SM = pl.BlockSpec(memory_space=pltpu.SMEM)


def call(
    body,
    outs,
    ins,
    specs,
    scratch=(),
    flops=1_000_000,
    name=None,
    limit=VMEM_LIMIT,
):
    moved = sum(a.size * a.dtype.itemsize for a in ins) + sum(
        o.size * jnp.dtype(o.dtype).itemsize for o in outs
    )
    single = len(outs) == 1
    return pl.pallas_call(
        body,
        out_shape=outs[0] if single else tuple(outs),
        in_specs=specs,
        out_specs=VM if single else tuple(VM for _ in outs),
        scratch_shapes=list(scratch),
        compiler_params=pltpu.CompilerParams(vmem_limit_bytes=limit),
        cost_estimate=pl.CostEstimate(flops=flops, bytes_accessed=moved, transcendentals=0),
        name=name,
    )(*ins)


def shape(*dims, dtype=F32):
    return jax.ShapeDtypeStruct(dims, dtype)


def split3(value):
    top = value.astype(BF16)
    rest = value - top.astype(F32)
    middle = rest.astype(BF16)
    low = (rest - middle.astype(F32)).astype(BF16)
    return (top, middle, low)


def shifted_lanes(value, by):
    depth = value.shape[1]
    lane = lax.broadcasted_iota(jnp.int32, value.shape, 1)
    if by > 0:
        return jnp.where(lane < depth - by, pltpu.roll(value, depth - by, 1), 0.0)
    return jnp.where(lane >= -by, pltpu.roll(value, -by, 1), 0.0)


def shifted_rows(value, by):
    count = value.shape[0]
    row = lax.broadcasted_iota(jnp.int32, value.shape, 0)
    if by > 0:
        return jnp.where(row < count - by, pltpu.roll(value, count - by, 0), 0.0)
    return jnp.where(row >= -by, pltpu.roll(value, -by, 0), 0.0)


def pack_x_body(feat_ref, fwd_ref, back_ref, up_ref, down_ref, edge_ref, sems):
    channels, size_x = feat_ref.shape[:2]
    pairs = []
    for n, (out_ref, start, row) in enumerate(
        ((up_ref, size_x - 4, size_x - 1), (down_ref, 0, 0))
    ):
        pairs += [
            (feat_ref.at[:, row], edge_ref.at[n]),
            (fwd_ref.at[pl.ds(start, 4)], out_ref.at[pl.ds(0, 4)]),
            (back_ref.at[pl.ds(start, 4)], out_ref.at[pl.ds(4, 4)]),
        ]
    copies = [
        pltpu.make_async_copy(source, target, sems.at[n])
        for n, (source, target) in enumerate(pairs)
    ]
    for copy in copies:
        copy.start()
    for copy in copies:
        copy.wait()
    up_ref[8 : 8 + channels] = edge_ref[0].astype(F32)
    down_ref[8 : 8 + channels] = edge_ref[1].astype(F32)


def wave_rows(size_x):
    return size_x * 12


def pack_waves(fwd_ref, back_ref, upward, out_ref, first, edge_ref, low_ref):
    size_x, size_y, depth = fwd_ref.shape
    start, near = (size_y - 4, 2) if upward else (0, 0)
    edge_ref[:, 0:4] = fwd_ref[:, start : start + 4]
    edge_ref[:, 4:8] = back_ref[:, start : start + 4]
    value = edge_ref[...].reshape(size_x * 8, depth)
    high = value.astype(BF16)
    out_ref[first : first + size_x * 8] = high
    edge_ref[...] = (value - high.astype(F32)).reshape(size_x, 8, depth)
    quarter = size_x // 4
    for q in range(4):
        part = slice(q * quarter, (q + 1) * quarter)
        low_ref[:, 4 * q : 4 * q + 2] = edge_ref[part, near : near + 2]
        low_ref[:, 4 * q + 2 : 4 * q + 4] = edge_ref[part, 4 + near : 6 + near]
    out_ref[first + size_x * 8 : first + size_x * 12] = (
        low_ref[...].reshape(size_x * 4, depth).astype(BF16)
    )


def unpack_waves(buffer_ref, upward, first, size_x, edge_ref, low_ref):
    depth = buffer_ref.shape[1]
    near = 2 if upward else 0
    quarter = size_x // 4
    edge_ref[...] = (
        buffer_ref[first : first + size_x * 8].astype(F32).reshape(size_x, 8, depth)
    )
    low_ref[...] = (
        buffer_ref[first + size_x * 8 : first + size_x * 12]
        .astype(F32)
        .reshape(quarter, 16, depth)
    )
    for q in range(4):
        part = slice(q * quarter, (q + 1) * quarter)
        edge_ref[part, near : near + 2] += low_ref[:, 4 * q : 4 * q + 2]
        edge_ref[part, 4 + near : 6 + near] += low_ref[:, 4 * q + 2 : 4 * q + 4]


def pack_y_body(feat_ref, fwd_ref, back_ref, up_ref, down_ref, plane_ref, edge_ref, rest_ref):
    channels, size_x, size_y, depth = feat_ref.shape
    first = channels * size_x
    for c in range(channels):
        plane_ref[...] = feat_ref[c].astype(F32)
        for out_ref, y in ((up_ref, size_y - 1), (down_ref, 0)):
            out_ref[c * size_x : (c + 1) * size_x] = plane_ref[:, y, :].astype(BF16)
    for out_ref, upward in ((up_ref, True), (down_ref, False)):
        out_ref[first : first + 16] = jnp.zeros((16, depth), BF16)
        pack_waves(fwd_ref, back_ref, upward, out_ref, first + 16, edge_ref, rest_ref)


def corners_body(up_in_ref, down_in_ref, low_ref, high_ref, up_ref, down_ref):
    size_y, depth = low_ref.shape[1:]
    channels = low_ref.shape[0] - 8
    size_x = (up_ref.shape[0] - 16) // (channels + 12)
    first = channels * size_x
    row = lax.broadcasted_iota(jnp.int32, (16, depth), 0)
    for in_ref, out_ref, y in ((up_in_ref, up_ref, size_y - 1), (down_in_ref, down_ref, 0)):
        out_ref[0:first] = in_ref[0:first]
        out_ref[first + 16 :] = in_ref[first + 16 :]
        tail = jnp.zeros((16, depth), F32)
        for c in range(channels):
            tail = jnp.where(row == 2 * c, low_ref[8 + c, y : y + 1, :], tail)
            tail = jnp.where(row == 2 * c + 1, high_ref[8 + c, y : y + 1, :], tail)
        out_ref[first : first + 16] = tail.astype(BF16)


def fill_features(ext_ref, feat_ref, low_ref, high_ref):
    channels, size_x = feat_ref.shape[:2]
    for c in range(channels):
        ext_ref[c, 0] = low_ref[8 + c]
        ext_ref[c, 1 : 1 + size_x] = feat_ref[c].astype(F32)
        ext_ref[c, 1 + size_x] = high_ref[8 + c]


def conv_body(feat_ref, low_ref, high_ref, weight_ref, total_ref, ext_ref):
    channels, size_x = feat_ref.shape[:2]
    fill_features(ext_ref, feat_ref, low_ref, high_ref)
    together = 2

    def some_rows(i, carry):
        start = i * together
        terms = [[[None] * 3 for _ in range(3)] for _ in range(together)]
        for c in range(channels):
            inputs = [ext_ref[c, start + r] for r in range(together + 2)]
            for dx in range(3):
                for dy in range(3):
                    for dz in range(3):
                        weight = weight_ref[c, 9 * dx + 3 * dy + dz]
                        for r in range(together):
                            part = weight * inputs[r + dx]
                            old = terms[r][dy][dz]
                            terms[r][dy][dz] = part if old is None else old + part
        for r in range(together):
            total = None
            for dy in range(3):
                part = (
                    terms[r][dy][1]
                    + shifted_lanes(terms[r][dy][0], -1)
                    + shifted_lanes(terms[r][dy][2], 1)
                )
                if dy != 1:
                    part = shifted_rows(part, dy - 1)
                total = part if total is None else total + part
            total_ref[start + r] = total
        return carry

    lax.fori_loop(0, size_x // together, some_rows, 0)


def load_plane(plane_ref, buffer_ref, c, size_x, channels):
    plane_ref[8 : 8 + size_x] = buffer_ref[c * size_x : (c + 1) * size_x].astype(F32)
    tail = buffer_ref[channels * size_x : channels * size_x + 16].astype(F32)
    plane_ref[7:8] = tail[2 * c : 2 * c + 1]
    plane_ref[8 + size_x : 9 + size_x] = tail[2 * c + 1 : 2 * c + 2]


def conv_edge_body(low_ref, high_ref, weight_ref, out_ref, plane_ref):
    size_x = out_ref.shape[0] // 2
    channels = weight_ref.shape[0]
    for side, (buffer_ref, dy) in enumerate(((low_ref, 0), (high_ref, 2))):
        terms = [None] * 3
        for c in range(channels):
            held_ref = plane_ref.at[side * channels + c]
            load_plane(held_ref, buffer_ref, c, size_x, channels)
            for dx in range(3):
                plane = held_ref[7 + dx : 7 + dx + size_x]
                for dz in range(3):
                    part = weight_ref[c, 9 * dx + 3 * dy + dz] * plane
                    terms[dz] = part if terms[dz] is None else terms[dz] + part
        total = terms[1] + shifted_lanes(terms[0], -1) + shifted_lanes(terms[2], 1)
        out_ref[side * size_x : (side + 1) * size_x] = total


def raw_body(parts_ref, rims_ref, out_ref):
    copies, rows, size_y, depth = parts_ref.shape
    total = parts_ref[0]
    for n in range(1, copies):
        total = total + parts_ref[n]
    first = rows * size_y
    total = total.reshape(first, depth)
    rims = rims_ref[...]
    for n in range(copies):
        out_ref[n, 0:first] = total
        out_ref[n, first:] = rims


def update_body(parts_ref, damping_ref, out_ref):
    count, rows = parts_ref.shape[:2]
    half = rows // 2
    total = parts_ref[0]
    for n in range(1, count):
        total = total + parts_ref[n]
    update = total[:half] / (total[half:] + damping_ref[0])
    for n in range(count):
        out_ref[n] = update


def receiver_hits(receivers_ref, place_ref, plane_y, size_x, size_y):
    shift_y = plane_y.bit_length() - 1
    receivers = receivers_ref[...]
    place_x = lax.shift_right_logical(receivers, shift_y) - place_ref[0]
    place_y = (receivers & (plane_y - 1)) - place_ref[1]
    inside = (place_x >= 0) & (place_x < size_x) & (place_y >= 0) & (place_y < size_y)
    cell = jnp.where(inside, place_x * size_y + place_y, -1)
    cells = lax.broadcasted_iota(jnp.int32, (size_x * size_y, receivers.shape[1]), 0)
    return (cells == cell).astype(F32).astype(BF16)


def exact_product(parts, other, contract, parts_first):
    total = None
    for part in parts:
        pair = (part, other) if parts_first else (other, part)
        product = lax.dot_general(
            *pair, (contract, ((), ())), preferred_element_type=F32
        )
        total = product if total is None else total + product
    return total


def sample(fwd_ref, hit, trace_ref):
    size_x, size_y, depth = fwd_ref.shape
    field = fwd_ref[...].reshape(size_x * size_y, depth)
    total = exact_product(split3(field), hit, ((0,), (0,)), True)
    trace_ref[...] = total[RDEPTH : RDEPTH + 1, :]


def trace_body(plane_y, first_ref, second_ref, place_ref, receivers_ref, *out_refs):
    size_x, size_y, _ = first_ref.shape
    hit = receiver_hits(receivers_ref, place_ref, plane_y, size_x, size_y)
    for fwd_ref, trace_ref in zip((first_ref, second_ref), out_refs):
        sample(fwd_ref, hit, trace_ref)


def inner_body(moment, plane_y, *refs):
    fwd_ref, back_ref, fwd_old_ref, back_old_ref = refs[:4]
    size_x, size_y, depth = fwd_ref.shape
    rows = 4
    if moment == 0:
        place_ref, receivers_ref, residual_ref, wavelet_ref, x_low_ref, x_high_ref = refs[4:10]
        fwd_ahead_ref, back_ahead_ref, lap_fwd_ref, lap_back_ref = refs[10:14]
        later_ref, wavelet_out_ref, x_ref, y_ref, inject_ref = refs[14:]
        wavelet_out_ref[...] = wavelet_ref[...]
        hit = receiver_hits(receivers_ref, place_ref, plane_y, size_x, size_y)
        for n, out_ref in enumerate((inject_ref, later_ref)):
            injected = jnp.where(
                lax.broadcasted_iota(jnp.int32, (depth, hit.shape[1]), 0) == RDEPTH,
                residual_ref[0, n : n + 1, :],
                0.0,
            )
            out_ref[...] = exact_product(split3(injected), hit, ((1,), (1,)), False).reshape(
                size_x, size_y, depth
            )
    else:
        inject_ref = refs[4]
        fwd_ahead_ref, back_ahead_ref, lap_fwd_ref, lap_back_ref = refs[5:9]
        x_ref, y_ref = refs[9:]
    zero_x = jnp.zeros((4, size_y, depth), F32)
    y_ref[:, 0:8] = jnp.zeros((size_x, 8, depth), F32)
    y_ref[:, 8 + size_y : 16 + size_y] = jnp.zeros((size_x, 8, depth), F32)
    for first, ref, old_ref, ahead_ref, lap_ref in (
        (0, fwd_ref, fwd_old_ref, fwd_ahead_ref, lap_fwd_ref),
        (4, back_ref, back_old_ref, back_ahead_ref, lap_back_ref),
    ):
        x_ref[0:4] = zero_x if moment else x_low_ref[first : first + 4]
        x_ref[4 : 4 + size_x] = ref[...]
        x_ref[4 + size_x : 8 + size_x] = zero_x if moment else x_high_ref[first : first + 4]
        y_ref[:, 8 : 8 + size_y] = ref[...]

        def one_block(i, carry):
            start = i * rows
            here = pl.ds(start, rows)
            centre = ref[here]
            flat = centre.reshape(rows * size_y, depth)
            result = (3.0 * COEFFICIENTS[0]) * centre
            for k in range(1, 5):
                along_x = x_ref[pl.ds(start + 4 + k, rows)] + x_ref[pl.ds(start + 4 - k, rows)]
                along_y = (
                    y_ref[here, 8 + k : 8 + k + size_y, :] + y_ref[here, 8 - k : 8 - k + size_y, :]
                )
                along_z = shifted_lanes(flat, k) + shifted_lanes(flat, -k)
                result = result + COEFFICIENTS[k] * (
                    along_x + along_y + along_z.reshape(centre.shape)
                )
            if first:
                result = result + inject_ref[here]
            lap_ref[here] = result
            ahead_ref[here] = 2.0 * centre - old_ref[here]
            return carry

        lax.fori_loop(0, size_x // rows, one_block, 0)


def step_body(moment, plane_y, *refs):
    fwd_ahead_ref, back_ahead_ref, lap_fwd_ref, lap_back_ref = refs[:4]
    y_low_ref, y_high_ref, place_ref, wavelet_ref = refs[4:8]
    refs = refs[8:]
    if moment == 0:
        raw_ref = refs[0]
        (fwd_new_ref, back_new_ref, lap_ref, squashed_ref) = refs[1:5]
        (x_up_ref, x_down_ref, y_up_ref, y_down_ref) = refs[5:9]
        refs = refs[9:]
        size_x, size_y, depth = squashed_ref.shape
        shots = raw_ref.shape[0]
        rows = size_x // shots
        first = rows * size_y
        rims = None
        for n in range(shots):
            squashed_ref[n * rows : (n + 1) * rows] = raw_ref[n, 0:first].reshape(
                rows, size_y, depth
            )
            part = raw_ref[n, first:]
            rims = part if rims is None else rims + part
        squashed_ref[:, 0:1, :] += rims[:size_x].reshape(size_x, 1, depth)
        squashed_ref[:, size_y - 1 : size_y, :] += rims[size_x:].reshape(size_x, 1, depth)
    else:
        squashed_ref, x_low_ref, x_high_ref, lap_old_ref, back_ref = refs[:5]
        (fwd_new_ref, back_new_ref, sums_ref) = refs[5:8]
        refs = refs[8:]
    edge_ref, rest_ref, *sides = refs
    size_x, size_y, depth = fwd_ahead_ref.shape
    start_row = y_low_ref.shape[0] - wave_rows(size_x)
    for n, (buffer_ref, upward) in enumerate(((y_low_ref, True), (y_high_ref, False))):
        unpack_waves(buffer_ref, upward, start_row, size_x, edge_ref, rest_ref)
        for m in range(2):
            side_ref = sides[2 * m + n]
            at, empty = (4, 8) if upward else (8, 0)
            side_ref[:, empty : empty + 8] = jnp.zeros((size_x, 8, depth), F32)
            side_ref[:, at : at + 4] = edge_ref[:, 4 * m : 4 * m + 4]

    anchor_x, anchor_y, source = place_ref[0], place_ref[1], place_ref[2]
    shift_y = plane_y.bit_length() - 1
    shift_z = depth.bit_length() - 1
    column = lax.shift_right_logical(source, shift_z)
    source_x = lax.shift_right_logical(column, shift_y) - anchor_x
    source_y = (column & (plane_y - 1)) - anchor_y
    source_z = source & (depth - 1)
    here = (source_x >= 0) & (source_x < size_x) & (source_y >= 0) & (source_y < size_y)
    spot = jnp.where(here, (source_x * size_y + source_y) * depth + source_z, -1)
    amplitude = wavelet_ref[0, moment]

    def edges(lap, m, start):
        block = slice(start, start + 4)
        low = high = None
        for k in range(1, 5):
            a = COEFFICIENTS[k] * sides[2 * m][block, 8 - k : 16 - k, :]
            b = COEFFICIENTS[k] * sides[2 * m + 1][block, k : 8 + k, :]
            low, high = (a, b) if low is None else (low + a, high + b)
        parts = [low, high]
        if size_y > 16:
            parts.insert(1, jnp.zeros((4, size_y - 16, depth), F32))
        lap = lap + jnp.concatenate(parts, axis=1)
        if moment == 0 or start not in (0, size_x - 4):
            return lap
        parts = []
        for j in range(4):
            total = None
            if start == 0:
                picks = [(k, x_low_ref, 4 * m + 4 + j - k) for k in range(j + 1, 5)]
            else:
                picks = [(k, x_high_ref, 4 * m + j + k - 4) for k in range(4 - j, 5)]
            for k, ref, row in picks:
                part = COEFFICIENTS[k] * ref[row]
                total = part if total is None else total + part
            parts.append(total)
        return lap + jnp.stack(parts)

    for start in range(0, size_x, 4):
        here = slice(start, start + 4)
        squashed = squashed_ref[here]
        if moment == 0:
            squashed = jax.nn.sigmoid(squashed)
            squashed_ref[here] = squashed
        courant = 0.02 + 0.16 * squashed
        lap_fwd = edges(lap_fwd_ref[here], 0, start)
        lap_back = edges(lap_back_ref[here], 1, start)
        dims = lap_fwd.shape
        index = (
            lax.broadcasted_iota(jnp.int32, dims, 0) * (size_y * depth)
            + lax.broadcasted_iota(jnp.int32, dims, 1) * depth
            + lax.broadcasted_iota(jnp.int32, dims, 2)
        )
        added = jnp.where(index == spot - start * (size_y * depth), amplitude, 0.0)
        fwd_new_ref[here] = fwd_ahead_ref[here] + courant * (lap_fwd + added)
        back_new = back_ahead_ref[here] + courant * lap_back
        back_new_ref[here] = back_new
        if moment == 0:
            lap_ref[here] = lap_fwd
        else:
            rows = sums_ref.shape[1] // 2
            n, at = start // rows, start % rows
            lap_old = lap_old_ref[here]
            sums_ref[n, at : at + 4] = lap_old * back_ref[here] + lap_fwd * back_new
            sums_ref[n, rows + at : rows + at + 4] = lap_old * lap_old + lap_fwd * lap_fwd

    if moment == 0:
        x_up_ref[0:4] = fwd_new_ref[size_x - 4 : size_x]
        x_up_ref[4:8] = back_new_ref[size_x - 4 : size_x]
        x_down_ref[0:4] = fwd_new_ref[0:4]
        x_down_ref[4:8] = back_new_ref[0:4]
        pack_waves(fwd_new_ref, back_new_ref, True, y_up_ref, 0, edge_ref, rest_ref)
        pack_waves(fwd_new_ref, back_new_ref, False, y_down_ref, 0, edge_ref, rest_ref)


def gradient_body(
    update_ref,
    squashed_ref,
    feat_ref,
    x_low_ref,
    x_high_ref,
    y_low_ref,
    y_high_ref,
    first_ref,
    second_ref,
    out_ref,
    left_ref,
    right_ref,
    plane_ref,
    rows_ref,
):
    size_x, size_y, depth = update_ref.shape
    channels = feat_ref.shape[0]
    copies = out_ref.shape[0]
    cells = size_x * size_y

    def one_block(i, carry):
        for j in range(4):
            x = 4 * i + j
            squashed = squashed_ref[x]
            pulled = update_ref[x] * (0.16 * squashed * (1.0 - squashed))
            for dy in range(3):
                moved = pulled if dy == 1 else shifted_rows(pulled, 1 - dy)
                high = moved.astype(BF16)
                left_ref[2 * dy, x] = high
                left_ref[2 * dy + 1, x] = (moved - high.astype(F32)).astype(BF16)
            plane_ref[1, pl.ds(x, 1)] = pulled[0:1, :]
            plane_ref[2, pl.ds(x, 1)] = pulled[size_y - 1 : size_y, :]
        return carry

    lax.fori_loop(0, size_x // 4, one_block, 0)
    last = cells - size_y
    for c in range(channels):
        lanes = [slice((3 * c + dx) * depth, (3 * c + dx + 1) * depth) for dx in range(3)]
        own = feat_ref[c].reshape(cells, depth)
        right_ref[0:size_y, lanes[0]] = x_low_ref[8 + c].astype(BF16)
        right_ref[size_y:cells, lanes[0]] = own[0:last]
        right_ref[:, lanes[1]] = own
        right_ref[0:last, lanes[2]] = own[size_y:cells]
        right_ref[last:cells, lanes[2]] = x_high_ref[8 + c].astype(BF16)
    ahead = lax.broadcasted_iota(jnp.int32, (depth, depth), 1) - (
        lax.broadcasted_iota(jnp.int32, (depth, depth), 0)
    )
    for dy in range(3):
        left = jnp.concatenate(
            [left_ref[2 * dy + part].reshape(cells, depth) for part in range(2)], axis=1
        )
        product = lax.dot_general(
            left, right_ref[...], (((0,), (0,)), ((), ())), preferred_element_type=F32
        )
        for c in range(channels):
            for dx in range(3):
                lanes = slice((3 * c + dx) * depth, (3 * c + dx + 1) * depth)
                block = product[0:depth, lanes] + product[depth : 2 * depth, lanes]
                for dz in range(3):
                    at = c * 27 + 9 * dx + 3 * dy + dz
                    rows_ref[at : at + 1] = jnp.sum(
                        jnp.where(ahead == dz - 1, block, 0.0), axis=0, keepdims=True
                    )
    at = channels * 27
    rows_ref[at:] = jnp.zeros((rows_ref.shape[0] - at, depth), F32)

    for buffer_ref, dy, which in ((y_low_ref, 0, 1), (y_high_ref, 2, 2)):
        pulled = plane_ref[which, 0:size_x]
        along = [pulled if dz == 1 else shifted_lanes(pulled, 1 - dz) for dz in range(3)]
        for c in range(channels):
            load_plane(plane_ref.at[0], buffer_ref, c, size_x, channels)
            for dx in range(3):
                features = plane_ref[0, 7 + dx : 7 + dx + size_x]
                for dz in range(3):
                    at = c * 27 + 9 * dx + 3 * dy + dz
                    rows_ref[at : at + 1] += jnp.sum(
                        features * along[dz], axis=0, keepdims=True
                    )

    ones = jnp.ones((8, depth), BF16)
    sums = None
    for part in split3(rows_ref[...]):
        product = lax.dot_general(
            ones, part, (((1,), (1,)), ((), ())), preferred_element_type=F32
        )
        sums = product if sums is None else sums + product
    count = first_ref.shape[1]
    for n in range(copies):
        out_ref[n, :, 0:count] = first_ref[...]
        out_ref[n, :, count : 2 * count] = second_ref[...]
        out_ref[n, :, 2 * count : 2 * count + depth] = sums[0:1]


def total_body(shares_ref, trace_ref, grad_ref):
    copies = shares_ref.shape[0]
    count = trace_ref.shape[2]
    channels, offsets = grad_ref.shape
    total = shares_ref[0]
    for n in range(1, copies):
        total = total + shares_ref[n]
    trace_ref[0, 0:1, :] = total[:, 0:count]
    trace_ref[0, 1:2, :] = total[:, count : 2 * count]
    last = total[:, 2 * count :]
    lanes = last.shape[1]
    last = jnp.broadcast_to(last, (8, lanes))
    for c in range(channels):
        turned = last if c == 0 else pltpu.roll(last, lanes - c * offsets, 1)
        grad_ref[c : c + 1, :] = turned[0:1, 0:offsets]


def keep_body(value_ref, out_ref):
    out_ref[...] = value_ref[...]


def neighbours(up, down, axis):
    count = lax.axis_size(axis)
    low = lax.ppermute(up, axis, [(i, i + 1) for i in range(count - 1)])
    high = lax.ppermute(down, axis, [(i + 1, i) for i in range(count - 1)])
    return low, high


def per_device(
    features,
    conv_weight,
    fwd_prev,
    fwd_now,
    back_prev,
    back_now,
    sources,
    wavelet,
    receivers,
    residual,
    damping,
):
    channels, size_x, size_y, depth = features.shape
    shots = lax.axis_size("shot")
    rows = size_x // shots
    count = receivers.shape[1]
    plane_y = size_y * lax.axis_size("gy")
    blocks = lax.axis_size("gx") * lax.axis_size("gy")
    grid = (size_x, size_y, depth)
    fwd_prev, fwd_now, back_prev, back_now = (
        a.reshape(grid) for a in (fwd_prev, fwd_now, back_prev, back_now)
    )
    place = jnp.stack(
        [
            lax.axis_index("gx") * size_x,
            lax.axis_index("gy") * size_y,
            sources[0],
        ]
    ).astype(jnp.int32)

    x_shape = shape(8 + channels, size_y, depth)
    with jax.named_scope("pack_x"):
        x_up, x_down = call(
            pack_x_body,
            [x_shape, x_shape],
            (features, fwd_now, back_now),
            [pl.BlockSpec(memory_space=pltpu.HBM)] * 3,
            scratch=[
                pltpu.VMEM((2, channels, size_y, depth), BF16),
                pltpu.SemaphoreType.DMA((6,)),
            ],
            name="pack_x",
            limit=VMEM_WHOLE,
        )
    packing = [
        pltpu.VMEM((size_x, 8, depth), F32),
        pltpu.VMEM((size_x // 4, 16, depth), F32),
    ]
    y_shape = shape(channels * size_x + 16 + wave_rows(size_x), depth, dtype=BF16)
    with jax.named_scope("pack_y"):
        y_up, y_down = call(
            pack_y_body,
            [y_shape, y_shape],
            (features, fwd_now, back_now),
            [VM] * 3,
            scratch=[pltpu.VMEM(grid, F32)] + packing,
            name="pack_y",
        )
    with jax.named_scope("halo_x"):
        x_low, x_high = neighbours(x_up, x_down, "gx")
    with jax.named_scope("corners"):
        y_up, y_down = call(
            corners_body,
            [y_shape, y_shape],
            (y_up, y_down, x_low, x_high),
            [VM] * 4,
            name="corners",
        )
    with jax.named_scope("halo_y"):
        y_low, y_high = neighbours(y_up, y_down, "gy")
    ext = pltpu.VMEM((channels, size_x + 2, size_y, depth), F32)
    full = shape(*grid)
    inner_scratch = [
        pltpu.VMEM((size_x + 8, size_y, depth), F32),
        pltpu.VMEM((size_x, size_y + 16, depth), F32),
        pltpu.VMEM(grid, F32),
    ]
    step_scratch = packing + [pltpu.VMEM((size_x, 16, depth), F32)] * 4
    work = 60 * size_x * size_y * depth
    with jax.named_scope("inner_1"):
        inner_1 = call(
            functools.partial(inner_body, 0, plane_y),
            [full] * 5 + [shape(*wavelet.shape)],
            (fwd_now, back_now, fwd_prev, back_prev)
            + (place, receivers, residual, wavelet, x_low, x_high),
            [VM] * 4 + [SM] + [VM] * 5,
            scratch=inner_scratch,
            flops=work,
            name="inner_1",
        )
    with jax.named_scope("conv"):
        main = call(
            conv_body,
            [full],
            (features, x_low, x_high, conv_weight),
            [VM, VM, VM, SM],
            scratch=[ext],
            flops=54 * channels * size_x * size_y * depth,
            name="conv",
        )
    with jax.named_scope("raw"):
        parts = lax.all_to_all(main, "shot", 0, 0, tiled=True)
        y_low, *inner_1 = lax.optimization_barrier((y_low, *inner_1))
        rims = call(
            conv_edge_body,
            [shape(2 * size_x, depth)],
            (y_low, y_high, conv_weight),
            [VM] * 2 + [SM],
            scratch=[pltpu.VMEM((2 * channels, size_x + 16, depth), F32)],
            flops=AHEAD,
            name="conv_edge",
        )
        each = rows * size_y + 2 * size_x
        raw = call(
            raw_body,
            [shape(shots, each, depth)],
            (parts.reshape(shots, rows, size_y, depth), rims),
            [VM] * 2,
            name="raw",
        )
        raw = lax.all_to_all(raw.reshape(shots * each, depth), "shot", 0, 0, tiled=True)
        raw = raw.reshape(shots, each, depth)

    later, wavelet = inner_1[4:]
    with jax.named_scope("step_1"):
        fwd_1, back_1, lap_1, squashed, x_up, x_down, y_up, y_down = call(
            functools.partial(step_body, 0, plane_y),
            [full] * 4
            + [shape(8, size_y, depth)] * 2
            + [shape(wave_rows(size_x), depth, dtype=BF16)] * 2,
            (
                *inner_1[:4],
                y_low,
                y_high,
                place,
                wavelet,
                raw,
            ),
            [VM] * 6 + [SM] * 2 + [VM],
            scratch=step_scratch,
            name="step_1",
        )
    with jax.named_scope("halo_2"):
        x_low_2, x_high_2 = neighbours(x_up, x_down, "gx")
        y_low_2, y_high_2 = neighbours(y_up, y_down, "gy")
    with jax.named_scope("inner_2"):
        fwd_ahead, back_ahead, lap_fwd, lap_back = call(
            functools.partial(inner_body, 1, plane_y),
            [full] * 4,
            (fwd_1, back_1, fwd_now, back_now, later),
            [VM] * 5,
            scratch=inner_scratch[:2],
            flops=work,
            name="inner_2",
        )
    with jax.named_scope("step_2"):
        fwd_2, back_2, sums = call(
            functools.partial(step_body, 1, plane_y),
            [full, full, shape(shots, 2 * rows, size_y, depth)],
            (
                fwd_ahead,
                back_ahead,
                lap_fwd,
                lap_back,
                y_low_2,
                y_high_2,
                place,
                wavelet,
                squashed,
                x_low_2,
                x_high_2,
                lap_1,
                back_1,
            ),
            [VM] * 6 + [SM] * 2 + [VM] * 5,
            scratch=step_scratch,
            name="step_2",
        )
    with jax.named_scope("traces"):
        trace_1, trace_2 = call(
            functools.partial(trace_body, plane_y),
            [shape(1, count)] * 2,
            (fwd_1, fwd_2, place, receivers),
            [VM, VM, SM, VM],
            name="traces",
        )
    with jax.named_scope("update"):
        sums = lax.all_to_all(
            sums.reshape(shots * 2 * rows, size_y, depth), "shot", 0, 0, tiled=True
        )
        update = call(
            update_body,
            [shape(shots, rows, size_y, depth)],
            (sums.reshape(shots, 2 * rows, size_y, depth), damping),
            [VM, SM],
            name="update",
        )
        update = lax.all_to_all(update.reshape(grid), "shot", 0, 0, tiled=True)
    with jax.named_scope("gradient"):
        share = call(
            gradient_body,
            [shape(blocks, 1, 2 * count + depth)],
            (update, squashed, features, x_low, x_high, y_low, y_high, trace_1, trace_2),
            [VM] * 9,
            scratch=[
                pltpu.VMEM((6,) + grid, BF16),
                pltpu.VMEM((size_x * size_y, 3 * channels * depth), BF16),
                pltpu.VMEM((3, size_x + 16, depth), F32),
                pltpu.VMEM((128, depth), F32),
            ],
            flops=54 * channels * size_x * size_y * depth,
            name="gradient",
        )
        share, update = lax.optimization_barrier((share, update))
        shares = lax.all_to_all(share, ("gx", "gy"), 0, 0, tiled=True)
        shares = shares.reshape(blocks, 1, 2 * count + depth)
        traces, weight_grad = call(
            total_body,
            [shape(1, 2, count), shape(channels, 27)],
            (shares,),
            [VM],
            name="total",
        )
        update = call(keep_body, [full], (update,), [VM], name="keep")
    return (fwd_2[None], back_2[None], traces, update, weight_grad)


def solution(mesh):
    in_specs = (
        P("shot", "gx", "gy", None),
        P("shot", None),
        P("shot", "gx", "gy", None),
        P("shot", "gx", "gy", None),
        P("shot", "gx", "gy", None),
        P("shot", "gx", "gy", None),
        P("shot"),
        P("shot", None),
        P("shot", None),
        P("shot", None, None),
        P(),
    )
    out_specs = (
        P("shot", "gx", "gy", None),
        P("shot", "gx", "gy", None),
        P("shot", None, None),
        P("gx", "gy", None),
        P("shot", None),
    )
    return jax.shard_map(
        per_device, mesh=mesh, in_specs=in_specs, out_specs=out_specs, check_vma=False
    )
```

```python
import functools

import jax
import jax.numpy as jnp
from jax import lax
from jax.experimental import pallas as pl
from jax.experimental.pallas import tpu as pltpu
from jax.sharding import PartitionSpec as P

RDEPTH = 3
COEFFICIENTS = (-205.0 / 72.0, 8.0 / 5.0, -1.0 / 5.0, 8.0 / 315.0, -1.0 / 560.0)
F32 = jnp.float32
BF16 = jnp.bfloat16
VMEM_LIMIT = 48 * 1024 * 1024
AHEAD = 50_000_000_000
VMEM_WHOLE = 63 * 1024 * 1024

VM = pl.BlockSpec(memory_space=pltpu.VMEM)
SM = pl.BlockSpec(memory_space=pltpu.SMEM)


def call(
    body,
    outs,
    ins,
    specs,
    scratch=(),
    flops=1_000_000,
    name=None,
    limit=VMEM_LIMIT,
):
    moved = sum(a.size * a.dtype.itemsize for a in ins) + sum(
        o.size * jnp.dtype(o.dtype).itemsize for o in outs
    )
    single = len(outs) == 1
    return pl.pallas_call(
        body,
        out_shape=outs[0] if single else tuple(outs),
        in_specs=specs,
        out_specs=VM if single else tuple(VM for _ in outs),
        scratch_shapes=list(scratch),
        compiler_params=pltpu.CompilerParams(vmem_limit_bytes=limit),
        cost_estimate=pl.CostEstimate(flops=flops, bytes_accessed=moved, transcendentals=0),
        name=name,
    )(*ins)


def shape(*dims, dtype=F32):
    return jax.ShapeDtypeStruct(dims, dtype)


def split3(value):
    top = value.astype(BF16)
    rest = value - top.astype(F32)
    middle = rest.astype(BF16)
    low = (rest - middle.astype(F32)).astype(BF16)
    return (top, middle, low)


def shifted_lanes(value, by):
    depth = value.shape[1]
    lane = lax.broadcasted_iota(jnp.int32, value.shape, 1)
    if by > 0:
        return jnp.where(lane < depth - by, pltpu.roll(value, depth - by, 1), 0.0)
    return jnp.where(lane >= -by, pltpu.roll(value, -by, 1), 0.0)


def shifted_rows(value, by):
    count = value.shape[0]
    row = lax.broadcasted_iota(jnp.int32, value.shape, 0)
    if by > 0:
        return jnp.where(row < count - by, pltpu.roll(value, count - by, 0), 0.0)
    return jnp.where(row >= -by, pltpu.roll(value, -by, 0), 0.0)


def pack_x_body(feat_ref, fwd_ref, back_ref, up_ref, down_ref, edge_ref, sems):
    channels, size_x = feat_ref.shape[:2]
    pairs = []
    for n, (out_ref, start, row) in enumerate(
        ((up_ref, size_x - 4, size_x - 1), (down_ref, 0, 0))
    ):
        pairs += [
            (feat_ref.at[:, row], edge_ref.at[n]),
            (fwd_ref.at[pl.ds(start, 4)], out_ref.at[pl.ds(0, 4)]),
            (back_ref.at[pl.ds(start, 4)], out_ref.at[pl.ds(4, 4)]),
        ]
    copies = [
        pltpu.make_async_copy(source, target, sems.at[n])
        for n, (source, target) in enumerate(pairs)
    ]
    for copy in copies:
        copy.start()
    for copy in copies:
        copy.wait()
    up_ref[8 : 8 + channels] = edge_ref[0].astype(F32)
    down_ref[8 : 8 + channels] = edge_ref[1].astype(F32)


def wave_rows(size_x):
    return size_x * 12


def pack_waves(fwd_ref, back_ref, upward, out_ref, first, edge_ref, low_ref):
    size_x, size_y, depth = fwd_ref.shape
    start, near = (size_y - 4, 2) if upward else (0, 0)
    edge_ref[:, 0:4] = fwd_ref[:, start : start + 4]
    edge_ref[:, 4:8] = back_ref[:, start : start + 4]
    value = edge_ref[...].reshape(size_x * 8, depth)
    high = value.astype(BF16)
    out_ref[first : first + size_x * 8] = high
    edge_ref[...] = (value - high.astype(F32)).reshape(size_x, 8, depth)
    quarter = size_x // 4
    for q in range(4):
        part = slice(q * quarter, (q + 1) * quarter)
        low_ref[:, 4 * q : 4 * q + 2] = edge_ref[part, near : near + 2]
        low_ref[:, 4 * q + 2 : 4 * q + 4] = edge_ref[part, 4 + near : 6 + near]
    out_ref[first + size_x * 8 : first + size_x * 12] = (
        low_ref[...].reshape(size_x * 4, depth).astype(BF16)
    )


def unpack_waves(buffer_ref, upward, first, size_x, edge_ref, low_ref):
    depth = buffer_ref.shape[1]
    near = 2 if upward else 0
    quarter = size_x // 4
    edge_ref[...] = (
        buffer_ref[first : first + size_x * 8].astype(F32).reshape(size_x, 8, depth)
    )
    low_ref[...] = (
        buffer_ref[first + size_x * 8 : first + size_x * 12]
        .astype(F32)
        .reshape(quarter, 16, depth)
    )
    for q in range(4):
        part = slice(q * quarter, (q + 1) * quarter)
        edge_ref[part, near : near + 2] += low_ref[:, 4 * q : 4 * q + 2]
        edge_ref[part, 4 + near : 6 + near] += low_ref[:, 4 * q + 2 : 4 * q + 4]


def pack_y_body(feat_ref, fwd_ref, back_ref, up_ref, down_ref, plane_ref, edge_ref, rest_ref):
    channels, size_x, size_y, depth = feat_ref.shape
    first = channels * size_x
    for c in range(channels):
        plane_ref[...] = feat_ref[c].astype(F32)
        for out_ref, y in ((up_ref, size_y - 1), (down_ref, 0)):
            out_ref[c * size_x : (c + 1) * size_x] = plane_ref[:, y, :].astype(BF16)
    for out_ref, upward in ((up_ref, True), (down_ref, False)):
        out_ref[first : first + 16] = jnp.zeros((16, depth), BF16)
        pack_waves(fwd_ref, back_ref, upward, out_ref, first + 16, edge_ref, rest_ref)


def corners_body(up_in_ref, down_in_ref, low_ref, high_ref, up_ref, down_ref):
    size_y, depth = low_ref.shape[1:]
    channels = low_ref.shape[0] - 8
    size_x = (up_ref.shape[0] - 16) // (channels + 12)
    first = channels * size_x
    row = lax.broadcasted_iota(jnp.int32, (16, depth), 0)
    for in_ref, out_ref, y in ((up_in_ref, up_ref, size_y - 1), (down_in_ref, down_ref, 0)):
        out_ref[0:first] = in_ref[0:first]
        out_ref[first + 16 :] = in_ref[first + 16 :]
        tail = jnp.zeros((16, depth), F32)
        for c in range(channels):
            tail = jnp.where(row == 2 * c, low_ref[8 + c, y : y + 1, :], tail)
            tail = jnp.where(row == 2 * c + 1, high_ref[8 + c, y : y + 1, :], tail)
        out_ref[first : first + 16] = tail.astype(BF16)


def fill_features(ext_ref, feat_ref, low_ref, high_ref):
    channels, size_x = feat_ref.shape[:2]
    for c in range(channels):
        ext_ref[c, 0] = low_ref[8 + c]
        ext_ref[c, 1 : 1 + size_x] = feat_ref[c].astype(F32)
        ext_ref[c, 1 + size_x] = high_ref[8 + c]


def conv_body(feat_ref, low_ref, high_ref, weight_ref, total_ref, wide_ref, ext_ref):
    channels, size_x = feat_ref.shape[:2]
    fill_features(ext_ref, feat_ref, low_ref, high_ref)
    together = 2

    def some_rows(start):
        terms = [[[None] * 3 for _ in range(3)] for _ in range(together)]
        for c in range(channels):
            inputs = [ext_ref[c, start + r] for r in range(together + 2)]
            for dx in range(3):
                for dy in range(3):
                    for dz in range(3):
                        weight = weight_ref[c, 9 * dx + 3 * dy + dz]
                        for r in range(together):
                            part = weight * inputs[r + dx]
                            old = terms[r][dy][dz]
                            terms[r][dy][dz] = part if old is None else old + part
        for r in range(together):
            total = None
            for dy in range(3):
                part = (
                    terms[r][dy][1]
                    + shifted_lanes(terms[r][dy][0], -1)
                    + shifted_lanes(terms[r][dy][2], 1)
                )
                if dy != 1:
                    part = shifted_rows(part, dy - 1)
                total = part if total is None else total + part
            total_ref[start + r] = total

    for start in range(0, size_x, together):
        some_rows(start)
    at = 0
    for dy in (0, 2):
        for c in range(channels):
            for dx in range(3):
                for dz in range(3):
                    weight = weight_ref[c, 9 * dx + 3 * dy + dz]
                    wide_ref[at : at + 1] = jnp.full((1, wide_ref.shape[1]), weight, F32)
                    at += 1


def load_plane(plane_ref, buffer_ref, c, size_x, channels):
    plane_ref[8 : 8 + size_x] = buffer_ref[c * size_x : (c + 1) * size_x].astype(F32)
    tail = buffer_ref[channels * size_x : channels * size_x + 16].astype(F32)
    plane_ref[7:8] = tail[2 * c : 2 * c + 1]
    plane_ref[8 + size_x : 9 + size_x] = tail[2 * c + 1 : 2 * c + 2]


def conv_edge_body(low_ref, high_ref, wide_ref, out_ref, plane_ref):
    size_x = out_ref.shape[0] // 2
    channels = wide_ref.shape[0] // 18
    at = 0
    for side, buffer_ref in enumerate((low_ref, high_ref)):
        terms = [None] * 3
        for c in range(channels):
            held_ref = plane_ref.at[side * channels + c]
            load_plane(held_ref, buffer_ref, c, size_x, channels)
            for dx in range(3):
                plane = held_ref[7 + dx : 7 + dx + size_x]
                for dz in range(3):
                    part = wide_ref[at : at + 1] * plane
                    terms[dz] = part if terms[dz] is None else terms[dz] + part
                    at += 1
        total = terms[1] + shifted_lanes(terms[0], -1) + shifted_lanes(terms[2], 1)
        out_ref[side * size_x : (side + 1) * size_x] = total


def raw_body(parts_ref, rims_ref, out_ref):
    copies, rows, size_y, depth = parts_ref.shape
    total = parts_ref[0]
    for n in range(1, copies):
        total = total + parts_ref[n]
    first = rows * size_y
    total = total.reshape(first, depth)
    rims = rims_ref[...]
    for n in range(copies):
        out_ref[n, 0:first] = total
        out_ref[n, first:] = rims


def update_body(parts_ref, damping_ref, out_ref):
    count, rows = parts_ref.shape[:2]
    half = rows // 2
    total = parts_ref[0]
    for n in range(1, count):
        total = total + parts_ref[n]
    update = total[:half] / (total[half:] + damping_ref[0])
    for n in range(count):
        out_ref[n] = update


def receiver_hits(receivers_ref, place_ref, plane_y, size_x, size_y):
    shift_y = plane_y.bit_length() - 1
    receivers = receivers_ref[...]
    place_x = lax.shift_right_logical(receivers, shift_y) - place_ref[0]
    place_y = (receivers & (plane_y - 1)) - place_ref[1]
    inside = (place_x >= 0) & (place_x < size_x) & (place_y >= 0) & (place_y < size_y)
    cell = jnp.where(inside, place_x * size_y + place_y, -1)
    cells = lax.broadcasted_iota(jnp.int32, (size_x * size_y, receivers.shape[1]), 0)
    return (cells == cell).astype(F32).astype(BF16)


def exact_product(parts, other, contract, parts_first):
    total = None
    for part in parts:
        pair = (part, other) if parts_first else (other, part)
        product = lax.dot_general(
            *pair, (contract, ((), ())), preferred_element_type=F32
        )
        total = product if total is None else total + product
    return total


def sample(fwd_ref, hit, trace_ref):
    size_x, size_y, depth = fwd_ref.shape
    field = fwd_ref[...].reshape(size_x * size_y, depth)
    total = exact_product(split3(field), hit, ((0,), (0,)), True)
    trace_ref[...] = total[RDEPTH : RDEPTH + 1, :]


def trace_body(plane_y, first_ref, second_ref, place_ref, receivers_ref, *out_refs):
    size_x, size_y, _ = first_ref.shape
    hit = receiver_hits(receivers_ref, place_ref, plane_y, size_x, size_y)
    for fwd_ref, trace_ref in zip((first_ref, second_ref), out_refs):
        sample(fwd_ref, hit, trace_ref)


def inner_body(moment, plane_y, *refs):
    fwd_ref, back_ref, fwd_old_ref, back_old_ref = refs[:4]
    size_x, size_y, depth = fwd_ref.shape
    rows = 4
    if moment == 0:
        place_ref, receivers_ref, residual_ref, wavelet_ref, x_low_ref, x_high_ref = refs[4:10]
        fwd_ahead_ref, back_ahead_ref, lap_fwd_ref, lap_back_ref = refs[10:14]
        later_ref, spot_ref, amplitude_ref, x_ref, y_ref, inject_ref = refs[14:]
        anchor_x, anchor_y, source = place_ref[0], place_ref[1], place_ref[2]
        shift_y = plane_y.bit_length() - 1
        shift_z = depth.bit_length() - 1
        column = lax.shift_right_logical(source, shift_z)
        source_x = lax.shift_right_logical(column, shift_y) - anchor_x
        source_y = (column & (plane_y - 1)) - anchor_y
        source_z = source & (depth - 1)
        here = (source_x >= 0) & (source_x < size_x) & (source_y >= 0) & (source_y < size_y)
        spot = jnp.where(here, (source_x * size_y + source_y) * depth + source_z, -1)
        spot_ref[...] = jnp.full(spot_ref.shape, spot, jnp.int32)
        for n in range(2):
            amplitude_ref[n] = jnp.full(amplitude_ref.shape[1:], wavelet_ref[0, n], F32)
        hit = receiver_hits(receivers_ref, place_ref, plane_y, size_x, size_y)
        for n, out_ref in enumerate((inject_ref, later_ref)):
            injected = jnp.where(
                lax.broadcasted_iota(jnp.int32, (depth, hit.shape[1]), 0) == RDEPTH,
                residual_ref[0, n : n + 1, :],
                0.0,
            )
            out_ref[...] = exact_product(split3(injected), hit, ((1,), (1,)), False).reshape(
                size_x, size_y, depth
            )
    else:
        inject_ref = refs[4]
        fwd_ahead_ref, back_ahead_ref, lap_fwd_ref, lap_back_ref = refs[5:9]
        x_ref, y_ref = refs[9:]
    zero_x = jnp.zeros((4, size_y, depth), F32)
    y_ref[:, 0:8] = jnp.zeros((size_x, 8, depth), F32)
    y_ref[:, 8 + size_y : 16 + size_y] = jnp.zeros((size_x, 8, depth), F32)
    for first, ref, old_ref, ahead_ref, lap_ref in (
        (0, fwd_ref, fwd_old_ref, fwd_ahead_ref, lap_fwd_ref),
        (4, back_ref, back_old_ref, back_ahead_ref, lap_back_ref),
    ):
        x_ref[0:4] = zero_x if moment else x_low_ref[first : first + 4]
        x_ref[4 : 4 + size_x] = ref[...]
        x_ref[4 + size_x : 8 + size_x] = zero_x if moment else x_high_ref[first : first + 4]
        y_ref[:, 8 : 8 + size_y] = ref[...]

        def one_block(i, carry):
            start = i * rows
            here = pl.ds(start, rows)
            centre = ref[here]
            flat = centre.reshape(rows * size_y, depth)
            result = (3.0 * COEFFICIENTS[0]) * centre
            for k in range(1, 5):
                along_x = x_ref[pl.ds(start + 4 + k, rows)] + x_ref[pl.ds(start + 4 - k, rows)]
                along_y = (
                    y_ref[here, 8 + k : 8 + k + size_y, :] + y_ref[here, 8 - k : 8 - k + size_y, :]
                )
                along_z = shifted_lanes(flat, k) + shifted_lanes(flat, -k)
                result = result + COEFFICIENTS[k] * (
                    along_x + along_y + along_z.reshape(centre.shape)
                )
            if first:
                result = result + inject_ref[here]
            lap_ref[here] = result
            ahead_ref[here] = 2.0 * centre - old_ref[here]
            return carry

        for i in range(size_x // rows):
            one_block(i, 0)


def step_body(moment, plane_y, *refs):
    fwd_ahead_ref, back_ahead_ref, lap_fwd_ref, lap_back_ref = refs[:4]
    y_low_ref, y_high_ref, spot_ref, amplitude_ref = refs[4:8]
    refs = refs[8:]
    if moment == 0:
        raw_ref = refs[0]
        (fwd_new_ref, back_new_ref, lap_ref, squashed_ref) = refs[1:5]
        (x_up_ref, x_down_ref, y_up_ref, y_down_ref) = refs[5:9]
        refs = refs[9:]
        size_x, size_y, depth = squashed_ref.shape
        shots = raw_ref.shape[0]
        rows = size_x // shots
        first = rows * size_y
        rims = None
        for n in range(shots):
            squashed_ref[n * rows : (n + 1) * rows] = raw_ref[n, 0:first].reshape(
                rows, size_y, depth
            )
            part = raw_ref[n, first:]
            rims = part if rims is None else rims + part
        squashed_ref[:, 0:1, :] += rims[:size_x].reshape(size_x, 1, depth)
        squashed_ref[:, size_y - 1 : size_y, :] += rims[size_x:].reshape(size_x, 1, depth)
    else:
        squashed_ref, x_low_ref, x_high_ref, lap_old_ref, back_ref = refs[:5]
        (fwd_new_ref, back_new_ref, sums_ref) = refs[5:8]
        refs = refs[8:]
    edge_ref, rest_ref, *sides = refs
    size_x, size_y, depth = fwd_ahead_ref.shape
    start_row = y_low_ref.shape[0] - wave_rows(size_x)
    for n, (buffer_ref, upward) in enumerate(((y_low_ref, True), (y_high_ref, False))):
        unpack_waves(buffer_ref, upward, start_row, size_x, edge_ref, rest_ref)
        for m in range(2):
            side_ref = sides[2 * m + n]
            at, empty = (4, 8) if upward else (8, 0)
            side_ref[:, empty : empty + 8] = jnp.zeros((size_x, 8, depth), F32)
            side_ref[:, at : at + 4] = edge_ref[:, 4 * m : 4 * m + 4]

    spot, amplitude = spot_ref[0:1, :], amplitude_ref[moment, 0:1, :]

    def edges(lap, m, start):
        block = slice(start, start + 4)
        low = high = None
        for k in range(1, 5):
            a = COEFFICIENTS[k] * sides[2 * m][block, 8 - k : 16 - k, :]
            b = COEFFICIENTS[k] * sides[2 * m + 1][block, k : 8 + k, :]
            low, high = (a, b) if low is None else (low + a, high + b)
        parts = [low, high]
        if size_y > 16:
            parts.insert(1, jnp.zeros((4, size_y - 16, depth), F32))
        lap = lap + jnp.concatenate(parts, axis=1)
        if moment == 0 or start not in (0, size_x - 4):
            return lap
        parts = []
        for j in range(4):
            total = None
            if start == 0:
                picks = [(k, x_low_ref, 4 * m + 4 + j - k) for k in range(j + 1, 5)]
            else:
                picks = [(k, x_high_ref, 4 * m + j + k - 4) for k in range(4 - j, 5)]
            for k, ref, row in picks:
                part = COEFFICIENTS[k] * ref[row]
                total = part if total is None else total + part
            parts.append(total)
        return lap + jnp.stack(parts)

    for start in range(0, size_x, 4):
        here = slice(start, start + 4)
        squashed = squashed_ref[here]
        if moment == 0:
            squashed = jax.nn.sigmoid(squashed)
            squashed_ref[here] = squashed
        courant = 0.02 + 0.16 * squashed
        lap_fwd = edges(lap_fwd_ref[here], 0, start)
        lap_back = edges(lap_back_ref[here], 1, start)
        dims = lap_fwd.shape
        index = (
            lax.broadcasted_iota(jnp.int32, dims, 0) * (size_y * depth)
            + lax.broadcasted_iota(jnp.int32, dims, 1) * depth
            + lax.broadcasted_iota(jnp.int32, dims, 2)
        )
        added = jnp.where(index == spot - start * (size_y * depth), amplitude, 0.0)
        fwd_new_ref[here] = fwd_ahead_ref[here] + courant * (lap_fwd + added)
        back_new = back_ahead_ref[here] + courant * lap_back
        back_new_ref[here] = back_new
        if moment == 0:
            lap_ref[here] = lap_fwd
        else:
            rows = sums_ref.shape[1] // 2
            n, at = start // rows, start % rows
            lap_old = lap_old_ref[here]
            sums_ref[n, at : at + 4] = lap_old * back_ref[here] + lap_fwd * back_new
            sums_ref[n, rows + at : rows + at + 4] = lap_old * lap_old + lap_fwd * lap_fwd

    if moment == 0:
        x_up_ref[0:4] = fwd_new_ref[size_x - 4 : size_x]
        x_up_ref[4:8] = back_new_ref[size_x - 4 : size_x]
        x_down_ref[0:4] = fwd_new_ref[0:4]
        x_down_ref[4:8] = back_new_ref[0:4]
        pack_waves(fwd_new_ref, back_new_ref, True, y_up_ref, 0, edge_ref, rest_ref)
        pack_waves(fwd_new_ref, back_new_ref, False, y_down_ref, 0, edge_ref, rest_ref)


def gradient_body(
    update_ref,
    squashed_ref,
    feat_ref,
    x_low_ref,
    x_high_ref,
    y_low_ref,
    y_high_ref,
    first_ref,
    second_ref,
    out_ref,
    left_ref,
    right_ref,
    plane_ref,
    rows_ref,
):
    size_x, size_y, depth = update_ref.shape
    channels = feat_ref.shape[0]
    copies = out_ref.shape[0]
    cells = size_x * size_y

    for x in range(size_x):
        squashed = squashed_ref[x]
        pulled = update_ref[x] * (0.16 * squashed * (1.0 - squashed))
        for dy in range(3):
            moved = pulled if dy == 1 else shifted_rows(pulled, 1 - dy)
            high = moved.astype(BF16)
            left_ref[2 * dy, x] = high
            left_ref[2 * dy + 1, x] = (moved - high.astype(F32)).astype(BF16)
        plane_ref[1, x : x + 1] = pulled[0:1, :]
        plane_ref[2, x : x + 1] = pulled[size_y - 1 : size_y, :]
    last = cells - size_y
    for c in range(channels):
        lanes = [slice((3 * c + dx) * depth, (3 * c + dx + 1) * depth) for dx in range(3)]
        own = feat_ref[c].reshape(cells, depth)
        right_ref[0:size_y, lanes[0]] = x_low_ref[8 + c].astype(BF16)
        right_ref[size_y:cells, lanes[0]] = own[0:last]
        right_ref[:, lanes[1]] = own
        right_ref[0:last, lanes[2]] = own[size_y:cells]
        right_ref[last:cells, lanes[2]] = x_high_ref[8 + c].astype(BF16)
    ahead = lax.broadcasted_iota(jnp.int32, (depth, depth), 1) - (
        lax.broadcasted_iota(jnp.int32, (depth, depth), 0)
    )
    for dy in range(3):
        left = jnp.concatenate(
            [left_ref[2 * dy + part].reshape(cells, depth) for part in range(2)], axis=1
        )
        product = lax.dot_general(
            left, right_ref[...], (((0,), (0,)), ((), ())), preferred_element_type=F32
        )
        for c in range(channels):
            for dx in range(3):
                lanes = slice((3 * c + dx) * depth, (3 * c + dx + 1) * depth)
                block = product[0:depth, lanes] + product[depth : 2 * depth, lanes]
                for dz in range(3):
                    at = c * 27 + 9 * dx + 3 * dy + dz
                    rows_ref[at : at + 1] = jnp.sum(
                        jnp.where(ahead == dz - 1, block, 0.0), axis=0, keepdims=True
                    )
    at = channels * 27
    rows_ref[at:] = jnp.zeros((rows_ref.shape[0] - at, depth), F32)

    for buffer_ref, dy, which in ((y_low_ref, 0, 1), (y_high_ref, 2, 2)):
        pulled = plane_ref[which, 0:size_x]
        along = [pulled if dz == 1 else shifted_lanes(pulled, 1 - dz) for dz in range(3)]
        for c in range(channels):
            load_plane(plane_ref.at[0], buffer_ref, c, size_x, channels)
            for dx in range(3):
                features = plane_ref[0, 7 + dx : 7 + dx + size_x]
                for dz in range(3):
                    at = c * 27 + 9 * dx + 3 * dy + dz
                    rows_ref[at : at + 1] += jnp.sum(
                        features * along[dz], axis=0, keepdims=True
                    )

    ones = jnp.ones((8, depth), BF16)
    sums = None
    for part in split3(rows_ref[...]):
        product = lax.dot_general(
            ones, part, (((1,), (1,)), ((), ())), preferred_element_type=F32
        )
        sums = product if sums is None else sums + product
    count = first_ref.shape[1]
    for n in range(copies):
        out_ref[n, :, 0:count] = first_ref[...]
        out_ref[n, :, count : 2 * count] = second_ref[...]
        out_ref[n, :, 2 * count : 2 * count + depth] = sums[0:1]


def total_body(shares_ref, trace_ref, grad_ref):
    copies = shares_ref.shape[0]
    count = trace_ref.shape[2]
    channels, offsets = grad_ref.shape
    total = shares_ref[0]
    for n in range(1, copies):
        total = total + shares_ref[n]
    trace_ref[0, 0:1, :] = total[:, 0:count]
    trace_ref[0, 1:2, :] = total[:, count : 2 * count]
    last = total[:, 2 * count :]
    lanes = last.shape[1]
    last = jnp.broadcast_to(last, (8, lanes))
    for c in range(channels):
        turned = last if c == 0 else pltpu.roll(last, lanes - c * offsets, 1)
        grad_ref[c : c + 1, :] = turned[0:1, 0:offsets]


def keep_body(value_ref, out_ref):
    out_ref[...] = value_ref[...]


def neighbours(up, down, axis):
    count = lax.axis_size(axis)
    low = lax.ppermute(up, axis, [(i, i + 1) for i in range(count - 1)])
    high = lax.ppermute(down, axis, [(i + 1, i) for i in range(count - 1)])
    return low, high


def per_device(
    features,
    conv_weight,
    fwd_prev,
    fwd_now,
    back_prev,
    back_now,
    sources,
    wavelet,
    receivers,
    residual,
    damping,
):
    channels, size_x, size_y, depth = features.shape
    shots = lax.axis_size("shot")
    rows = size_x // shots
    count = receivers.shape[1]
    plane_y = size_y * lax.axis_size("gy")
    blocks = lax.axis_size("gx") * lax.axis_size("gy")
    grid = (size_x, size_y, depth)
    fwd_prev, fwd_now, back_prev, back_now = (
        a.reshape(grid) for a in (fwd_prev, fwd_now, back_prev, back_now)
    )
    place = jnp.stack(
        [
            lax.axis_index("gx") * size_x,
            lax.axis_index("gy") * size_y,
            sources[0],
        ]
    ).astype(jnp.int32)

    x_shape = shape(8 + channels, size_y, depth)
    with jax.named_scope("pack_x"):
        x_up, x_down = call(
            pack_x_body,
            [x_shape, x_shape],
            (features, fwd_now, back_now),
            [pl.BlockSpec(memory_space=pltpu.HBM)] * 3,
            scratch=[
                pltpu.VMEM((2, channels, size_y, depth), BF16),
                pltpu.SemaphoreType.DMA((6,)),
            ],
            name="pack_x",
            limit=VMEM_WHOLE,
        )
    packing = [
        pltpu.VMEM((size_x, 8, depth), F32),
        pltpu.VMEM((size_x // 4, 16, depth), F32),
    ]
    y_shape = shape(channels * size_x + 16 + wave_rows(size_x), depth, dtype=BF16)
    with jax.named_scope("pack_y"):
        y_up, y_down = call(
            pack_y_body,
            [y_shape, y_shape],
            (features, fwd_now, back_now),
            [VM] * 3,
            scratch=[pltpu.VMEM(grid, F32)] + packing,
            name="pack_y",
        )
    with jax.named_scope("halo_x"):
        x_low, x_high = neighbours(x_up, x_down, "gx")
    with jax.named_scope("corners"):
        y_up, y_down = call(
            corners_body,
            [y_shape, y_shape],
            (y_up, y_down, x_low, x_high),
            [VM] * 4,
            name="corners",
        )
    with jax.named_scope("halo_y"):
        y_low, y_high = neighbours(y_up, y_down, "gy")
    ext = pltpu.VMEM((channels, size_x + 2, size_y, depth), F32)
    full = shape(*grid)
    inner_scratch = [
        pltpu.VMEM((size_x + 8, size_y, depth), F32),
        pltpu.VMEM((size_x, size_y + 16, depth), F32),
        pltpu.VMEM(grid, F32),
    ]
    step_scratch = packing + [pltpu.VMEM((size_x, 16, depth), F32)] * 4
    work = 60 * size_x * size_y * depth
    with jax.named_scope("inner_1"):
        inner_1 = call(
            functools.partial(inner_body, 0, plane_y),
            [full] * 5 + [shape(8, depth, dtype=jnp.int32), shape(2, 8, depth)],
            (fwd_now, back_now, fwd_prev, back_prev)
            + (place, receivers, residual, wavelet, x_low, x_high),
            [VM] * 4 + [SM] + [VM] * 2 + [SM] + [VM] * 2,
            scratch=inner_scratch,
            flops=work,
            name="inner_1",
        )
    with jax.named_scope("conv"):
        main, wide = call(
            conv_body,
            [full, shape(18 * channels, depth)],
            (features, x_low, x_high, conv_weight),
            [VM, VM, VM, SM],
            scratch=[ext],
            flops=54 * channels * size_x * size_y * depth,
            name="conv",
        )
    with jax.named_scope("raw"):
        parts = lax.all_to_all(main, "shot", 0, 0, tiled=True)
        y_low, *inner_1 = lax.optimization_barrier((y_low, *inner_1))
        rims = call(
            conv_edge_body,
            [shape(2 * size_x, depth)],
            (y_low, y_high, wide),
            [VM] * 3,
            scratch=[pltpu.VMEM((2 * channels, size_x + 16, depth), F32)],
            flops=AHEAD,
            name="conv_edge",
        )
        each = rows * size_y + 2 * size_x
        raw = call(
            raw_body,
            [shape(shots, each, depth)],
            (parts.reshape(shots, rows, size_y, depth), rims),
            [VM] * 2,
            name="raw",
        )
        raw = lax.all_to_all(raw.reshape(shots * each, depth), "shot", 0, 0, tiled=True)
        raw = raw.reshape(shots, each, depth)

    later, spot, amplitude = inner_1[4:]
    with jax.named_scope("step_1"):
        fwd_1, back_1, lap_1, squashed, x_up, x_down, y_up, y_down = call(
            functools.partial(step_body, 0, plane_y),
            [full] * 4
            + [shape(8, size_y, depth)] * 2
            + [shape(wave_rows(size_x), depth, dtype=BF16)] * 2,
            (
                *inner_1[:4],
                y_low,
                y_high,
                spot,
                amplitude,
                raw,
            ),
            [VM] * 9,
            scratch=step_scratch,
            name="step_1",
        )
    with jax.named_scope("halo_2"):
        x_low_2, x_high_2 = neighbours(x_up, x_down, "gx")
        y_low_2, y_high_2 = neighbours(y_up, y_down, "gy")
    with jax.named_scope("inner_2"):
        fwd_ahead, back_ahead, lap_fwd, lap_back = call(
            functools.partial(inner_body, 1, plane_y),
            [full] * 4,
            (fwd_1, back_1, fwd_now, back_now, later),
            [VM] * 5,
            scratch=inner_scratch[:2],
            flops=work,
            name="inner_2",
        )
    with jax.named_scope("step_2"):
        fwd_2, back_2, sums = call(
            functools.partial(step_body, 1, plane_y),
            [full, full, shape(shots, 2 * rows, size_y, depth)],
            (
                fwd_ahead,
                back_ahead,
                lap_fwd,
                lap_back,
                y_low_2,
                y_high_2,
                spot,
                amplitude,
                squashed,
                x_low_2,
                x_high_2,
                lap_1,
                back_1,
            ),
            [VM] * 13,
            scratch=step_scratch,
            name="step_2",
        )
    with jax.named_scope("traces"):
        trace_1, trace_2 = call(
            functools.partial(trace_body, plane_y),
            [shape(1, count)] * 2,
            (fwd_1, fwd_2, place, receivers),
            [VM, VM, SM, VM],
            name="traces",
        )
    with jax.named_scope("update"):
        sums = lax.all_to_all(
            sums.reshape(shots * 2 * rows, size_y, depth), "shot", 0, 0, tiled=True
        )
        update = call(
            update_body,
            [shape(shots, rows, size_y, depth)],
            (sums.reshape(shots, 2 * rows, size_y, depth), damping),
            [VM, SM],
            name="update",
        )
        update = lax.all_to_all(update.reshape(grid), "shot", 0, 0, tiled=True)
    with jax.named_scope("gradient"):
        share = call(
            gradient_body,
            [shape(blocks, 1, 2 * count + depth)],
            (update, squashed, features, x_low, x_high, y_low, y_high, trace_1, trace_2),
            [VM] * 9,
            scratch=[
                pltpu.VMEM((6,) + grid, BF16),
                pltpu.VMEM((size_x * size_y, 3 * channels * depth), BF16),
                pltpu.VMEM((3, size_x + 16, depth), F32),
                pltpu.VMEM((128, depth), F32),
            ],
            flops=54 * channels * size_x * size_y * depth,
            name="gradient",
        )
        share, update = lax.optimization_barrier((share, update))
        shares = lax.all_to_all(share, ("gx", "gy"), 0, 0, tiled=True)
        shares = shares.reshape(blocks, 1, 2 * count + depth)
        traces, weight_grad = call(
            total_body,
            [shape(1, 2, count), shape(channels, 27)],
            (shares,),
            [VM],
            name="total",
        )
        update = call(keep_body, [full], (update,), [VM], name="keep")
    return (fwd_2[None], back_2[None], traces, update, weight_grad)


def solution(mesh):
    in_specs = (
        P("shot", "gx", "gy", None),
        P("shot", None),
        P("shot", "gx", "gy", None),
        P("shot", "gx", "gy", None),
        P("shot", "gx", "gy", None),
        P("shot", "gx", "gy", None),
        P("shot"),
        P("shot", None),
        P("shot", None),
        P("shot", None, None),
        P(),
    )
    out_specs = (
        P("shot", "gx", "gy", None),
        P("shot", "gx", "gy", None),
        P("shot", None, None),
        P("gx", "gy", None),
        P("shot", None),
    )
    return jax.shard_map(
        per_device, mesh=mesh, in_specs=in_specs, out_specs=out_specs, check_vma=False
    )
```

```python
import functools

import jax
import jax.numpy as jnp
from jax import lax
from jax.experimental import pallas as pl
from jax.experimental.pallas import tpu as pltpu
from jax.sharding import PartitionSpec as P

RDEPTH = 3
COEFFICIENTS = (-205.0 / 72.0, 8.0 / 5.0, -1.0 / 5.0, 8.0 / 315.0, -1.0 / 560.0)
F32 = jnp.float32
BF16 = jnp.bfloat16
VMEM_LIMIT = 48 * 1024 * 1024
AHEAD = 50_000_000_000
VMEM_WHOLE = 63 * 1024 * 1024

VM = pl.BlockSpec(memory_space=pltpu.VMEM)
SM = pl.BlockSpec(memory_space=pltpu.SMEM)


def call(
    body,
    outs,
    ins,
    specs,
    scratch=(),
    flops=1_000_000,
    name=None,
    limit=VMEM_LIMIT,
):
    moved = sum(a.size * a.dtype.itemsize for a in ins) + sum(
        o.size * jnp.dtype(o.dtype).itemsize for o in outs
    )
    single = len(outs) == 1
    return pl.pallas_call(
        body,
        out_shape=outs[0] if single else tuple(outs),
        in_specs=specs,
        out_specs=VM if single else tuple(VM for _ in outs),
        scratch_shapes=list(scratch),
        compiler_params=pltpu.CompilerParams(vmem_limit_bytes=limit),
        cost_estimate=pl.CostEstimate(flops=flops, bytes_accessed=moved, transcendentals=0),
        name=name,
    )(*ins)


def shape(*dims, dtype=F32):
    return jax.ShapeDtypeStruct(dims, dtype)


def split3(value):
    top = value.astype(BF16)
    rest = value - top.astype(F32)
    middle = rest.astype(BF16)
    low = (rest - middle.astype(F32)).astype(BF16)
    return (top, middle, low)


def shifted_lanes(value, by):
    depth = value.shape[1]
    lane = lax.broadcasted_iota(jnp.int32, value.shape, 1)
    if by > 0:
        return jnp.where(lane < depth - by, pltpu.roll(value, depth - by, 1), 0.0)
    return jnp.where(lane >= -by, pltpu.roll(value, -by, 1), 0.0)


def shifted_rows(value, by):
    count = value.shape[0]
    row = lax.broadcasted_iota(jnp.int32, value.shape, 0)
    if by > 0:
        return jnp.where(row < count - by, pltpu.roll(value, count - by, 0), 0.0)
    return jnp.where(row >= -by, pltpu.roll(value, -by, 0), 0.0)


def pack_x_body(feat_ref, fwd_ref, back_ref, up_ref, down_ref, edge_ref, sems):
    channels, size_x = feat_ref.shape[:2]
    pairs = []
    for n, (out_ref, start, row) in enumerate(
        ((up_ref, size_x - 4, size_x - 1), (down_ref, 0, 0))
    ):
        pairs += [
            (feat_ref.at[:, row], edge_ref.at[n]),
            (fwd_ref.at[pl.ds(start, 4)], out_ref.at[pl.ds(0, 4)]),
            (back_ref.at[pl.ds(start, 4)], out_ref.at[pl.ds(4, 4)]),
        ]
    copies = [
        pltpu.make_async_copy(source, target, sems.at[n])
        for n, (source, target) in enumerate(pairs)
    ]
    for copy in copies:
        copy.start()
    for copy in copies:
        copy.wait()
    up_ref[8 : 8 + channels] = edge_ref[0].astype(F32)
    down_ref[8 : 8 + channels] = edge_ref[1].astype(F32)


def wave_rows(size_x):
    return size_x * 12


def pack_waves(fwd_ref, back_ref, upward, out_ref, first, edge_ref, low_ref):
    size_x, size_y, depth = fwd_ref.shape
    start, near = (size_y - 4, 2) if upward else (0, 0)
    edge_ref[:, 0:4] = fwd_ref[:, start : start + 4]
    edge_ref[:, 4:8] = back_ref[:, start : start + 4]
    value = edge_ref[...].reshape(size_x * 8, depth)
    high = value.astype(BF16)
    out_ref[first : first + size_x * 8] = high
    edge_ref[...] = (value - high.astype(F32)).reshape(size_x, 8, depth)
    quarter = size_x // 4
    for q in range(4):
        part = slice(q * quarter, (q + 1) * quarter)
        low_ref[:, 4 * q : 4 * q + 2] = edge_ref[part, near : near + 2]
        low_ref[:, 4 * q + 2 : 4 * q + 4] = edge_ref[part, 4 + near : 6 + near]
    out_ref[first + size_x * 8 : first + size_x * 12] = (
        low_ref[...].reshape(size_x * 4, depth).astype(BF16)
    )


def unpack_waves(buffer_ref, upward, first, size_x, edge_ref, low_ref):
    depth = buffer_ref.shape[1]
    near = 2 if upward else 0
    quarter = size_x // 4
    edge_ref[...] = (
        buffer_ref[first : first + size_x * 8].astype(F32).reshape(size_x, 8, depth)
    )
    low_ref[...] = (
        buffer_ref[first + size_x * 8 : first + size_x * 12]
        .astype(F32)
        .reshape(quarter, 16, depth)
    )
    for q in range(4):
        part = slice(q * quarter, (q + 1) * quarter)
        edge_ref[part, near : near + 2] += low_ref[:, 4 * q : 4 * q + 2]
        edge_ref[part, 4 + near : 6 + near] += low_ref[:, 4 * q + 2 : 4 * q + 4]


def pack_y_body(feat_ref, fwd_ref, back_ref, up_ref, down_ref, plane_ref, edge_ref, rest_ref):
    channels, size_x, size_y, depth = feat_ref.shape
    first = channels * size_x
    for c in range(channels):
        plane_ref[...] = feat_ref[c].astype(F32)
        for out_ref, y in ((up_ref, size_y - 1), (down_ref, 0)):
            out_ref[c * size_x : (c + 1) * size_x] = plane_ref[:, y, :].astype(BF16)
    for out_ref, upward in ((up_ref, True), (down_ref, False)):
        out_ref[first : first + 16] = jnp.zeros((16, depth), BF16)
        pack_waves(fwd_ref, back_ref, upward, out_ref, first + 16, edge_ref, rest_ref)


def corners_body(up_in_ref, down_in_ref, low_ref, high_ref, up_ref, down_ref):
    size_y, depth = low_ref.shape[1:]
    channels = low_ref.shape[0] - 8
    size_x = (up_ref.shape[0] - 16) // (channels + 12)
    first = channels * size_x
    row = lax.broadcasted_iota(jnp.int32, (16, depth), 0)
    for in_ref, out_ref, y in ((up_in_ref, up_ref, size_y - 1), (down_in_ref, down_ref, 0)):
        out_ref[0:first] = in_ref[0:first]
        out_ref[first + 16 :] = in_ref[first + 16 :]
        tail = jnp.zeros((16, depth), F32)
        for c in range(channels):
            tail = jnp.where(row == 2 * c, low_ref[8 + c, y : y + 1, :], tail)
            tail = jnp.where(row == 2 * c + 1, high_ref[8 + c, y : y + 1, :], tail)
        out_ref[first : first + 16] = tail.astype(BF16)


def fill_features(ext_ref, feat_ref, low_ref, high_ref):
    channels, size_x = feat_ref.shape[:2]
    for c in range(channels):
        ext_ref[c, 0] = low_ref[8 + c]
        ext_ref[c, 1 : 1 + size_x] = feat_ref[c].astype(F32)
        ext_ref[c, 1 + size_x] = high_ref[8 + c]


def conv_body(feat_ref, low_ref, high_ref, weight_ref, total_ref, wide_ref, ext_ref):
    channels, size_x = feat_ref.shape[:2]
    fill_features(ext_ref, feat_ref, low_ref, high_ref)
    together = 2

    def some_rows(start):
        terms = [[[None] * 3 for _ in range(3)] for _ in range(together)]
        for c in range(channels):
            inputs = [ext_ref[c, start + r] for r in range(together + 2)]
            for dx in range(3):
                for dy in range(3):
                    for dz in range(3):
                        weight = weight_ref[c, 9 * dx + 3 * dy + dz]
                        for r in range(together):
                            part = weight * inputs[r + dx]
                            old = terms[r][dy][dz]
                            terms[r][dy][dz] = part if old is None else old + part
        for r in range(together):
            total = None
            for dy in range(3):
                part = (
                    terms[r][dy][1]
                    + shifted_lanes(terms[r][dy][0], -1)
                    + shifted_lanes(terms[r][dy][2], 1)
                )
                if dy != 1:
                    part = shifted_rows(part, dy - 1)
                total = part if total is None else total + part
            total_ref[start + r] = total

    for start in range(0, size_x, together):
        some_rows(start)
    at = 0
    for dy in (0, 2):
        for c in range(channels):
            for dx in range(3):
                for dz in range(3):
                    weight = weight_ref[c, 9 * dx + 3 * dy + dz]
                    wide_ref[at : at + 1] = jnp.full((1, wide_ref.shape[1]), weight, F32)
                    at += 1


def load_plane(plane_ref, buffer_ref, c, size_x, channels):
    plane_ref[8 : 8 + size_x] = buffer_ref[c * size_x : (c + 1) * size_x].astype(F32)
    tail = buffer_ref[channels * size_x : channels * size_x + 16].astype(F32)
    plane_ref[7:8] = tail[2 * c : 2 * c + 1]
    plane_ref[8 + size_x : 9 + size_x] = tail[2 * c + 1 : 2 * c + 2]


def conv_edge_body(low_ref, high_ref, wide_ref, out_ref, plane_ref):
    size_x = out_ref.shape[0] // 2
    channels = wide_ref.shape[0] // 18
    at = 0
    for side, buffer_ref in enumerate((low_ref, high_ref)):
        terms = [None] * 3
        for c in range(channels):
            held_ref = plane_ref.at[side * channels + c]
            load_plane(held_ref, buffer_ref, c, size_x, channels)
            for dx in range(3):
                plane = held_ref[7 + dx : 7 + dx + size_x]
                for dz in range(3):
                    part = wide_ref[at : at + 1] * plane
                    terms[dz] = part if terms[dz] is None else terms[dz] + part
                    at += 1
        total = terms[1] + shifted_lanes(terms[0], -1) + shifted_lanes(terms[2], 1)
        out_ref[side * size_x : (side + 1) * size_x] = total


def raw_body(parts_ref, rims_ref, out_ref):
    copies, rows, size_y, depth = parts_ref.shape
    total = parts_ref[0]
    for n in range(1, copies):
        total = total + parts_ref[n]
    first = rows * size_y
    total = total.reshape(first, depth)
    rims = rims_ref[...]
    for n in range(copies):
        out_ref[n, 0:first] = total
        out_ref[n, first:] = rims


def update_body(parts_ref, damping_ref, out_ref):
    count, rows = parts_ref.shape[:2]
    half = rows // 2
    total = parts_ref[0]
    for n in range(1, count):
        total = total + parts_ref[n]
    update = total[:half] / (total[half:] + damping_ref[0])
    for n in range(count):
        out_ref[n] = update


def receiver_hits(receivers_ref, place_ref, plane_y, size_x, size_y):
    shift_y = plane_y.bit_length() - 1
    receivers = receivers_ref[...]
    place_x = lax.shift_right_logical(receivers, shift_y) - place_ref[0]
    place_y = (receivers & (plane_y - 1)) - place_ref[1]
    inside = (place_x >= 0) & (place_x < size_x) & (place_y >= 0) & (place_y < size_y)
    cell = jnp.where(inside, place_x * size_y + place_y, -1)
    cells = lax.broadcasted_iota(jnp.int32, (size_x * size_y, receivers.shape[1]), 0)
    return (cells == cell).astype(F32).astype(BF16)


def exact_product(parts, other, contract, parts_first):
    total = None
    for part in parts:
        pair = (part, other) if parts_first else (other, part)
        product = lax.dot_general(
            *pair, (contract, ((), ())), preferred_element_type=F32
        )
        total = product if total is None else total + product
    return total


def sample(fwd_ref, hit, trace_ref):
    size_x, size_y, depth = fwd_ref.shape
    field = fwd_ref[...].reshape(size_x * size_y, depth)
    total = exact_product(split3(field), hit, ((0,), (0,)), True)
    trace_ref[...] = total[RDEPTH : RDEPTH + 1, :]


def trace_body(plane_y, first_ref, second_ref, place_ref, receivers_ref, *out_refs):
    size_x, size_y, _ = first_ref.shape
    hit = receiver_hits(receivers_ref, place_ref, plane_y, size_x, size_y)
    for fwd_ref, trace_ref in zip((first_ref, second_ref), out_refs):
        sample(fwd_ref, hit, trace_ref)


def spread(sums, out_ref):
    size_x, size_y, depth = out_ref.shape
    top, middle, low = (part.astype(F32) for part in split3(sums))
    row = lax.broadcasted_iota(jnp.int32, (16, sums.shape[1]), 0)
    parts = jnp.where(row == 0, top, jnp.where(row == 1, middle, jnp.where(row == 2, low, 0.0)))
    lane = lax.broadcasted_iota(jnp.int32, (16, depth), 1)
    plane = (lane == RDEPTH).astype(F32).astype(BF16)
    out_ref[...] = lax.dot_general(
        parts.astype(BF16), plane, (((0,), (0,)), ((), ())), preferred_element_type=F32
    ).reshape(size_x, size_y, depth)


def inner_body(moment, plane_y, *refs):
    fwd_ref, back_ref, fwd_old_ref, back_old_ref = refs[:4]
    size_x, size_y, depth = fwd_ref.shape
    rows = 4
    if moment == 0:
        place_ref, receivers_ref, residual_ref, wavelet_ref, x_low_ref, x_high_ref = refs[4:10]
        fwd_ahead_ref, back_ahead_ref, lap_fwd_ref, lap_back_ref = refs[10:14]
        later_ref, spot_ref, amplitude_ref, x_ref, y_ref, inject_ref = refs[14:]
        anchor_x, anchor_y, source = place_ref[0], place_ref[1], place_ref[2]
        shift_y = plane_y.bit_length() - 1
        shift_z = depth.bit_length() - 1
        column = lax.shift_right_logical(source, shift_z)
        source_x = lax.shift_right_logical(column, shift_y) - anchor_x
        source_y = (column & (plane_y - 1)) - anchor_y
        source_z = source & (depth - 1)
        here = (source_x >= 0) & (source_x < size_x) & (source_y >= 0) & (source_y < size_y)
        spot = jnp.where(here, (source_x * size_y + source_y) * depth + source_z, -1)
        spot_ref[...] = jnp.full(spot_ref.shape, spot, jnp.int32)
        for n in range(2):
            amplitude_ref[n] = jnp.full(amplitude_ref.shape[1:], wavelet_ref[0, n], F32)
        hit = receiver_hits(receivers_ref, place_ref, plane_y, size_x, size_y)
        sums = []
        for n in range(2):
            injected = jnp.broadcast_to(residual_ref[0, n : n + 1, :], (16, hit.shape[1]))
            sums.append(exact_product(split3(injected), hit, ((1,), (1,)), True)[0:1, :])
        later_ref[...] = sums[1]
        spread(sums[0], inject_ref)
    else:
        later_ref = refs[4]
        fwd_ahead_ref, back_ahead_ref, lap_fwd_ref, lap_back_ref = refs[5:9]
        x_ref, y_ref, inject_ref = refs[9:]
        spread(later_ref[...], inject_ref)
    zero_x = jnp.zeros((4, size_y, depth), F32)
    y_ref[:, 0:8] = jnp.zeros((size_x, 8, depth), F32)
    y_ref[:, 8 + size_y : 16 + size_y] = jnp.zeros((size_x, 8, depth), F32)
    for first, ref, old_ref, ahead_ref, lap_ref in (
        (0, fwd_ref, fwd_old_ref, fwd_ahead_ref, lap_fwd_ref),
        (4, back_ref, back_old_ref, back_ahead_ref, lap_back_ref),
    ):
        x_ref[0:4] = zero_x if moment else x_low_ref[first : first + 4]
        x_ref[4 : 4 + size_x] = ref[...]
        x_ref[4 + size_x : 8 + size_x] = zero_x if moment else x_high_ref[first : first + 4]
        y_ref[:, 8 : 8 + size_y] = ref[...]

        def one_block(i, carry):
            start = i * rows
            here = pl.ds(start, rows)
            centre = ref[here]
            flat = centre.reshape(rows * size_y, depth)
            result = (3.0 * COEFFICIENTS[0]) * centre
            for k in range(1, 5):
                along_x = x_ref[pl.ds(start + 4 + k, rows)] + x_ref[pl.ds(start + 4 - k, rows)]
                along_y = (
                    y_ref[here, 8 + k : 8 + k + size_y, :] + y_ref[here, 8 - k : 8 - k + size_y, :]
                )
                along_z = shifted_lanes(flat, k) + shifted_lanes(flat, -k)
                result = result + COEFFICIENTS[k] * (
                    along_x + along_y + along_z.reshape(centre.shape)
                )
            if first:
                result = result + inject_ref[here]
            lap_ref[here] = result
            ahead_ref[here] = 2.0 * centre - old_ref[here]
            return carry

        for i in range(size_x // rows):
            one_block(i, 0)


def step_body(moment, plane_y, *refs):
    fwd_ahead_ref, back_ahead_ref, lap_fwd_ref, lap_back_ref = refs[:4]
    y_low_ref, y_high_ref, spot_ref, amplitude_ref = refs[4:8]
    refs = refs[8:]
    if moment == 0:
        raw_ref = refs[0]
        (fwd_new_ref, back_new_ref, lap_ref, squashed_ref) = refs[1:5]
        (x_up_ref, x_down_ref, y_up_ref, y_down_ref) = refs[5:9]
        refs = refs[9:]
        size_x, size_y, depth = squashed_ref.shape
        shots = raw_ref.shape[0]
        rows = size_x // shots
        first = rows * size_y
        rims = None
        for n in range(shots):
            squashed_ref[n * rows : (n + 1) * rows] = raw_ref[n, 0:first].reshape(
                rows, size_y, depth
            )
            part = raw_ref[n, first:]
            rims = part if rims is None else rims + part
        squashed_ref[:, 0:1, :] += rims[:size_x].reshape(size_x, 1, depth)
        squashed_ref[:, size_y - 1 : size_y, :] += rims[size_x:].reshape(size_x, 1, depth)
    else:
        squashed_ref, x_low_ref, x_high_ref, lap_old_ref, back_ref = refs[:5]
        (fwd_new_ref, back_new_ref, sums_ref) = refs[5:8]
        refs = refs[8:]
    edge_ref, rest_ref, *sides = refs
    size_x, size_y, depth = fwd_ahead_ref.shape
    start_row = y_low_ref.shape[0] - wave_rows(size_x)
    for n, (buffer_ref, upward) in enumerate(((y_low_ref, True), (y_high_ref, False))):
        unpack_waves(buffer_ref, upward, start_row, size_x, edge_ref, rest_ref)
        for m in range(2):
            side_ref = sides[2 * m + n]
            at, empty = (4, 8) if upward else (8, 0)
            side_ref[:, empty : empty + 8] = jnp.zeros((size_x, 8, depth), F32)
            side_ref[:, at : at + 4] = edge_ref[:, 4 * m : 4 * m + 4]

    spot, amplitude = spot_ref[0:1, :], amplitude_ref[moment, 0:1, :]

    def edges(lap, m, start):
        block = slice(start, start + 4)
        low = high = None
        for k in range(1, 5):
            a = COEFFICIENTS[k] * sides[2 * m][block, 8 - k : 16 - k, :]
            b = COEFFICIENTS[k] * sides[2 * m + 1][block, k : 8 + k, :]
            low, high = (a, b) if low is None else (low + a, high + b)
        parts = [low, high]
        if size_y > 16:
            parts.insert(1, jnp.zeros((4, size_y - 16, depth), F32))
        lap = lap + jnp.concatenate(parts, axis=1)
        if moment == 0 or start not in (0, size_x - 4):
            return lap
        parts = []
        for j in range(4):
            total = None
            if start == 0:
                picks = [(k, x_low_ref, 4 * m + 4 + j - k) for k in range(j + 1, 5)]
            else:
                picks = [(k, x_high_ref, 4 * m + j + k - 4) for k in range(4 - j, 5)]
            for k, ref, row in picks:
                part = COEFFICIENTS[k] * ref[row]
                total = part if total is None else total + part
            parts.append(total)
        return lap + jnp.stack(parts)

    for start in range(0, size_x, 4):
        here = slice(start, start + 4)
        squashed = squashed_ref[here]
        if moment == 0:
            squashed = jax.nn.sigmoid(squashed)
            squashed_ref[here] = squashed
        courant = 0.02 + 0.16 * squashed
        lap_fwd = edges(lap_fwd_ref[here], 0, start)
        lap_back = edges(lap_back_ref[here], 1, start)
        dims = lap_fwd.shape
        index = (
            lax.broadcasted_iota(jnp.int32, dims, 0) * (size_y * depth)
            + lax.broadcasted_iota(jnp.int32, dims, 1) * depth
            + lax.broadcasted_iota(jnp.int32, dims, 2)
        )
        added = jnp.where(index == spot - start * (size_y * depth), amplitude, 0.0)
        fwd_new_ref[here] = fwd_ahead_ref[here] + courant * (lap_fwd + added)
        back_new = back_ahead_ref[here] + courant * lap_back
        back_new_ref[here] = back_new
        if moment == 0:
            lap_ref[here] = lap_fwd
        else:
            rows = sums_ref.shape[1] // 2
            n, at = start // rows, start % rows
            lap_old = lap_old_ref[here]
            sums_ref[n, at : at + 4] = lap_old * back_ref[here] + lap_fwd * back_new
            sums_ref[n, rows + at : rows + at + 4] = lap_old * lap_old + lap_fwd * lap_fwd

    if moment == 0:
        x_up_ref[0:4] = fwd_new_ref[size_x - 4 : size_x]
        x_up_ref[4:8] = back_new_ref[size_x - 4 : size_x]
        x_down_ref[0:4] = fwd_new_ref[0:4]
        x_down_ref[4:8] = back_new_ref[0:4]
        pack_waves(fwd_new_ref, back_new_ref, True, y_up_ref, 0, edge_ref, rest_ref)
        pack_waves(fwd_new_ref, back_new_ref, False, y_down_ref, 0, edge_ref, rest_ref)


def gradient_body(
    update_ref,
    squashed_ref,
    feat_ref,
    x_low_ref,
    x_high_ref,
    y_low_ref,
    y_high_ref,
    first_ref,
    second_ref,
    out_ref,
    left_ref,
    right_ref,
    plane_ref,
    rows_ref,
):
    size_x, size_y, depth = update_ref.shape
    channels = feat_ref.shape[0]
    copies = out_ref.shape[0]
    cells = size_x * size_y

    for x in range(size_x):
        squashed = squashed_ref[x]
        pulled = update_ref[x] * (0.16 * squashed * (1.0 - squashed))
        for dy in range(3):
            moved = pulled if dy == 1 else shifted_rows(pulled, 1 - dy)
            high = moved.astype(BF16)
            left_ref[2 * dy, x] = high
            left_ref[2 * dy + 1, x] = (moved - high.astype(F32)).astype(BF16)
        plane_ref[1, x : x + 1] = pulled[0:1, :]
        plane_ref[2, x : x + 1] = pulled[size_y - 1 : size_y, :]
    last = cells - size_y
    for c in range(channels):
        lanes = [slice((3 * c + dx) * depth, (3 * c + dx + 1) * depth) for dx in range(3)]
        own = feat_ref[c].reshape(cells, depth)
        right_ref[0:size_y, lanes[0]] = x_low_ref[8 + c].astype(BF16)
        right_ref[size_y:cells, lanes[0]] = own[0:last]
        right_ref[:, lanes[1]] = own
        right_ref[0:last, lanes[2]] = own[size_y:cells]
        right_ref[last:cells, lanes[2]] = x_high_ref[8 + c].astype(BF16)
    ahead = lax.broadcasted_iota(jnp.int32, (depth, depth), 1) - (
        lax.broadcasted_iota(jnp.int32, (depth, depth), 0)
    )
    for dy in range(3):
        left = jnp.concatenate(
            [left_ref[2 * dy + part].reshape(cells, depth) for part in range(2)], axis=1
        )
        product = lax.dot_general(
            left, right_ref[...], (((0,), (0,)), ((), ())), preferred_element_type=F32
        )
        for c in range(channels):
            for dx in range(3):
                lanes = slice((3 * c + dx) * depth, (3 * c + dx + 1) * depth)
                block = product[0:depth, lanes] + product[depth : 2 * depth, lanes]
                for dz in range(3):
                    at = c * 27 + 9 * dx + 3 * dy + dz
                    rows_ref[at : at + 1] = jnp.sum(
                        jnp.where(ahead == dz - 1, block, 0.0), axis=0, keepdims=True
                    )
    at = channels * 27
    rows_ref[at:] = jnp.zeros((rows_ref.shape[0] - at, depth), F32)

    for buffer_ref, dy, which in ((y_low_ref, 0, 1), (y_high_ref, 2, 2)):
        pulled = plane_ref[which, 0:size_x]
        along = [pulled if dz == 1 else shifted_lanes(pulled, 1 - dz) for dz in range(3)]
        for c in range(channels):
            load_plane(plane_ref.at[0], buffer_ref, c, size_x, channels)
            for dx in range(3):
                features = plane_ref[0, 7 + dx : 7 + dx + size_x]
                for dz in range(3):
                    at = c * 27 + 9 * dx + 3 * dy + dz
                    rows_ref[at : at + 1] += jnp.sum(
                        features * along[dz], axis=0, keepdims=True
                    )

    ones = jnp.ones((8, depth), BF16)
    sums = None
    for part in split3(rows_ref[...]):
        product = lax.dot_general(
            ones, part, (((1,), (1,)), ((), ())), preferred_element_type=F32
        )
        sums = product if sums is None else sums + product
    count = first_ref.shape[1]
    for n in range(copies):
        out_ref[n, :, 0:count] = first_ref[...]
        out_ref[n, :, count : 2 * count] = second_ref[...]
        out_ref[n, :, 2 * count : 2 * count + depth] = sums[0:1]


def total_body(shares_ref, trace_ref, grad_ref):
    copies = shares_ref.shape[0]
    count = trace_ref.shape[2]
    channels, offsets = grad_ref.shape
    total = shares_ref[0]
    for n in range(1, copies):
        total = total + shares_ref[n]
    trace_ref[0, 0:1, :] = total[:, 0:count]
    trace_ref[0, 1:2, :] = total[:, count : 2 * count]
    last = total[:, 2 * count :]
    lanes = last.shape[1]
    last = jnp.broadcast_to(last, (8, lanes))
    for c in range(channels):
        turned = last if c == 0 else pltpu.roll(last, lanes - c * offsets, 1)
        grad_ref[c : c + 1, :] = turned[0:1, 0:offsets]


def keep_body(value_ref, out_ref):
    out_ref[...] = value_ref[...]


def neighbours(up, down, axis):
    count = lax.axis_size(axis)
    low = lax.ppermute(up, axis, [(i, i + 1) for i in range(count - 1)])
    high = lax.ppermute(down, axis, [(i + 1, i) for i in range(count - 1)])
    return low, high


def per_device(
    features,
    conv_weight,
    fwd_prev,
    fwd_now,
    back_prev,
    back_now,
    sources,
    wavelet,
    receivers,
    residual,
    damping,
):
    channels, size_x, size_y, depth = features.shape
    shots = lax.axis_size("shot")
    rows = size_x // shots
    count = receivers.shape[1]
    plane_y = size_y * lax.axis_size("gy")
    blocks = lax.axis_size("gx") * lax.axis_size("gy")
    grid = (size_x, size_y, depth)
    fwd_prev, fwd_now, back_prev, back_now = (
        a.reshape(grid) for a in (fwd_prev, fwd_now, back_prev, back_now)
    )
    place = jnp.stack(
        [
            lax.axis_index("gx") * size_x,
            lax.axis_index("gy") * size_y,
            sources[0],
        ]
    ).astype(jnp.int32)

    x_shape = shape(8 + channels, size_y, depth)
    with jax.named_scope("pack_x"):
        x_up, x_down = call(
            pack_x_body,
            [x_shape, x_shape],
            (features, fwd_now, back_now),
            [pl.BlockSpec(memory_space=pltpu.HBM)] * 3,
            scratch=[
                pltpu.VMEM((2, channels, size_y, depth), BF16),
                pltpu.SemaphoreType.DMA((6,)),
            ],
            name="pack_x",
            limit=VMEM_WHOLE,
        )
    packing = [
        pltpu.VMEM((size_x, 8, depth), F32),
        pltpu.VMEM((size_x // 4, 16, depth), F32),
    ]
    y_shape = shape(channels * size_x + 16 + wave_rows(size_x), depth, dtype=BF16)
    with jax.named_scope("pack_y"):
        y_up, y_down = call(
            pack_y_body,
            [y_shape, y_shape],
            (features, fwd_now, back_now),
            [VM] * 3,
            scratch=[pltpu.VMEM(grid, F32)] + packing,
            name="pack_y",
        )
    with jax.named_scope("halo_x"):
        x_low, x_high = neighbours(x_up, x_down, "gx")
    with jax.named_scope("corners"):
        y_up, y_down = call(
            corners_body,
            [y_shape, y_shape],
            (y_up, y_down, x_low, x_high),
            [VM] * 4,
            name="corners",
        )
    with jax.named_scope("halo_y"):
        y_low, y_high = neighbours(y_up, y_down, "gy")
    ext = pltpu.VMEM((channels, size_x + 2, size_y, depth), F32)
    full = shape(*grid)
    inner_scratch = [
        pltpu.VMEM((size_x + 8, size_y, depth), F32),
        pltpu.VMEM((size_x, size_y + 16, depth), F32),
        pltpu.VMEM(grid, F32),
    ]
    step_scratch = packing + [pltpu.VMEM((size_x, 16, depth), F32)] * 4
    work = 60 * size_x * size_y * depth
    with jax.named_scope("inner_1"):
        inner_1 = call(
            functools.partial(inner_body, 0, plane_y),
            [full] * 4
            + [shape(1, size_x * size_y), shape(8, depth, dtype=jnp.int32), shape(2, 8, depth)],
            (fwd_now, back_now, fwd_prev, back_prev)
            + (place, receivers, residual, wavelet, x_low, x_high),
            [VM] * 4 + [SM] + [VM] * 2 + [SM] + [VM] * 2,
            scratch=inner_scratch,
            flops=work,
            name="inner_1",
        )
    with jax.named_scope("conv"):
        main, wide = call(
            conv_body,
            [full, shape(18 * channels, depth)],
            (features, x_low, x_high, conv_weight),
            [VM, VM, VM, SM],
            scratch=[ext],
            flops=54 * channels * size_x * size_y * depth,
            name="conv",
        )
    with jax.named_scope("raw"):
        parts = lax.all_to_all(main, "shot", 0, 0, tiled=True)
        y_low, *inner_1 = lax.optimization_barrier((y_low, *inner_1))
        rims = call(
            conv_edge_body,
            [shape(2 * size_x, depth)],
            (y_low, y_high, wide),
            [VM] * 3,
            scratch=[pltpu.VMEM((2 * channels, size_x + 16, depth), F32)],
            flops=AHEAD,
            name="conv_edge",
        )
        each = rows * size_y + 2 * size_x
        raw = call(
            raw_body,
            [shape(shots, each, depth)],
            (parts.reshape(shots, rows, size_y, depth), rims),
            [VM] * 2,
            name="raw",
        )
        raw = lax.all_to_all(raw.reshape(shots * each, depth), "shot", 0, 0, tiled=True)
        raw = raw.reshape(shots, each, depth)

    later, spot, amplitude = inner_1[4:]
    with jax.named_scope("step_1"):
        fwd_1, back_1, lap_1, squashed, x_up, x_down, y_up, y_down = call(
            functools.partial(step_body, 0, plane_y),
            [full] * 4
            + [shape(8, size_y, depth)] * 2
            + [shape(wave_rows(size_x), depth, dtype=BF16)] * 2,
            (
                *inner_1[:4],
                y_low,
                y_high,
                spot,
                amplitude,
                raw,
            ),
            [VM] * 9,
            scratch=step_scratch,
            name="step_1",
        )
    with jax.named_scope("halo_2"):
        x_low_2, x_high_2 = neighbours(x_up, x_down, "gx")
        y_low_2, y_high_2 = neighbours(y_up, y_down, "gy")
    with jax.named_scope("inner_2"):
        fwd_ahead, back_ahead, lap_fwd, lap_back = call(
            functools.partial(inner_body, 1, plane_y),
            [full] * 4,
            (fwd_1, back_1, fwd_now, back_now, later),
            [VM] * 5,
            scratch=inner_scratch,
            flops=work,
            name="inner_2",
        )
    with jax.named_scope("step_2"):
        fwd_2, back_2, sums = call(
            functools.partial(step_body, 1, plane_y),
            [full, full, shape(shots, 2 * rows, size_y, depth)],
            (
                fwd_ahead,
                back_ahead,
                lap_fwd,
                lap_back,
                y_low_2,
                y_high_2,
                spot,
                amplitude,
                squashed,
                x_low_2,
                x_high_2,
                lap_1,
                back_1,
            ),
            [VM] * 13,
            scratch=step_scratch,
            name="step_2",
        )
    with jax.named_scope("traces"):
        trace_1, trace_2 = call(
            functools.partial(trace_body, plane_y),
            [shape(1, count)] * 2,
            (fwd_1, fwd_2, place, receivers),
            [VM, VM, SM, VM],
            name="traces",
        )
    with jax.named_scope("update"):
        sums = lax.all_to_all(
            sums.reshape(shots * 2 * rows, size_y, depth), "shot", 0, 0, tiled=True
        )
        update = call(
            update_body,
            [shape(shots, rows, size_y, depth)],
            (sums.reshape(shots, 2 * rows, size_y, depth), damping),
            [VM, SM],
            name="update",
        )
        update = lax.all_to_all(update.reshape(grid), "shot", 0, 0, tiled=True)
    with jax.named_scope("gradient"):
        share = call(
            gradient_body,
            [shape(blocks, 1, 2 * count + depth)],
            (update, squashed, features, x_low, x_high, y_low, y_high, trace_1, trace_2),
            [VM] * 9,
            scratch=[
                pltpu.VMEM((6,) + grid, BF16),
                pltpu.VMEM((size_x * size_y, 3 * channels * depth), BF16),
                pltpu.VMEM((3, size_x + 16, depth), F32),
                pltpu.VMEM((128, depth), F32),
            ],
            flops=54 * channels * size_x * size_y * depth,
            name="gradient",
        )
        share, update = lax.optimization_barrier((share, update))
        shares = lax.all_to_all(share, ("gx", "gy"), 0, 0, tiled=True)
        shares = shares.reshape(blocks, 1, 2 * count + depth)
        traces, weight_grad = call(
            total_body,
            [shape(1, 2, count), shape(channels, 27)],
            (shares,),
            [VM],
            name="total",
        )
        update = call(keep_body, [full], (update,), [VM], name="keep")
    return (fwd_2[None], back_2[None], traces, update, weight_grad)


def solution(mesh):
    in_specs = (
        P("shot", "gx", "gy", None),
        P("shot", None),
        P("shot", "gx", "gy", None),
        P("shot", "gx", "gy", None),
        P("shot", "gx", "gy", None),
        P("shot", "gx", "gy", None),
        P("shot"),
        P("shot", None),
        P("shot", None),
        P("shot", None, None),
        P(),
    )
    out_specs = (
        P("shot", "gx", "gy", None),
        P("shot", "gx", "gy", None),
        P("shot", None, None),
        P("gx", "gy", None),
        P("shot", None),
    )
    return jax.shard_map(
        per_device, mesh=mesh, in_specs=in_specs, out_specs=out_specs, check_vma=False
    )
```
